256 devices in a mesh: band: 16 (over z, x_hi), gy: 4 (over x_lo, core), gz: 4 (over y).
Axes of the slice: x: 4 (x_hi: 2, x_lo: 2; x = x_hi * 2 + x_lo), y: 4, z: 8, core: 2. Of those that a mesh axis runs over, the one named last changes fastest.
Arguments:
- orbitals: bfloat16 [32, 128, 128, 256], P('band', 'gy', 'gz'), may hold values from -6 to 6
- potential: float32 [128, 128, 128], P(('gy', 'gz')), may hold values from -6 to 6
- cutoff_mask: int32 [128, 128, 128], P('gy', 'gz'), may hold values from 0 to 1, as said below
- channels: bfloat16 [4, 128, 128, 128], P(None, 'gy', 'gz'), may hold values from -0.125 to 0.125
- positions: float32 [8, 3], replicated, may hold values from 0 to 1
- proj_atom: int32 [32], replicated, may hold values from 0 to 7
- proj_chan: int32 [32], replicated, may hold values from 0 to 3
- coupling: float32 [32], replicated, may hold values from 0.5 to 2
- occupations: float32 [32], P('band'), may hold values from 0.03125 to 0.09375
Outputs:
- applied: bfloat16 [32, 128, 128, 256], P('band', 'gy', 'gz')
- density: float32 [128, 128, 128], P(('gy', 'gz'))
The draws below stay inside these ranges and needn't reach their ends.
Inputs may be any that keep to these rules, and one draw needn't show every extreme that they name: With s = f(ky)^2 + f(kz)^2 + f(kx)^2, cutoff_mask is 1 wherever s < 56^2 and 0 wherever s >= 128^2 / 4; in between each plane wave's value is its own.
All inputs are finite; a program needn't handle non-finite values.
Results may differ from the reference program's by a relative error of at most 0.018.
Values may be sent and summed in bfloat16 or wider, within the bound.
No kernel may reach another device: no remote copies, remote signals or barrier semaphores. Data moves between devices by JAX's collectives and lax.ppermute only.
A program may use at most 128 MiB of HBM per device.

```python
import math
import jax
import jax.numpy as jnp
from jax import lax

NG = 128
BANDS = 32
CHAN = 4
ATOMS = 8
PROJ = 32


def draw_cutoff_mask(key, part):
    key = jax.random.fold_in(key, 7)
    inner = 7 * NG // 16 * (7 * NG // 16)
    outer = NG // 2 * (NG // 2)
    limits = jax.random.randint(key, (NG, NG, NG), inner, outer + 1, dtype=jnp.int32)
    grid_index = jnp.arange(NG, dtype=jnp.int32)
    wave_number = jnp.where(grid_index >= NG // 2, grid_index - NG, grid_index)
    squared = wave_number * wave_number
    total = squared[:, None, None] + squared[None, :, None] + squared[None, None, :]
    return (total < limits).astype(jnp.int32)


def set_ends(entries, rng, least, high):
    extent = entries.shape
    spot = [jax.random.randint(jax.random.fold_in(rng, axis), (), 0, extent[axis]) for axis in range(len(extent))]
    entries = entries.at[tuple(spot)].set(least)
    longest = extent.index(max(extent))
    spot[longest] = (spot[longest] + 1) % extent[longest]
    return entries.at[tuple(spot)].set(high)


def shard_levels(key, extent, cuts, smallest, largest):
    level, own = 1.0, jax.random.fold_in(key, 6)
    for position, blocks in cuts:
        steps = jnp.exp(jax.random.uniform(jax.random.fold_in(own, position), (blocks,), jnp.float32, smallest / len(cuts), largest / len(cuts)))
        level = level * jnp.repeat(steps, extent[position] // blocks).reshape([-1 if axis == position else 1 for axis in range(len(extent))])
    return level


def scatter_about(own_key, shape, width, most, pieces=(), held_as=jnp.bfloat16):
    entries = width * jax.random.normal(own_key, shape, jnp.float32)
    if pieces:
        entries = entries * shard_levels(own_key, shape, pieces, -0.22, 0.18)
    return jnp.clip(entries, -most, most).astype(held_as)


def setup_inputs(seed: int = 0) -> dict:
    arg_keys = jax.random.split(jax.random.key(seed), 10)
    orbitals = scatter_about(arg_keys[0], (BANDS, NG, NG, 2 * NG), 1.0, 6.0, ((0, 16), (1, 4), (2, 4)))
    potential = scatter_about(arg_keys[1], (NG, NG, NG), 1.0, 6.0, ((0, 16),), jnp.float32)
    cutoff_mask = draw_cutoff_mask(jax.random.fold_in(arg_keys[9], 71), 0)
    channels = scatter_about(arg_keys[3], (CHAN, NG, NG, NG), (1.0 / (2 * NG ** 3 * PROJ) ** 0.25), 0.125, ((1, 4), (2, 4)))
    positions = jnp.clip(jax.random.uniform(arg_keys[4], (ATOMS, 3), jnp.float32, 0.0, 1.0), 0.0, 1.0)
    proj_atom = set_ends(jax.random.randint(arg_keys[5], (PROJ,), 0, ATOMS), jax.random.fold_in(arg_keys[5], 1), 0, ATOMS - 1).astype(jnp.int32)
    proj_chan = set_ends(jax.random.randint(arg_keys[6], (PROJ,), 0, CHAN), jax.random.fold_in(arg_keys[6], 1), 0, CHAN - 1).astype(jnp.int32)
    coupling = jnp.clip(jnp.exp(jax.random.uniform(arg_keys[7], (PROJ,), jnp.float32, math.log(0.5), math.log(2.0))), 0.5, 2.0)
    occupations = jnp.clip(0.03125 + 0.0625 * jax.random.uniform(arg_keys[8], (BANDS,), jnp.float32) ** shard_levels(arg_keys[8], (BANDS,), ((0, 16),), -0.2, 0.2), 0.03125, 0.09375)
    return dict(orbitals=orbitals, potential=potential, cutoff_mask=cutoff_mask, channels=channels, positions=positions, proj_atom=proj_atom, proj_chan=proj_chan, coupling=coupling, occupations=occupations)


kinetic_scale = 1.0 / 1024.0

def dft_table(length, sign_value):
    grid_index = jnp.arange(length, dtype=jnp.int32)
    product = grid_index[:, None] * grid_index[None, :] % length
    phase_angle = 2.0 * math.pi / length * product.astype(jnp.float32)
    cosine_part = jnp.cos(phase_angle) / math.sqrt(length)
    sine_part = sign_value * jnp.sin(phase_angle) / math.sqrt(length)
    upper_rows = jnp.stack([cosine_part, -sine_part], axis=1)
    lower_rows = jnp.stack([sine_part, cosine_part], axis=1)
    return jnp.stack([upper_rows, lower_rows], axis=0).astype(jnp.bfloat16)

def frequencies(first_index, span, length):
    grid_index = first_index + jnp.arange(span, dtype=jnp.int32)
    return jnp.where(grid_index >= length // 2, grid_index - length, grid_index).astype(jnp.float32)

def axis_phase(coordinate, freq):
    phase_angle = 2.0 * math.pi * (coordinate[:, None] * freq[None, :])
    return (jnp.cos(phase_angle), jnp.sin(phase_angle))

def projector_parts(channels, positions, atom_ids, kind_ids, freq_y, freq_z, freq_x):
    atom_hot = (atom_ids[:, None] == jnp.arange(positions.shape[0], dtype=jnp.int32)[None, :]).astype(jnp.float32)
    located = jnp.dot(atom_hot, positions, precision=lax.Precision.HIGHEST)
    kind_hot = (kind_ids[:, None] == jnp.arange(channels.shape[0], dtype=jnp.int32)[None, :]).astype(jnp.bfloat16)
    radial = jnp.einsum('bc,cyzx->byzx', kind_hot, channels, preferred_element_type=jnp.float32)
    cos_y, sin_y = axis_phase(located[:, 1], freq_y)
    cos_z, sin_z = axis_phase(located[:, 2], freq_z)
    cos_x, sin_x = axis_phase(located[:, 0], freq_x)
    cos_yz = cos_y[:, :, None] * cos_z[:, None, :] - sin_y[:, :, None] * sin_z[:, None, :]
    sin_yz = sin_y[:, :, None] * cos_z[:, None, :] + cos_y[:, :, None] * sin_z[:, None, :]
    cosine = cos_yz[..., None] * cos_x[:, None, None, :] - sin_yz[..., None] * sin_x[:, None, None, :]
    sine = sin_yz[..., None] * cos_x[:, None, None, :] + cos_yz[..., None] * sin_x[:, None, None, :]
    real_beta = (radial * cosine).astype(jnp.bfloat16)
    imag_beta = (-(radial * sine)).astype(jnp.bfloat16)
    return (real_beta, imag_beta)

def reference(orbitals, potential, cutoff_mask, channels, positions, proj_atom, proj_chan, coupling, occupations):
    length = NG
    high = lax.Precision.HIGHEST
    inverse = dft_table(length, 1.0)
    forward = dft_table(length, -1.0)
    inv_x = jnp.transpose(inverse, (2, 3, 0, 1)).reshape(2 * length, 2, length).astype(jnp.float32)
    fwd_x = jnp.transpose(forward, (2, 3, 0, 1)).reshape(2, length, 2 * length).astype(jnp.float32)
    inv_f = inverse.astype(jnp.float32)
    fwd_f = forward.astype(jnp.float32)
    mask_full = jnp.concatenate([cutoff_mask, cutoff_mask], axis=2) != 0
    masked = jnp.where(mask_full[None], orbitals, jnp.zeros_like(orbitals))
    freq = frequencies(0, length, length)
    energy = kinetic_scale * 0.5 * (freq[:, None, None] ** 2 + freq[None, :, None] ** 2 + freq[None, None, :] ** 2)
    energy = jnp.concatenate([energy, energy], axis=2)
    block_size = min(PROJ, 16)
    block_count = PROJ // block_size
    atom_blocks = proj_atom.reshape(block_count, block_size)
    kind_blocks = proj_chan.reshape(block_count, block_size)
    real_orbs = masked[..., :length].astype(jnp.float32)
    imag_orbs = masked[..., length:].astype(jnp.float32)

    def intersection_step(state_in, indices):
        real_beta, imag_beta = projector_parts(channels, positions, indices[0], indices[1], freq, freq, freq)
        real_beta = real_beta.astype(jnp.float32)
        imag_beta = imag_beta.astype(jnp.float32)
        real_over = jnp.einsum('pyzx,nyzx->pn', real_beta, real_orbs) + jnp.einsum('pyzx,nyzx->pn', imag_beta, imag_orbs)
        imag_over = jnp.einsum('pyzx,nyzx->pn', real_beta, imag_orbs) - jnp.einsum('pyzx,nyzx->pn', imag_beta, real_orbs)
        return (state_in, jnp.stack([real_over, imag_over], axis=0))
    unused, intersections = lax.scan(intersection_step, jnp.zeros((), jnp.float32), (atom_blocks, kind_blocks))
    coefficients = intersections * coupling.reshape(block_count, 1, block_size, 1)
    coefficients = coefficients.astype(jnp.bfloat16)

    def apply_step(running, inputs):
        real_beta, imag_beta = projector_parts(channels, positions, inputs[0], inputs[1], freq, freq, freq)
        real_beta = real_beta.astype(jnp.float32)
        imag_beta = imag_beta.astype(jnp.float32)
        coef_real = inputs[2][0].astype(jnp.float32)
        coef_imag = inputs[2][1].astype(jnp.float32)
        real_sum = running[0] + jnp.einsum('pn,pyzx->nyzx', coef_real, real_beta) - jnp.einsum('pn,pyzx->nyzx', coef_imag, imag_beta)
        imag_sum = running[1] + jnp.einsum('pn,pyzx->nyzx', coef_imag, real_beta) + jnp.einsum('pn,pyzx->nyzx', coef_real, imag_beta)
        return ((real_sum, imag_sum), None)
    start_sums = (jnp.zeros(real_orbs.shape, jnp.float32), jnp.zeros(real_orbs.shape, jnp.float32))
    sums, unused_two = lax.scan(apply_step, start_sums, (atom_blocks, kind_blocks, coefficients))
    nonlocal_part = jnp.concatenate([sums[0], sums[1]], axis=3)

    def band_step(density, inputs):
        orbital, extra, weight = inputs
        spread = jnp.einsum('yzk,kcj->yzcj', orbital.astype(jnp.float32), inv_x, precision=high).astype(jnp.bfloat16)
        rotated = jnp.einsum('yzcj,ducy->uzdj', spread.astype(jnp.float32), inv_f, precision=high).astype(jnp.bfloat16)
        real_field = jnp.einsum('uzdj,fwdz->fjuw', rotated.astype(jnp.float32), inv_f, precision=high)
        density = density + weight * lax.optimization_barrier(jnp.sum(real_field * real_field, axis=0))
        scaled = (potential[None] * real_field).astype(jnp.bfloat16)
        back_z = jnp.einsum('fjuw,dzfw->uzdj', scaled.astype(jnp.float32), fwd_f, precision=high).astype(jnp.bfloat16)
        folded = jnp.einsum('uzdj,cydu->yzcj', back_z.astype(jnp.float32), fwd_f, precision=high).astype(jnp.bfloat16)
        local_g = jnp.einsum('yzcj,cjk->yzk', folded.astype(jnp.float32), fwd_x, precision=high)
        total = energy * orbital.astype(jnp.float32) + local_g + extra
        applied = jnp.where(mask_full, total, jnp.zeros_like(total)).astype(jnp.bfloat16)
        return (density, applied)
    density, applied = lax.scan(band_step, jnp.zeros((length, length, length), jnp.float32), (masked, nonlocal_part, occupations))
    return (applied, density)
```

```python
import functools
import math

import jax
import jax.numpy as jnp
import ml_dtypes
import numpy as np
from jax import lax
from jax.experimental import pallas as pl
from jax.experimental.pallas import tpu as pltpu
from jax.sharding import PartitionSpec as P

kinetic_scale = 1.0 / 1024.0
vmem_bytes = 48 * 1024 * 1024
bf16 = jnp.bfloat16
f32 = jnp.float32


def dft_table(length, sign_value):
    grid_index = np.arange(length)
    product = grid_index[:, None] * grid_index[None, :] % length
    phase_angle = np.float32(2.0 * math.pi / length) * product.astype(np.float32)
    cosine_part = np.cos(phase_angle) / np.float32(math.sqrt(length))
    sine_part = sign_value * np.sin(phase_angle) / np.float32(math.sqrt(length))
    upper_rows = np.stack([cosine_part, -sine_part], axis=1)
    lower_rows = np.stack([sine_part, cosine_part], axis=1)
    return np.stack([upper_rows, lower_rows], axis=0).astype(np.float32)


def rounded(table, rows):
    return jnp.asarray(np.ascontiguousarray(table).reshape(rows, -1).astype(ml_dtypes.bfloat16))


def frequencies(first_index, span, length):
    grid_index = first_index + jnp.arange(span, dtype=jnp.int32)
    return jnp.where(grid_index >= length // 2, grid_index - length, grid_index).astype(f32)


def axis_phase(coordinate, freq):
    phase_angle = 2.0 * math.pi * (coordinate[:, None] * freq[None, :])
    return (jnp.cos(phase_angle), jnp.sin(phase_angle))


def dot(left, right):
    return jnp.dot(left, right, preferred_element_type=f32)


def dot_nt(left, right):
    return lax.dot_general(left, right, (((1,), (1,)), ((), ())), preferred_element_type=f32)


def dot_tn(left, right):
    return lax.dot_general(left, right, (((0,), (0,)), ((), ())), preferred_element_type=f32)


def spread_kernel(orbitals_ref, mask_ref, table_ref, out_ref):
    length = mask_ref.shape[2]
    dests = out_ref.shape[0]
    thin = length // dests
    mask = jnp.where(mask_ref[...] != 0, 1.0, 0.0).astype(bf16)
    mask = jnp.concatenate([mask, mask], axis=2)
    lane = lax.broadcasted_iota(jnp.int32, (length, 128), 1)
    for pair in range(0, mask_ref.shape[0], 2):
        rows = []
        for y in (pair, pair + 1):
            both = jnp.concatenate([orbitals_ref[0, y] * mask[y], orbitals_ref[1, y] * mask[y]], axis=0)
            rows += [both, both]
        spread = dot_nt(table_ref[...], jnp.concatenate(rows, axis=0))
        tiles = []
        for half in range(2):
            cols = slice(half * 128, half * 128 + 128)
            tile = jnp.where(lane < 64, spread[:length, cols], spread[length:, cols])
            tiles.append(tile.reshape(dests, thin, 128))
        out_ref[:, pair * thin : (pair + 2) * thin, :] = jnp.concatenate(tiles, axis=1).astype(bf16)


def overlap_kernel(orbitals_ref, mask_ref, channels_ref, phase_ref, wave_ref, out_ref, sums_ref):
    step = pl.program_id(0)
    rows = mask_ref.shape[0] * mask_ref.shape[1]
    length = mask_ref.shape[2]
    atoms = wave_ref.shape[0] // 2
    kinds = channels_ref.shape[0]
    mask = jnp.where(mask_ref[...] != 0, 1.0, 0.0).astype(bf16)
    orbs = [orbitals_ref[n].reshape(rows, 2 * length) for n in range(2)]
    columns = []
    for c in range(kinds):
        radial = (channels_ref[c] * mask).reshape(rows, length)
        radial = jnp.concatenate([radial, radial], axis=1)
        columns += [radial * orbs[0], radial * orbs[1]]
    part = dot(phase_ref[...], jnp.concatenate(columns, axis=1))

    @pl.when(step == 0)
    def first():
        sums_ref[...] = part

    @pl.when(step > 0)
    def later():
        sums_ref[...] += part

    @pl.when(step == pl.num_programs(0) - 1)
    def last():
        cos_x, sin_x = wave_ref[:atoms], wave_ref[atoms:]
        lane = lax.broadcasted_iota(jnp.int32, (atoms, 128), 1)
        total = jnp.zeros((atoms, 128), f32)
        for pair in range(kinds * 2):
            base = pair * 2 * length
            real_cols = slice(base, base + length)
            imag_cols = slice(base + length, base + 2 * length)
            real = sums_ref[:atoms, real_cols] - sums_ref[atoms:, imag_cols]
            imag = sums_ref[atoms:, real_cols] + sums_ref[:atoms, imag_cols]
            real_over = jnp.sum(real * cos_x - imag * sin_x, axis=1, keepdims=True)
            imag_over = jnp.sum(real * sin_x + imag * cos_x, axis=1, keepdims=True)
            total = jnp.where(lane == 2 * pair, real_over, total)
            total = jnp.where(lane == 2 * pair + 1, imag_over, total)
        high = total.astype(bf16).astype(f32)
        out_ref[...] = jnp.concatenate([high, total - high], axis=0).astype(bf16)


def field_kernel(arrived_ref, potential_ref, weight_ref, z_ref, y_ref, density_ref, scaled_ref, work_ref):
    thin = potential_ref.shape[0]
    length = potential_ref.shape[1]
    parts = arrived_ref.shape[0] // 4
    rows = arrived_ref.shape[1]
    for sy in range(parts):
        columns = jnp.concatenate([arrived_ref[sy * 4 + sz] for sz in range(4)], axis=1)
        halfway = dot(columns, z_ref[...])
        for tile in range(4):
            work_ref[tile, sy * rows : (sy + 1) * rows, :] = halfway[:, tile * 128 : tile * 128 + 128]
    for x in range(thin):
        plane = [work_ref[tile, pl.ds(x, length, stride=thin), :].astype(bf16) for tile in range(4)]
        stacked = jnp.concatenate(
            [
                jnp.concatenate([plane[0], plane[2]], axis=1),
                jnp.concatenate([plane[1], plane[3]], axis=1),
            ],
            axis=0,
        )
        field = dot(y_ref[...], stacked)
        real, imag = field[:length], field[length:]
        square = real * real + imag * imag
        density = weight_ref[0] * square[:, :length] + weight_ref[1] * square[:, length:]
        density_ref[x * length : (x + 1) * length, :] = density.astype(bf16)
        potential = potential_ref[x]
        potential = jnp.concatenate([potential, potential], axis=1)
        potential = jnp.concatenate([potential, potential], axis=0)
        scaled_ref[x] = (potential * field).astype(bf16)


def fold_kernel(scaled_ref, overlap_ref, z_ref, y_ref, out_ref, work_ref):
    thin = scaled_ref.shape[0]
    length = scaled_ref.shape[1] // 2
    parts = out_ref.shape[0] // 4
    rows = length * thin // parts
    for x in range(thin):
        folded = dot(y_ref[...], scaled_ref[x]).astype(bf16)
        real, imag = folded[:length], folded[length:]
        columns = jnp.concatenate(
            [real[:, :length], imag[:, :length], real[:, length:], imag[:, length:]], axis=1
        )
        halfway = dot(columns, z_ref[...])
        for tile in range(4):
            work_ref[tile, pl.ds(x, length, stride=thin), :] = halfway[:, tile * 128 : tile * 128 + 128]
    for sy in range(parts):
        for sz in range(4):
            block = work_ref[sz, sy * rows : (sy + 1) * rows, :]
            out_ref[sy * 4 + sz, :rows, :] = block.astype(bf16)
    for s in range(out_ref.shape[0]):
        out_ref[s, rows:, :] = overlap_ref[...]


def apply_kernel(
    first_ref,
    returned_ref,
    overlap_ref,
    orbitals_ref,
    mask_ref,
    channels_ref,
    phase_ref,
    wave_ref,
    strength_ref,
    table_ref,
    out_ref,
    factor_ref,
):
    step = pl.program_id(0)
    rows_y, rows_z, length = mask_ref.shape
    atoms = wave_ref.shape[0] // 2
    kinds = channels_ref.shape[0]
    sources = returned_ref.shape[0]
    thin = length // sources

    @pl.when(step == 0)
    def factors():
        cos_x, sin_x = wave_ref[:atoms], wave_ref[atoms:]
        summed = jnp.sum(overlap_ref[...].astype(f32), axis=0)
        coef = (summed[:atoms] + summed[atoms:]) * strength_ref[...]
        for pair in range(kinds * 2):
            coef_real = coef[:, 2 * pair : 2 * pair + 1]
            coef_imag = coef[:, 2 * pair + 1 : 2 * pair + 2]
            real = cos_x * coef_real + sin_x * coef_imag
            imag = cos_x * coef_imag - sin_x * coef_real
            base = pair * 2 * length
            factor_ref[:, base : base + length] = jnp.concatenate([real, imag], axis=0).astype(bf16)
            factor_ref[:, base + length : base + 2 * length] = jnp.concatenate(
                [imag, -real], axis=0
            ).astype(bf16)

    def squared(start, axis):
        index = start + lax.broadcasted_iota(jnp.int32, mask_ref.shape, axis)
        wave = jnp.where(index >= length // 2, index - length, index)
        return wave * wave

    energy = squared(first_ref[0] + step * rows_y, 0) + squared(first_ref[1], 1) + squared(0, 2)
    energy = kinetic_scale * 0.5 * energy.astype(f32)
    inside = mask_ref[...] != 0
    phase = phase_ref[...]
    for pair in range(0, rows_y, 2):
        block = returned_ref[:, pair * thin : (pair + 2) * thin, :].astype(f32)
        planes = jnp.concatenate(
            [
                block[:, :thin].reshape(length, 128).astype(bf16),
                block[:, thin:].reshape(length, 128).astype(bf16),
            ],
            axis=1,
        )
        local = dot_tn(planes, table_ref[...])
        extra = dot_tn(phase[:, pair * rows_z : (pair + 2) * rows_z], factor_ref[...])
        for half in range(2):
            y = pair + half
            top = local[half * 128 : half * 128 + 64, : 2 * length]
            low = local[half * 128 + 64 : half * 128 + 128, 2 * length :]
            both = top + low
            radials = [channels_ref[c, y].astype(f32) for c in range(kinds)]
            for n in range(2):
                for part in range(2):
                    cols = slice(part * length, part * length + length)
                    total = both[n * rows_z : (n + 1) * rows_z, cols]
                    total = total + energy[y] * orbitals_ref[n, y, :, cols].astype(f32)
                    for c in range(kinds):
                        base = ((c * 2 + n) * 2 + part) * length
                        total = total + radials[c] * extra[
                            half * rows_z : (half + 1) * rows_z, base : base + length
                        ]
                    total = jnp.where(inside[y], total, 0.0)
                    out_ref[n, y, :, cols] = total.astype(bf16)


def shards(
    orbitals,
    potential,
    cutoff_mask,
    channels,
    positions,
    proj_atom,
    proj_chan,
    coupling,
    occupations,
):
    rows_y, rows_z, length = cutoff_mask.shape
    parts_y = lax.axis_size("gy")
    parts_z = lax.axis_size("gz")
    parts_band = lax.axis_size("band")
    places = parts_y * parts_z
    thin = length // places
    atoms = positions.shape[0]
    kinds = channels.shape[0]
    block = rows_y * thin
    inverse = dft_table(length, 1.0)
    forward = dft_table(length, -1.0)
    pick = np.eye(2, dtype=np.float32)
    split_inverse = inverse.reshape(2, length, 2, parts_z, rows_z)
    split_forward = forward.reshape(2, parts_z, rows_z, 2, length)
    inv_x = rounded(inverse, 2 * length)
    inv_z = rounded(np.einsum("fzcsl,nm->scnlmfz", split_inverse, pick), 4 * length)
    fwd_z = rounded(np.einsum("cslfz,nm->nfzscml", split_forward, pick), 4 * length)
    fwd_y = rounded(forward, 2 * length)
    fwd_x = rounded(np.einsum("rkcx->xcrk", forward), length)
    first_y = lax.axis_index("gy") * rows_y
    first_z = lax.axis_index("gz") * rows_z

    params = pltpu.CompilerParams(vmem_limit_bytes=vmem_bytes)
    steps = 4
    span = rows_y // steps
    whole = lambda *shape: pl.BlockSpec(shape, lambda i: (0,) * len(shape))
    orbitals_spec = pl.BlockSpec((2, span, rows_z, 2 * length), lambda i: (0, i, 0, 0))
    mask_spec = pl.BlockSpec((span, rows_z, length), lambda i: (i, 0, 0))
    channels_spec = pl.BlockSpec((kinds, span, rows_z, length), lambda i: (0, i, 0, 0))
    phase_spec = pl.BlockSpec((2 * atoms, span * rows_z), lambda i: (0, i))
    blocks_spec = pl.BlockSpec((places, span * thin, 128), lambda i: (0, i, 0))
    tile_spec = pl.BlockSpec((places, 16, 128), lambda i: (0, block // 16, 0))
    smem_spec = pl.BlockSpec(memory_space=pltpu.SMEM)

    spread = pl.pallas_call(
        spread_kernel,
        grid=(steps,),
        in_specs=[orbitals_spec, mask_spec, whole(2 * length, 2 * length)],
        out_specs=blocks_spec,
        out_shape=jax.ShapeDtypeStruct((places, block, 128), bf16),
        compiler_params=params,
        name="spread",
    )(orbitals, cutoff_mask, inv_x)
    arrived = lax.all_to_all(spread, ("gy", "gz"), split_axis=0, concat_axis=0, tiled=True)

    cos_y, sin_y = axis_phase(positions[:, 1], frequencies(first_y, rows_y, length))
    cos_z, sin_z = axis_phase(positions[:, 2], frequencies(first_z, rows_z, length))
    cos_x, sin_x = axis_phase(positions[:, 0], frequencies(0, length, length))
    cos_yz = cos_y[:, :, None] * cos_z[:, None, :] - sin_y[:, :, None] * sin_z[:, None, :]
    sin_yz = sin_y[:, :, None] * cos_z[:, None, :] + cos_y[:, :, None] * sin_z[:, None, :]
    phase = jnp.concatenate([cos_yz, sin_yz], axis=0).astype(bf16).reshape(2 * atoms, rows_y * rows_z)
    wave = jnp.concatenate([cos_x, sin_x], axis=0)
    chosen = (proj_atom[None, :] == jnp.arange(atoms, dtype=jnp.int32)[:, None])[:, None, :] & (
        proj_chan[None, :] == jnp.arange(kinds, dtype=jnp.int32)[:, None]
    )[None, :, :]
    strength = jnp.sum(jnp.where(chosen, coupling[None, None, :], 0.0), axis=2)
    strength = jnp.pad(jnp.repeat(strength, 4, axis=1), ((0, 0), (0, 128 - 4 * kinds)))

    overlap = pl.pallas_call(
        overlap_kernel,
        grid=(steps,),
        in_specs=[orbitals_spec, mask_spec, channels_spec, phase_spec, whole(2 * atoms, length)],
        out_specs=whole(2 * atoms, 128),
        out_shape=jax.ShapeDtypeStruct((2 * atoms, 128), bf16),
        scratch_shapes=[pltpu.VMEM((2 * atoms, kinds * 4 * length), f32)],
        compiler_params=params,
        name="overlap",
    )(orbitals, cutoff_mask, channels, phase, wave)

    density_part, scaled = pl.pallas_call(
        field_kernel,
        grid=(1,),
        in_specs=[
            whole(places, block, 128),
            whole(thin, length, length),
            smem_spec,
            whole(4 * length, 4 * length),
            whole(2 * length, 2 * length),
        ],
        out_specs=[whole(thin * length, length), whole(thin, 2 * length, 2 * length)],
        out_shape=[
            jax.ShapeDtypeStruct((thin * length, length), bf16),
            jax.ShapeDtypeStruct((thin, 2 * length, 2 * length), bf16),
        ],
        scratch_shapes=[pltpu.VMEM((4, length * thin, 128), f32)],
        compiler_params=params,
        name="field",
    )(arrived, potential, occupations, inv_z, inv_x)
    density_parts = lax.all_to_all(
        density_part.reshape(parts_band, -1, length), "band", split_axis=0, concat_axis=0, tiled=True
    )

    folded = pl.pallas_call(
        fold_kernel,
        grid=(1,),
        in_specs=[
            whole(thin, 2 * length, 2 * length),
            whole(2 * atoms, 128),
            whole(4 * length, 4 * length),
            whole(2 * length, 2 * length),
        ],
        out_specs=whole(places, block + 16, 128),
        out_shape=jax.ShapeDtypeStruct((places, block + 16, 128), bf16),
        scratch_shapes=[pltpu.VMEM((4, length * thin, 128), f32)],
        compiler_params=params,
        name="fold",
    )(scaled, overlap, fwd_z, fwd_y)
    returned = lax.all_to_all(folded, ("gy", "gz"), split_axis=0, concat_axis=0, tiled=True)

    density_own = jnp.sum(density_parts.astype(f32), axis=0).astype(bf16)
    density_copies = jnp.broadcast_to(density_own[None], density_parts.shape)
    density = lax.all_to_all(density_copies, "band", split_axis=0, concat_axis=0, tiled=True)

    applied = pl.pallas_call(
        apply_kernel,
        grid=(steps,),
        in_specs=[
            smem_spec,
            blocks_spec,
            tile_spec,
            orbitals_spec,
            mask_spec,
            channels_spec,
            phase_spec,
            whole(2 * atoms, length),
            whole(atoms, 128),
            whole(length, 4 * length),
        ],
        out_specs=orbitals_spec,
        out_shape=jax.ShapeDtypeStruct(orbitals.shape, bf16),
        scratch_shapes=[pltpu.VMEM((2 * atoms, kinds * 4 * length), bf16)],
        compiler_params=params,
        name="apply",
    )(
        jnp.stack([first_y, first_z]).astype(jnp.int32),
        returned,
        returned,
        orbitals,
        cutoff_mask,
        channels,
        phase,
        wave,
        strength,
        fwd_x,
    )
    return (applied, density.astype(f32).reshape(potential.shape))


def solution(mesh):
    placed = (
        P("band", "gy", "gz", None),
        P(("gy", "gz"), None, None),
        P("gy", "gz", None),
        P(None, "gy", "gz", None),
        P(),
        P(),
        P(),
        P(),
        P("band"),
    )
    return jax.shard_map(
        shards,
        mesh=mesh,
        in_specs=placed,
        out_specs=(P("band", "gy", "gz", None), P(("gy", "gz"), None, None)),
        check_vma=False,
    )
```

```python
import functools
import math

import jax
import jax.numpy as jnp
import ml_dtypes
import numpy as np
from jax import lax
from jax.experimental import pallas as pl
from jax.experimental.pallas import tpu as pltpu
from jax.sharding import PartitionSpec as P

kinetic_scale = 1.0 / 1024.0
vmem_bytes = 60 * 1024 * 1024
bf16 = jnp.bfloat16
f32 = jnp.float32


def dft_table(length, sign_value):
    grid_index = np.arange(length)
    product = grid_index[:, None] * grid_index[None, :] % length
    phase_angle = np.float32(2.0 * math.pi / length) * product.astype(np.float32)
    cosine_part = np.cos(phase_angle) / np.float32(math.sqrt(length))
    sine_part = sign_value * np.sin(phase_angle) / np.float32(math.sqrt(length))
    upper_rows = np.stack([cosine_part, -sine_part], axis=1)
    lower_rows = np.stack([sine_part, cosine_part], axis=1)
    return np.stack([upper_rows, lower_rows], axis=0).astype(np.float32)


def rounded(table, rows):
    return jnp.asarray(np.ascontiguousarray(table).reshape(rows, -1).astype(ml_dtypes.bfloat16))


def frequencies(first_index, span, length):
    grid_index = first_index + jnp.arange(span, dtype=jnp.int32)
    return jnp.where(grid_index >= length // 2, grid_index - length, grid_index).astype(f32)


def axis_phase(coordinate, freq):
    phase_angle = 2.0 * math.pi * (coordinate[:, None] * freq[None, :])
    return (jnp.cos(phase_angle), jnp.sin(phase_angle))


def dot(left, right):
    return jnp.dot(left, right, preferred_element_type=f32)


def dot_nt(left, right):
    return lax.dot_general(left, right, (((1,), (1,)), ((), ())), preferred_element_type=f32)


def dot_tn(left, right):
    return lax.dot_general(left, right, (((0,), (0,)), ((), ())), preferred_element_type=f32)


def spread_kernel(orbitals_ref, mask_ref, table_ref, out_ref):
    length = mask_ref.shape[2]
    dests = out_ref.shape[0]
    thin = length // dests
    mask = jnp.where(mask_ref[...] != 0, 1.0, 0.0).astype(bf16)
    mask = jnp.concatenate([mask, mask], axis=2)
    lane = lax.broadcasted_iota(jnp.int32, (length, 128), 1)
    for pair in range(0, mask_ref.shape[0], 2):
        rows = []
        for y in (pair, pair + 1):
            both = jnp.concatenate([orbitals_ref[0, y] * mask[y], orbitals_ref[1, y] * mask[y]], axis=0)
            rows += [both, both]
        spread = dot_nt(table_ref[...], jnp.concatenate(rows, axis=0))
        tiles = []
        for half in range(2):
            cols = slice(half * 128, half * 128 + 128)
            tile = jnp.where(lane < 64, spread[:length, cols], spread[length:, cols])
            tiles.append(tile.reshape(dests, thin, 128))
        out_ref[:, pair * thin : (pair + 2) * thin, :] = jnp.concatenate(tiles, axis=1).astype(bf16)


def overlap_kernel(orbitals_ref, mask_ref, channels_ref, phase_ref, wave_ref, out_ref, sums_ref):
    step = pl.program_id(0)
    rows = mask_ref.shape[0] * mask_ref.shape[1]
    length = mask_ref.shape[2]
    atoms = wave_ref.shape[0] // 2
    kinds = channels_ref.shape[0]
    mask = jnp.where(mask_ref[...] != 0, 1.0, 0.0).astype(bf16)
    orbs = [orbitals_ref[n].reshape(rows, 2 * length) for n in range(2)]
    columns = []
    for c in range(kinds):
        radial = (channels_ref[c] * mask).reshape(rows, length)
        radial = jnp.concatenate([radial, radial], axis=1)
        columns += [radial * orbs[0], radial * orbs[1]]
    part = dot(phase_ref[...], jnp.concatenate(columns, axis=1))

    @pl.when(step == 0)
    def first():
        sums_ref[...] = part

    @pl.when(step > 0)
    def later():
        sums_ref[...] += part

    @pl.when(step == pl.num_programs(0) - 1)
    def last():
        cos_x, sin_x = wave_ref[:atoms], wave_ref[atoms:]
        lane = lax.broadcasted_iota(jnp.int32, (atoms, 128), 1)
        total = jnp.zeros((atoms, 128), f32)
        for pair in range(kinds * 2):
            base = pair * 2 * length
            real_cols = slice(base, base + length)
            imag_cols = slice(base + length, base + 2 * length)
            real = sums_ref[:atoms, real_cols] - sums_ref[atoms:, imag_cols]
            imag = sums_ref[atoms:, real_cols] + sums_ref[:atoms, imag_cols]
            real_over = jnp.sum(real * cos_x - imag * sin_x, axis=1, keepdims=True)
            imag_over = jnp.sum(real * sin_x + imag * cos_x, axis=1, keepdims=True)
            total = jnp.where(lane == 2 * pair, real_over, total)
            total = jnp.where(lane == 2 * pair + 1, imag_over, total)
        high = total.astype(bf16).astype(f32)
        out_ref[...] = jnp.concatenate([high, total - high], axis=0).astype(bf16)


def field_kernel(arrived_ref, potential_ref, weight_ref, z_ref, y_ref, density_ref, scaled_ref, work_ref):
    thin = potential_ref.shape[0]
    length = potential_ref.shape[1]
    parts = arrived_ref.shape[0] // 4
    rows = arrived_ref.shape[1]
    for sy in range(parts):
        columns = jnp.concatenate([arrived_ref[sy * 4 + sz] for sz in range(4)], axis=1)
        halfway = dot(columns, z_ref[...])
        for tile in range(4):
            work_ref[tile, sy * rows : (sy + 1) * rows, :] = halfway[:, tile * 128 : tile * 128 + 128]
    for x in range(thin):
        plane = [work_ref[tile, pl.ds(x, length, stride=thin), :].astype(bf16) for tile in range(4)]
        stacked = jnp.concatenate(
            [
                jnp.concatenate([plane[0], plane[2]], axis=1),
                jnp.concatenate([plane[1], plane[3]], axis=1),
            ],
            axis=0,
        )
        field = dot(y_ref[...], stacked)
        real, imag = field[:length], field[length:]
        square = real * real + imag * imag
        density = weight_ref[0] * square[:, :length] + weight_ref[1] * square[:, length:]
        density_ref[x * length : (x + 1) * length, :] = density.astype(bf16)
        potential = potential_ref[x]
        potential = jnp.concatenate([potential, potential], axis=1)
        potential = jnp.concatenate([potential, potential], axis=0)
        scaled_ref[x] = (potential * field).astype(bf16)


def fold_kernel(scaled_ref, overlap_ref, z_ref, y_ref, out_ref, work_ref):
    thin = scaled_ref.shape[0]
    length = scaled_ref.shape[1] // 2
    parts = out_ref.shape[0] // 4
    rows = length * thin // parts
    for x in range(thin):
        folded = dot(y_ref[...], scaled_ref[x]).astype(bf16)
        real, imag = folded[:length], folded[length:]
        columns = jnp.concatenate(
            [real[:, :length], imag[:, :length], real[:, length:], imag[:, length:]], axis=1
        )
        halfway = dot(columns, z_ref[...])
        for tile in range(4):
            work_ref[tile, pl.ds(x, length, stride=thin), :] = halfway[:, tile * 128 : tile * 128 + 128]
    for sy in range(parts):
        for sz in range(4):
            block = work_ref[sz, sy * rows : (sy + 1) * rows, :]
            out_ref[sy * 4 + sz, :rows, :] = block.astype(bf16)
    for s in range(out_ref.shape[0]):
        out_ref[s, rows:, :] = overlap_ref[...]


def apply_kernel(
    first_ref,
    returned_ref,
    overlap_ref,
    orbitals_ref,
    mask_ref,
    channels_ref,
    phase_ref,
    wave_ref,
    strength_ref,
    table_ref,
    out_ref,
    factor_ref,
):
    step = pl.program_id(0)
    rows_y, rows_z, length = mask_ref.shape
    atoms = wave_ref.shape[0] // 2
    kinds = channels_ref.shape[0]
    sources = returned_ref.shape[0]
    thin = length // sources

    @pl.when(step == 0)
    def factors():
        cos_x, sin_x = wave_ref[:atoms], wave_ref[atoms:]
        summed = jnp.sum(overlap_ref[...].astype(f32), axis=0)
        coef = (summed[:atoms] + summed[atoms:]) * strength_ref[...]
        for pair in range(kinds * 2):
            coef_real = coef[:, 2 * pair : 2 * pair + 1]
            coef_imag = coef[:, 2 * pair + 1 : 2 * pair + 2]
            real = cos_x * coef_real + sin_x * coef_imag
            imag = cos_x * coef_imag - sin_x * coef_real
            base = pair * 2 * length
            factor_ref[:, base : base + length] = jnp.concatenate([real, imag], axis=0).astype(bf16)
            factor_ref[:, base + length : base + 2 * length] = jnp.concatenate(
                [imag, -real], axis=0
            ).astype(bf16)

    def squared(start, axis):
        index = start + lax.broadcasted_iota(jnp.int32, mask_ref.shape, axis)
        wave = jnp.where(index >= length // 2, index - length, index)
        return wave * wave

    energy = squared(first_ref[0] + step * rows_y, 0) + squared(first_ref[1], 1) + squared(0, 2)
    energy = kinetic_scale * 0.5 * energy.astype(f32)
    inside = mask_ref[...] != 0
    phase = phase_ref[...]
    for pair in range(0, rows_y, 2):
        block = returned_ref[:, pair * thin : (pair + 2) * thin, :].astype(f32)
        planes = jnp.concatenate(
            [
                block[:, :thin].reshape(length, 128).astype(bf16),
                block[:, thin:].reshape(length, 128).astype(bf16),
            ],
            axis=1,
        )
        local = dot_tn(planes, table_ref[...])
        extra = dot_tn(phase[:, pair * rows_z : (pair + 2) * rows_z], factor_ref[...])
        for half in range(2):
            y = pair + half
            top = local[half * 128 : half * 128 + 64, : 2 * length]
            low = local[half * 128 + 64 : half * 128 + 128, 2 * length :]
            both = top + low
            radials = [channels_ref[c, y].astype(f32) for c in range(kinds)]
            for n in range(2):
                for part in range(2):
                    cols = slice(part * length, part * length + length)
                    total = both[n * rows_z : (n + 1) * rows_z, cols]
                    total = total + energy[y] * orbitals_ref[n, y, :, cols].astype(f32)
                    for c in range(kinds):
                        base = ((c * 2 + n) * 2 + part) * length
                        total = total + radials[c] * extra[
                            half * rows_z : (half + 1) * rows_z, base : base + length
                        ]
                    total = jnp.where(inside[y], total, 0.0)
                    out_ref[n, y, :, cols] = total.astype(bf16)


def shards(
    orbitals,
    potential,
    cutoff_mask,
    channels,
    positions,
    proj_atom,
    proj_chan,
    coupling,
    occupations,
):
    rows_y, rows_z, length = cutoff_mask.shape
    parts_y = lax.axis_size("gy")
    parts_z = lax.axis_size("gz")
    parts_band = lax.axis_size("band")
    places = parts_y * parts_z
    thin = length // places
    atoms = positions.shape[0]
    kinds = channels.shape[0]
    block = rows_y * thin
    inverse = dft_table(length, 1.0)
    forward = dft_table(length, -1.0)
    pick = np.eye(2, dtype=np.float32)
    split_inverse = inverse.reshape(2, length, 2, parts_z, rows_z)
    split_forward = forward.reshape(2, parts_z, rows_z, 2, length)
    inv_x = rounded(inverse, 2 * length)
    inv_z = rounded(np.einsum("fzcsl,nm->scnlmfz", split_inverse, pick), 4 * length)
    fwd_z = rounded(np.einsum("cslfz,nm->nfzscml", split_forward, pick), 4 * length)
    fwd_y = rounded(forward, 2 * length)
    fwd_x = rounded(np.einsum("rkcx->xcrk", forward), length)
    first_y = lax.axis_index("gy") * rows_y
    first_z = lax.axis_index("gz") * rows_z

    params = pltpu.CompilerParams(vmem_limit_bytes=vmem_bytes)
    steps = 4
    span = rows_y // steps
    whole = lambda *shape: pl.BlockSpec(shape, lambda i: (0,) * len(shape))
    orbitals_spec = pl.BlockSpec((2, span, rows_z, 2 * length), lambda i: (0, i, 0, 0))
    mask_spec = pl.BlockSpec((span, rows_z, length), lambda i: (i, 0, 0))
    channels_spec = pl.BlockSpec((kinds, span, rows_z, length), lambda i: (0, i, 0, 0))
    phase_spec = pl.BlockSpec((2 * atoms, span * rows_z), lambda i: (0, i))
    blocks_spec = pl.BlockSpec((places, span * thin, 128), lambda i: (0, i, 0))
    tile_spec = pl.BlockSpec((places, 16, 128), lambda i: (0, block // 16, 0))
    smem_spec = pl.BlockSpec(memory_space=pltpu.SMEM)

    spread = pl.pallas_call(
        spread_kernel,
        grid=(steps,),
        in_specs=[orbitals_spec, mask_spec, whole(2 * length, 2 * length)],
        out_specs=blocks_spec,
        out_shape=jax.ShapeDtypeStruct((places, block, 128), bf16),
        compiler_params=params,
        name="spread",
    )(orbitals, cutoff_mask, inv_x)
    arrived = lax.all_to_all(spread, ("gy", "gz"), split_axis=0, concat_axis=0, tiled=True)

    cos_y, sin_y = axis_phase(positions[:, 1], frequencies(first_y, rows_y, length))
    cos_z, sin_z = axis_phase(positions[:, 2], frequencies(first_z, rows_z, length))
    cos_x, sin_x = axis_phase(positions[:, 0], frequencies(0, length, length))
    cos_yz = cos_y[:, :, None] * cos_z[:, None, :] - sin_y[:, :, None] * sin_z[:, None, :]
    sin_yz = sin_y[:, :, None] * cos_z[:, None, :] + cos_y[:, :, None] * sin_z[:, None, :]
    phase = jnp.concatenate([cos_yz, sin_yz], axis=0).astype(bf16).reshape(2 * atoms, rows_y * rows_z)
    wave = jnp.concatenate([cos_x, sin_x], axis=0)
    chosen = (proj_atom[None, :] == jnp.arange(atoms, dtype=jnp.int32)[:, None])[:, None, :] & (
        proj_chan[None, :] == jnp.arange(kinds, dtype=jnp.int32)[:, None]
    )[None, :, :]
    strength = jnp.sum(jnp.where(chosen, coupling[None, None, :], 0.0), axis=2)
    strength = jnp.pad(jnp.repeat(strength, 4, axis=1), ((0, 0), (0, 128 - 4 * kinds)))

    overlap = pl.pallas_call(
        overlap_kernel,
        grid=(steps,),
        in_specs=[orbitals_spec, mask_spec, channels_spec, phase_spec, whole(2 * atoms, length)],
        out_specs=whole(2 * atoms, 128),
        out_shape=jax.ShapeDtypeStruct((2 * atoms, 128), bf16),
        scratch_shapes=[pltpu.VMEM((2 * atoms, kinds * 4 * length), f32)],
        compiler_params=params,
        name="overlap",
    )(orbitals, cutoff_mask, channels, phase, wave)

    density_part, scaled = pl.pallas_call(
        field_kernel,
        grid=(1,),
        in_specs=[
            whole(places, block, 128),
            whole(thin, length, length),
            smem_spec,
            whole(4 * length, 4 * length),
            whole(2 * length, 2 * length),
        ],
        out_specs=[whole(thin * length, length), whole(thin, 2 * length, 2 * length)],
        out_shape=[
            jax.ShapeDtypeStruct((thin * length, length), bf16),
            jax.ShapeDtypeStruct((thin, 2 * length, 2 * length), bf16),
        ],
        scratch_shapes=[pltpu.VMEM((4, length * thin, 128), f32)],
        compiler_params=params,
        name="field",
    )(arrived, potential, occupations, inv_z, inv_x)
    density_parts = lax.all_to_all(
        density_part.reshape(parts_band, -1, length), "band", split_axis=0, concat_axis=0, tiled=True
    )

    folded = pl.pallas_call(
        fold_kernel,
        grid=(1,),
        in_specs=[
            whole(thin, 2 * length, 2 * length),
            whole(2 * atoms, 128),
            whole(4 * length, 4 * length),
            whole(2 * length, 2 * length),
        ],
        out_specs=whole(places, block + 16, 128),
        out_shape=jax.ShapeDtypeStruct((places, block + 16, 128), bf16),
        scratch_shapes=[pltpu.VMEM((4, length * thin, 128), f32)],
        compiler_params=params,
        name="fold",
    )(scaled, overlap, fwd_z, fwd_y)
    returned = lax.all_to_all(folded, ("gy", "gz"), split_axis=0, concat_axis=0, tiled=True)

    density_own = jnp.sum(density_parts.astype(f32), axis=0).astype(bf16)
    density_own, returned = lax.optimization_barrier((density_own, returned))
    density_copies = jnp.broadcast_to(density_own[None], density_parts.shape)
    density = lax.all_to_all(density_copies, "band", split_axis=0, concat_axis=0, tiled=True)

    applied = pl.pallas_call(
        apply_kernel,
        grid=(steps,),
        in_specs=[
            smem_spec,
            blocks_spec,
            tile_spec,
            orbitals_spec,
            mask_spec,
            channels_spec,
            phase_spec,
            whole(2 * atoms, length),
            whole(atoms, 128),
            whole(length, 4 * length),
        ],
        out_specs=orbitals_spec,
        out_shape=jax.ShapeDtypeStruct(orbitals.shape, bf16),
        scratch_shapes=[pltpu.VMEM((2 * atoms, kinds * 4 * length), bf16)],
        compiler_params=params,
        name="apply",
    )(
        jnp.stack([first_y, first_z]).astype(jnp.int32),
        returned,
        returned,
        orbitals,
        cutoff_mask,
        channels,
        phase,
        wave,
        strength,
        fwd_x,
    )
    return (applied, density.astype(f32).reshape(potential.shape))


def solution(mesh):
    placed = (
        P("band", "gy", "gz", None),
        P(("gy", "gz"), None, None),
        P("gy", "gz", None),
        P(None, "gy", "gz", None),
        P(),
        P(),
        P(),
        P(),
        P("band"),
    )
    return jax.shard_map(
        shards,
        mesh=mesh,
        in_specs=placed,
        out_specs=(P("band", "gy", "gz", None), P(("gy", "gz"), None, None)),
        check_vma=False,
    )
```

```python
import functools
import math

import jax
import jax.numpy as jnp
import ml_dtypes
import numpy as np
from jax import lax
from jax.experimental import pallas as pl
from jax.experimental.pallas import tpu as pltpu
from jax.sharding import PartitionSpec as P

kinetic_scale = 1.0 / 1024.0
vmem_bytes = 63 * 1024 * 1024
bf16 = jnp.bfloat16
f32 = jnp.float32


def dft_table(length, sign_value):
    grid_index = np.arange(length)
    product = grid_index[:, None] * grid_index[None, :] % length
    phase_angle = np.float32(2.0 * math.pi / length) * product.astype(np.float32)
    cosine_part = np.cos(phase_angle) / np.float32(math.sqrt(length))
    sine_part = sign_value * np.sin(phase_angle) / np.float32(math.sqrt(length))
    upper_rows = np.stack([cosine_part, -sine_part], axis=1)
    lower_rows = np.stack([sine_part, cosine_part], axis=1)
    return np.stack([upper_rows, lower_rows], axis=0).astype(np.float32)


def rounded(table, rows):
    return jnp.asarray(np.ascontiguousarray(table).reshape(rows, -1).astype(ml_dtypes.bfloat16))


def frequencies(first_index, span, length):
    grid_index = first_index + jnp.arange(span, dtype=jnp.int32)
    return jnp.where(grid_index >= length // 2, grid_index - length, grid_index).astype(f32)


def axis_phase(coordinate, freq):
    phase_angle = 2.0 * math.pi * (coordinate[:, None] * freq[None, :])
    return (jnp.cos(phase_angle), jnp.sin(phase_angle))


def dot(left, right):
    return jnp.dot(left, right, preferred_element_type=f32)


def dot_nt(left, right):
    return lax.dot_general(left, right, (((1,), (1,)), ((), ())), preferred_element_type=f32)


def dot_tn(left, right):
    return lax.dot_general(left, right, (((0,), (0,)), ((), ())), preferred_element_type=f32)


def root_weights(weight_ref, shape, axis, span):
    index = lax.broadcasted_iota(jnp.int32, shape, axis)
    return jnp.sqrt(jnp.where(index // span % 2 == 0, weight_ref[0], weight_ref[1]))


def spread_kernel(orbitals_ref, mask_ref, weight_ref, table_ref, out_ref, work_ref):
    rows_y, rows_z, length = mask_ref.shape
    mask = jnp.where(mask_ref[...] != 0, 1.0, 0.0).astype(bf16)
    mask = jnp.concatenate([mask, mask], axis=2)
    lane = lax.broadcasted_iota(jnp.int32, (length, 128), 1)
    roots = root_weights(weight_ref, (1, 128), 1, rows_z)
    for pair in range(0, rows_y, 2):
        rows = []
        for y in (pair, pair + 1):
            both = jnp.concatenate([orbitals_ref[0, y] * mask[y], orbitals_ref[1, y] * mask[y]], axis=0)
            rows += [both, both]
        spread = dot_nt(table_ref[...], jnp.concatenate(rows, axis=0))
        for half in range(2):
            cols = slice(half * 128, half * 128 + 128)
            tile = jnp.where(lane < 64, spread[:length, cols], spread[length:, cols])
            work_ref[pl.ds(pair + half, length, stride=rows_y), :] = tile * roots
    out_ref[...] = work_ref[...].reshape(out_ref.shape).astype(bf16)


def overlap_kernel(orbitals_ref, mask_ref, channels_ref, phase_ref, wave_ref, out_ref, sums_ref):
    step = pl.program_id(0)
    rows = mask_ref.shape[0] * mask_ref.shape[1]
    length = mask_ref.shape[2]
    atoms = wave_ref.shape[0] // 2
    kinds = channels_ref.shape[0]
    mask = jnp.where(mask_ref[...] != 0, 1.0, 0.0).astype(bf16)
    orbs = [orbitals_ref[n].reshape(rows, 2 * length) for n in range(2)]
    columns = []
    for c in range(kinds):
        radial = (channels_ref[c] * mask).reshape(rows, length)
        radial = jnp.concatenate([radial, radial], axis=1)
        columns += [radial * orbs[0], radial * orbs[1]]
    part = dot(phase_ref[...], jnp.concatenate(columns, axis=1))

    @pl.when(step == 0)
    def first():
        sums_ref[...] = part

    @pl.when(step > 0)
    def later():
        sums_ref[...] += part

    @pl.when(step == pl.num_programs(0) - 1)
    def last():
        cos_x, sin_x = wave_ref[:atoms], wave_ref[atoms:]
        lane = lax.broadcasted_iota(jnp.int32, (atoms, 128), 1)
        total = jnp.zeros((atoms, 128), f32)
        for pair in range(kinds * 2):
            base = pair * 2 * length
            real_cols = slice(base, base + length)
            imag_cols = slice(base + length, base + 2 * length)
            real = sums_ref[:atoms, real_cols] - sums_ref[atoms:, imag_cols]
            imag = sums_ref[atoms:, real_cols] + sums_ref[:atoms, imag_cols]
            real_over = jnp.sum(real * cos_x - imag * sin_x, axis=1, keepdims=True)
            imag_over = jnp.sum(real * sin_x + imag * cos_x, axis=1, keepdims=True)
            total = jnp.where(lane == 2 * pair, real_over, total)
            total = jnp.where(lane == 2 * pair + 1, imag_over, total)
        out_ref[...] = total


def field_kernel(
    arrived_ref,
    potential_ref,
    inv_z_ref,
    inv_y_ref,
    fwd_z_ref,
    fwd_y_ref,
    density_ref,
    out_ref,
    sums_ref,
):
    step = pl.program_id(0)
    planes, length = potential_ref.shape[:2]
    parts = arrived_ref.shape[0] // 4
    rows = arrived_ref.shape[1] // planes
    columns = jnp.concatenate(
        [jnp.concatenate([arrived_ref[sy * 4 + sz] for sz in range(4)], axis=1) for sy in range(parts)],
        axis=0,
    )
    halfway = dot(columns, inv_z_ref[...]).astype(bf16)
    stacked = []
    for x in range(planes):
        first = [(sy * planes + x) * rows for sy in range(parts)]
        plane = jnp.concatenate([halfway[start : start + rows] for start in first], axis=0)
        real = jnp.concatenate([plane[:, 0:128], plane[:, 256:384]], axis=1)
        imag = jnp.concatenate([plane[:, 128:256], plane[:, 384:512]], axis=1)
        stacked.append(jnp.concatenate([real, imag], axis=0))
    fields = [dot(inv_y_ref[...], block) for block in stacked]
    scaled = []
    for x, field in enumerate(fields):
        real, imag = field[:length], field[length:]
        square = real * real + imag * imag
        density = square[:, :length] + square[:, length:]
        here = slice(x * length, (x + 1) * length)
        sums_ref[here, :] = jnp.where(step == 0, density, sums_ref[here, :] + density)
        potential = jnp.concatenate([potential_ref[x], potential_ref[x]], axis=1)
        potential = jnp.concatenate([potential, potential], axis=0)
        scaled.append((potential * field).astype(bf16))
    folded = [dot(fwd_y_ref[...], block).astype(bf16) for block in scaled]
    back = []
    for block in folded:
        real, imag = block[:length], block[length:]
        back.append(
            jnp.concatenate([real[:, :length], imag[:, :length], real[:, length:], imag[:, length:]], axis=1)
        )
    back = dot(jnp.concatenate(back, axis=0), fwd_z_ref[...]).astype(bf16)
    for x in range(planes):
        for sy in range(parts):
            start = x * length + sy * rows
            for sz in range(4):
                out_ref[sy * 4 + sz, x * rows : (x + 1) * rows, :] = back[
                    start : start + rows, sz * 128 : sz * 128 + 128
                ]

    @pl.when(step == pl.num_programs(0) - 1)
    def last():
        density_ref[...] = sums_ref[...].astype(bf16)


def base_kernel(
    first_ref,
    overlap_ref,
    orbitals_ref,
    mask_ref,
    channels_ref,
    phase_ref,
    wave_ref,
    strength_ref,
    out_ref,
    factor_ref,
):
    step = pl.program_id(0)
    rows_y, rows_z, length = mask_ref.shape
    atoms = wave_ref.shape[0] // 2
    kinds = channels_ref.shape[0]

    @pl.when(step == 0)
    def factors():
        cos_x, sin_x = wave_ref[:atoms], wave_ref[atoms:]
        coef = overlap_ref[...] * strength_ref[...]
        for pair in range(kinds * 2):
            coef_real = coef[:, 2 * pair : 2 * pair + 1]
            coef_imag = coef[:, 2 * pair + 1 : 2 * pair + 2]
            real = cos_x * coef_real + sin_x * coef_imag
            imag = cos_x * coef_imag - sin_x * coef_real
            base = pair * 2 * length
            factor_ref[:, base : base + length] = jnp.concatenate([real, imag], axis=0).astype(bf16)
            factor_ref[:, base + length : base + 2 * length] = jnp.concatenate(
                [imag, -real], axis=0
            ).astype(bf16)

    def squared(start, axis):
        index = start + lax.broadcasted_iota(jnp.int32, mask_ref.shape, axis)
        wave = jnp.where(index >= length // 2, index - length, index)
        return wave * wave

    energy = squared(first_ref[0] + step * rows_y, 0) + squared(first_ref[1], 1) + squared(0, 2)
    energy = kinetic_scale * 0.5 * energy.astype(f32)
    for y in range(rows_y):
        extra = dot_tn(phase_ref[:, y * rows_z : (y + 1) * rows_z], factor_ref[...])
        radials = [channels_ref[c, y].astype(f32) for c in range(kinds)]
        for n in range(2):
            for part in range(2):
                cols = slice(part * length, part * length + length)
                total = energy[y] * orbitals_ref[n, y, :, cols].astype(f32)
                for c in range(kinds):
                    base = ((c * 2 + n) * 2 + part) * length
                    total = total + radials[c] * extra[:, base : base + length]
                out_ref[n, y, :, cols] = total


def apply_kernel(returned_ref, base_ref, mask_ref, weight_ref, table_ref, out_ref, work_ref):
    rows_y, rows_z, length = mask_ref.shape
    scale = 1.0 / root_weights(weight_ref, (2 * rows_z, 1), 0, rows_z)
    work_ref[...] = returned_ref[...].astype(f32).reshape(work_ref.shape)
    inside = mask_ref[...] != 0
    for pair in range(0, rows_y, 2):
        planes = jnp.concatenate(
            [work_ref[pl.ds(y, length, stride=rows_y), :].astype(bf16) for y in (pair, pair + 1)], axis=1
        )
        local = dot_tn(planes, table_ref[...])
        for half in range(2):
            y = pair + half
            both = local[half * 128 : half * 128 + 64, : 2 * length]
            both = scale * (both + local[half * 128 + 64 : half * 128 + 128, 2 * length :])
            keep = jnp.concatenate([inside[y], inside[y]], axis=1)
            for n in range(2):
                total = both[n * rows_z : (n + 1) * rows_z] + base_ref[n, y]
                out_ref[n, y] = jnp.where(keep, total, 0.0).astype(bf16)


def partners(axis, distance):
    return [(i, i ^ distance) for i in range(lax.axis_size(axis))]


def sum_over(part, axis, distances):
    got = [lax.ppermute(part, axis, partners(axis, d)).astype(f32) for d in distances]
    return (part.astype(f32) + got[0]) + (got[1] + got[2])


def shards(
    orbitals,
    potential,
    cutoff_mask,
    channels,
    positions,
    proj_atom,
    proj_chan,
    coupling,
    occupations,
):
    rows_y, rows_z, length = cutoff_mask.shape
    parts_y = lax.axis_size("gy")
    parts_z = lax.axis_size("gz")
    parts_band = lax.axis_size("band")
    places = parts_y * parts_z
    bands = 2
    outer = parts_band // bands
    thin = length // places
    planes = thin // bands
    atoms = positions.shape[0]
    kinds = channels.shape[0]
    groups = [
        [(first * bands + b) * places + place for b in range(bands) for place in range(places)]
        for first in range(outer)
    ]
    inverse = dft_table(length, 1.0)
    forward = dft_table(length, -1.0)
    pick = np.eye(2, dtype=np.float32)
    split_inverse = inverse.reshape(2, length, 2, parts_z, rows_z)
    split_forward = forward.reshape(2, parts_z, rows_z, 2, length)
    order = np.arange(length).reshape(places, bands, planes).transpose(1, 0, 2).reshape(-1)
    inv_x = rounded(inverse[:, order], 2 * length)
    inv_y = rounded(inverse, 2 * length)
    inv_z = rounded(np.einsum("fzcsl,nm->scnlmfz", split_inverse, pick), 4 * length)
    fwd_z = rounded(np.einsum("cslfz,nm->nfzscml", split_forward, pick), 4 * length)
    fwd_y = rounded(forward, 2 * length)
    fwd_x = rounded(np.einsum("rkcx->xcrk", forward[..., order]), length)
    first_y = lax.axis_index("gy") * rows_y
    first_z = lax.axis_index("gz") * rows_z
    band = lax.axis_index("band") % bands

    params = pltpu.CompilerParams(vmem_limit_bytes=vmem_bytes)

    def cost(microseconds):
        return pl.CostEstimate(
            flops=int(microseconds * 1.0e9), bytes_accessed=int(microseconds * 1.0e6), transcendentals=0
        )

    steps = 2
    span = rows_y // steps
    whole = lambda *shape: pl.BlockSpec(shape, lambda i: (0,) * len(shape))
    orbitals_spec = pl.BlockSpec((2, span, rows_z, 2 * length), lambda i: (0, i, 0, 0))
    mask_spec = pl.BlockSpec((span, rows_z, length), lambda i: (i, 0, 0))
    channels_spec = pl.BlockSpec((kinds, span, rows_z, length), lambda i: (0, i, 0, 0))
    phase_spec = pl.BlockSpec((2 * atoms, span * rows_z), lambda i: (0, i))
    chunks_spec = pl.BlockSpec((bands * places, planes, span, 128), lambda i: (0, 0, i, 0))
    chunk_shape = (bands * places, planes, rows_y, 128)
    smem_spec = pl.BlockSpec(memory_space=pltpu.SMEM)

    def exchange(chunks):
        return lax.all_to_all(
            chunks, ("band", "gy", "gz"), split_axis=0, concat_axis=0, tiled=True, axis_index_groups=groups
        )

    spread = pl.pallas_call(
        spread_kernel,
        grid=(steps,),
        in_specs=[orbitals_spec, mask_spec, smem_spec, whole(2 * length, 2 * length)],
        out_specs=chunks_spec,
        out_shape=jax.ShapeDtypeStruct(chunk_shape, bf16),
        scratch_shapes=[pltpu.VMEM((length * span, 128), f32)],
        compiler_params=params,
        cost_estimate=cost(4),
        name="spread",
    )(orbitals, cutoff_mask, occupations, inv_x)
    potential_part = lax.dynamic_slice_in_dim(potential, band * planes, planes, 0)

    spread, positions = lax.optimization_barrier((spread, positions))
    arrived = exchange(spread)

    cos_y, sin_y = axis_phase(positions[:, 1], frequencies(first_y, rows_y, length))
    cos_z, sin_z = axis_phase(positions[:, 2], frequencies(first_z, rows_z, length))
    cos_x, sin_x = axis_phase(positions[:, 0], frequencies(0, length, length))
    cos_yz = cos_y[:, :, None] * cos_z[:, None, :] - sin_y[:, :, None] * sin_z[:, None, :]
    sin_yz = sin_y[:, :, None] * cos_z[:, None, :] + cos_y[:, :, None] * sin_z[:, None, :]
    phase = jnp.concatenate([cos_yz, sin_yz], axis=0).astype(bf16).reshape(2 * atoms, rows_y * rows_z)
    wave = jnp.concatenate([cos_x, sin_x], axis=0)
    chosen = (proj_atom[None, :] == jnp.arange(atoms, dtype=jnp.int32)[:, None])[:, None, :] & (
        proj_chan[None, :] == jnp.arange(kinds, dtype=jnp.int32)[:, None]
    )[None, :, :]
    strength = jnp.sum(jnp.where(chosen, coupling[None, None, :], 0.0), axis=2)
    strength = jnp.pad(jnp.repeat(strength, 4, axis=1), ((0, 0), (0, 128 - 4 * kinds)))

    overlap = pl.pallas_call(
        overlap_kernel,
        grid=(steps,),
        in_specs=[orbitals_spec, mask_spec, channels_spec, phase_spec, whole(2 * atoms, length)],
        out_specs=whole(atoms, 128),
        out_shape=jax.ShapeDtypeStruct((atoms, 128), f32),
        scratch_shapes=[pltpu.VMEM((2 * atoms, kinds * 4 * length), f32)],
        compiler_params=params,
        cost_estimate=cost(3),
        name="overlap",
    )(orbitals, cutoff_mask, channels, phase, wave)
    overlap = sum_over(overlap, "gz", (1, 2, 3))
    arrived, overlap = lax.optimization_barrier((arrived, overlap))
    overlap = sum_over(overlap, "gy", (1, 2, 3))

    rows = planes * rows_y
    band_spec = pl.BlockSpec((places, rows, 128), lambda i: (i, 0, 0))
    density, folded = pl.pallas_call(
        field_kernel,
        grid=(bands,),
        in_specs=[
            band_spec,
            whole(planes, length, length),
            whole(4 * length, 4 * length),
            whole(2 * length, 2 * length),
            whole(4 * length, 4 * length),
            whole(2 * length, 2 * length),
        ],
        out_specs=[whole(planes * length, length), band_spec],
        out_shape=[
            jax.ShapeDtypeStruct((planes * length, length), bf16),
            jax.ShapeDtypeStruct((bands * places, rows, 128), bf16),
        ],
        scratch_shapes=[pltpu.VMEM((planes * length, length), f32)],
        compiler_params=params,
        cost_estimate=cost(6),
        name="field",
    )(arrived.reshape(bands * places, rows, 128), potential_part, inv_z, inv_y, fwd_z, fwd_y)
    returned = exchange(folded.reshape(chunk_shape))

    base = pl.pallas_call(
        base_kernel,
        grid=(steps,),
        in_specs=[
            smem_spec,
            whole(atoms, 128),
            orbitals_spec,
            mask_spec,
            channels_spec,
            phase_spec,
            whole(2 * atoms, length),
            whole(atoms, 128),
        ],
        out_specs=orbitals_spec,
        out_shape=jax.ShapeDtypeStruct(orbitals.shape, f32),
        scratch_shapes=[pltpu.VMEM((2 * atoms, kinds * 4 * length), bf16)],
        compiler_params=params,
        cost_estimate=cost(4),
        name="base",
    )(
        jnp.stack([first_y, first_z]).astype(jnp.int32),
        overlap,
        orbitals,
        cutoff_mask,
        channels,
        phase,
        wave,
        strength,
    )
    half = planes // 2 * length
    upper = lax.axis_index("band") // bands % 2
    mine = lax.dynamic_slice_in_dim(density, upper * half, half, 0)
    theirs = lax.dynamic_slice_in_dim(density, (1 - upper) * half, half, 0)
    near = lax.ppermute(theirs, "band", partners("band", bands))
    mine = (mine.astype(f32) + near.astype(f32)).astype(bf16)
    far = [lax.ppermute(mine, "band", partners("band", d * bands)) for d in (2, 4, 6) if d < outer]
    far, base = lax.optimization_barrier((far, base))
    if far:
        far = [part.astype(f32) for part in far]
        mine = ((mine.astype(f32) + far[0]) + (far[1] + far[2])).astype(bf16)
    copies = [lax.ppermute(mine, "band", partners("band", d)) for d in (1, 2, 3)]
    applied = pl.pallas_call(
        apply_kernel,
        grid=(steps,),
        in_specs=[chunks_spec, orbitals_spec, mask_spec, smem_spec, whole(length, 4 * length)],
        out_specs=orbitals_spec,
        out_shape=jax.ShapeDtypeStruct(orbitals.shape, bf16),
        scratch_shapes=[pltpu.VMEM((length * span, 128), f32)],
        compiler_params=params,
        cost_estimate=cost(4),
        name="apply",
    )(returned, base, cutoff_mask, occupations, fwd_x)
    copies, applied = lax.optimization_barrier((copies, applied))
    odd, high = band != 0, upper != 0
    pieces = [mine] + copies
    pieces = [jnp.where(odd, pieces[j ^ 1], pieces[j]) for j in range(4)]
    pieces = [jnp.where(high, pieces[j ^ 2], pieces[j]) for j in range(4)]
    density = jnp.concatenate([pieces[0], pieces[2], pieces[1], pieces[3]], axis=0)
    return (applied, density.astype(f32).reshape(potential.shape))


def solution(mesh):
    placed = (
        P("band", "gy", "gz", None),
        P(("gy", "gz"), None, None),
        P("gy", "gz", None),
        P(None, "gy", "gz", None),
        P(),
        P(),
        P(),
        P(),
        P("band"),
    )
    return jax.shard_map(
        shards,
        mesh=mesh,
        in_specs=placed,
        out_specs=(P("band", "gy", "gz", None), P(("gy", "gz"), None, None)),
        check_vma=False,
    )
```

```python
import functools
import math

import jax
import jax.numpy as jnp
import ml_dtypes
import numpy as np
from jax import lax
from jax.experimental import pallas as pl
from jax.experimental.pallas import tpu as pltpu
from jax.sharding import PartitionSpec as P

kinetic_scale = 1.0 / 1024.0
vmem_bytes = 63 * 1024 * 1024
bf16 = jnp.bfloat16
f32 = jnp.float32


def dft_table(length, sign_value):
    grid_index = np.arange(length)
    product = grid_index[:, None] * grid_index[None, :] % length
    phase_angle = np.float32(2.0 * math.pi / length) * product.astype(np.float32)
    cosine_part = np.cos(phase_angle) / np.float32(math.sqrt(length))
    sine_part = sign_value * np.sin(phase_angle) / np.float32(math.sqrt(length))
    upper_rows = np.stack([cosine_part, -sine_part], axis=1)
    lower_rows = np.stack([sine_part, cosine_part], axis=1)
    return np.stack([upper_rows, lower_rows], axis=0).astype(np.float32)


def rounded(table, rows):
    return jnp.asarray(np.ascontiguousarray(table).reshape(rows, -1).astype(ml_dtypes.bfloat16))


def frequencies(first_index, span, length):
    grid_index = first_index + jnp.arange(span, dtype=jnp.int32)
    return jnp.where(grid_index >= length // 2, grid_index - length, grid_index).astype(f32)


def axis_phase(coordinate, freq):
    phase_angle = 2.0 * math.pi * (coordinate[:, None] * freq[None, :])
    return (jnp.cos(phase_angle), jnp.sin(phase_angle))


def dot(left, right):
    return jnp.dot(left, right, preferred_element_type=f32)


def dot_nt(left, right):
    return lax.dot_general(left, right, (((1,), (1,)), ((), ())), preferred_element_type=f32)


def dot_tn(left, right):
    return lax.dot_general(left, right, (((0,), (0,)), ((), ())), preferred_element_type=f32)


def root_weights(weight_ref, shape, axis, span):
    index = lax.broadcasted_iota(jnp.int32, shape, axis)
    return jnp.sqrt(jnp.where(index // span % 2 == 0, weight_ref[0], weight_ref[1]))


def spread_kernel(orbitals_ref, mask_ref, weight_ref, table_ref, out_ref, work_ref):
    rows_y, rows_z, length = mask_ref.shape
    mask = jnp.where(mask_ref[...] != 0, 1.0, 0.0).astype(bf16)
    mask = jnp.concatenate([mask, mask], axis=2)
    lane = lax.broadcasted_iota(jnp.int32, (length, 128), 1)
    roots = root_weights(weight_ref, (1, 128), 1, rows_z)
    for pair in range(0, rows_y, 2):
        rows = []
        for y in (pair, pair + 1):
            both = jnp.concatenate([orbitals_ref[0, y] * mask[y], orbitals_ref[1, y] * mask[y]], axis=0)
            rows += [both, both]
        spread = dot_nt(table_ref[...], jnp.concatenate(rows, axis=0))
        for half in range(2):
            cols = slice(half * 128, half * 128 + 128)
            tile = jnp.where(lane < 64, spread[:length, cols], spread[length:, cols])
            work_ref[pl.ds(pair + half, length, stride=rows_y), :] = tile * roots
    out_ref[...] = work_ref[...].reshape(out_ref.shape).astype(bf16)


def overlap_kernel(orbitals_ref, mask_ref, channels_ref, phase_ref, wave_ref, out_ref, sums_ref):
    step = pl.program_id(0)
    rows = mask_ref.shape[0] * mask_ref.shape[1]
    length = mask_ref.shape[2]
    atoms = wave_ref.shape[0] // 2
    kinds = channels_ref.shape[0]
    mask = jnp.where(mask_ref[...] != 0, 1.0, 0.0).astype(bf16)
    orbs = [orbitals_ref[n].reshape(rows, 2 * length) for n in range(2)]
    columns = []
    for c in range(kinds):
        radial = (channels_ref[c] * mask).reshape(rows, length)
        radial = jnp.concatenate([radial, radial], axis=1)
        columns += [radial * orbs[0], radial * orbs[1]]
    part = dot(phase_ref[...], jnp.concatenate(columns, axis=1))

    @pl.when(step == 0)
    def first():
        sums_ref[...] = part

    @pl.when(step > 0)
    def later():
        sums_ref[...] += part

    @pl.when(step == pl.num_programs(0) - 1)
    def last():
        cos_x, sin_x = wave_ref[:atoms], wave_ref[atoms:]
        lane = lax.broadcasted_iota(jnp.int32, (atoms, 128), 1)
        total = jnp.zeros((atoms, 128), f32)
        for pair in range(kinds * 2):
            base = pair * 2 * length
            real_cols = slice(base, base + length)
            imag_cols = slice(base + length, base + 2 * length)
            real = sums_ref[:atoms, real_cols] - sums_ref[atoms:, imag_cols]
            imag = sums_ref[atoms:, real_cols] + sums_ref[:atoms, imag_cols]
            real_over = jnp.sum(real * cos_x - imag * sin_x, axis=1, keepdims=True)
            imag_over = jnp.sum(real * sin_x + imag * cos_x, axis=1, keepdims=True)
            total = jnp.where(lane == 2 * pair, real_over, total)
            total = jnp.where(lane == 2 * pair + 1, imag_over, total)
        out_ref[...] = total


def field_kernel(
    arrived_ref,
    potential_ref,
    inv_z_ref,
    inv_y_ref,
    fwd_z_ref,
    fwd_y_ref,
    density_ref,
    out_ref,
    sums_ref,
):
    step = pl.program_id(0)
    planes, length = potential_ref.shape[:2]
    parts = arrived_ref.shape[0] // 4
    rows = arrived_ref.shape[1] // planes
    columns = jnp.concatenate(
        [jnp.concatenate([arrived_ref[sy * 4 + sz] for sz in range(4)], axis=1) for sy in range(parts)],
        axis=0,
    )
    halfway = dot(columns, inv_z_ref[...]).astype(bf16)
    stacked = []
    for x in range(planes):
        first = [(sy * planes + x) * rows for sy in range(parts)]
        plane = jnp.concatenate([halfway[start : start + rows] for start in first], axis=0)
        real = jnp.concatenate([plane[:, 0:128], plane[:, 256:384]], axis=1)
        imag = jnp.concatenate([plane[:, 128:256], plane[:, 384:512]], axis=1)
        stacked.append(jnp.concatenate([real, imag], axis=0))
    fields = [dot(inv_y_ref[...], block) for block in stacked]
    scaled = []
    for x, field in enumerate(fields):
        real, imag = field[:length], field[length:]
        square = real * real + imag * imag
        density = square[:, :length] + square[:, length:]
        here = slice(x * length, (x + 1) * length)
        sums_ref[here, :] = jnp.where(step == 0, density, sums_ref[here, :] + density)
        potential = jnp.concatenate([potential_ref[x], potential_ref[x]], axis=1)
        potential = jnp.concatenate([potential, potential], axis=0)
        scaled.append((potential * field).astype(bf16))
    folded = [dot(fwd_y_ref[...], block).astype(bf16) for block in scaled]
    back = []
    for block in folded:
        real, imag = block[:length], block[length:]
        back.append(
            jnp.concatenate([real[:, :length], imag[:, :length], real[:, length:], imag[:, length:]], axis=1)
        )
    back = dot(jnp.concatenate(back, axis=0), fwd_z_ref[...]).astype(bf16)
    for x in range(planes):
        for sy in range(parts):
            start = x * length + sy * rows
            for sz in range(4):
                out_ref[sy * 4 + sz, x * rows : (x + 1) * rows, :] = back[
                    start : start + rows, sz * 128 : sz * 128 + 128
                ]

    @pl.when(step == pl.num_programs(0) - 1)
    def last():
        density_ref[...] = sums_ref[...].astype(bf16)


def base_kernel(
    first_ref,
    overlap_ref,
    orbitals_ref,
    mask_ref,
    channels_ref,
    phase_ref,
    wave_ref,
    strength_ref,
    out_ref,
    factor_ref,
):
    step = pl.program_id(0)
    rows_y, rows_z, length = mask_ref.shape
    atoms = wave_ref.shape[0] // 2
    kinds = channels_ref.shape[0]

    @pl.when(step == 0)
    def factors():
        cos_x, sin_x = wave_ref[:atoms], wave_ref[atoms:]
        coef = overlap_ref[...] * strength_ref[...]
        for pair in range(kinds * 2):
            coef_real = coef[:, 2 * pair : 2 * pair + 1]
            coef_imag = coef[:, 2 * pair + 1 : 2 * pair + 2]
            real = cos_x * coef_real + sin_x * coef_imag
            imag = cos_x * coef_imag - sin_x * coef_real
            base = pair * 2 * length
            factor_ref[:, base : base + length] = jnp.concatenate([real, imag], axis=0).astype(bf16)
            factor_ref[:, base + length : base + 2 * length] = jnp.concatenate(
                [imag, -real], axis=0
            ).astype(bf16)

    def squared(start, axis):
        index = start + lax.broadcasted_iota(jnp.int32, mask_ref.shape, axis)
        wave = jnp.where(index >= length // 2, index - length, index)
        return wave * wave

    energy = squared(first_ref[0] + step * rows_y, 0) + squared(first_ref[1], 1) + squared(0, 2)
    energy = kinetic_scale * 0.5 * energy.astype(f32)
    for y in range(rows_y):
        extra = dot_tn(phase_ref[:, y * rows_z : (y + 1) * rows_z], factor_ref[...])
        radials = [channels_ref[c, y].astype(f32) for c in range(kinds)]
        for n in range(2):
            for part in range(2):
                cols = slice(part * length, part * length + length)
                total = energy[y] * orbitals_ref[n, y, :, cols].astype(f32)
                for c in range(kinds):
                    base = ((c * 2 + n) * 2 + part) * length
                    total = total + radials[c] * extra[:, base : base + length]
                out_ref[n, y, :, cols] = total


def apply_kernel(returned_ref, base_ref, mask_ref, weight_ref, table_ref, out_ref, work_ref):
    rows_y, rows_z, length = mask_ref.shape
    scale = 1.0 / root_weights(weight_ref, (2 * rows_z, 1), 0, rows_z)
    work_ref[...] = returned_ref[...].astype(f32).reshape(work_ref.shape)
    inside = mask_ref[...] != 0
    for pair in range(0, rows_y, 2):
        planes = jnp.concatenate(
            [work_ref[pl.ds(y, length, stride=rows_y), :].astype(bf16) for y in (pair, pair + 1)], axis=1
        )
        local = dot_tn(planes, table_ref[...])
        for half in range(2):
            y = pair + half
            both = local[half * 128 : half * 128 + 64, : 2 * length]
            both = scale * (both + local[half * 128 + 64 : half * 128 + 128, 2 * length :])
            keep = jnp.concatenate([inside[y], inside[y]], axis=1)
            for n in range(2):
                total = both[n * rows_z : (n + 1) * rows_z] + base_ref[n, y]
                out_ref[n, y] = jnp.where(keep, total, 0.0).astype(bf16)


def partners(axis, distance):
    return [(i, i ^ distance) for i in range(lax.axis_size(axis))]


def sum_over(part, axis, distances):
    got = [lax.ppermute(part, axis, partners(axis, d)).astype(f32) for d in distances]
    return (part.astype(f32) + got[0]) + (got[1] + got[2])


def shards(
    orbitals,
    potential,
    cutoff_mask,
    channels,
    positions,
    proj_atom,
    proj_chan,
    coupling,
    occupations,
):
    rows_y, rows_z, length = cutoff_mask.shape
    parts_y = lax.axis_size("gy")
    parts_z = lax.axis_size("gz")
    parts_band = lax.axis_size("band")
    places = parts_y * parts_z
    bands = 2
    outer = parts_band // bands
    thin = length // places
    planes = thin // bands
    atoms = positions.shape[0]
    kinds = channels.shape[0]
    groups = [
        [(first * bands + b) * places + place for b in range(bands) for place in range(places)]
        for first in range(outer)
    ]
    inverse = dft_table(length, 1.0)
    forward = dft_table(length, -1.0)
    pick = np.eye(2, dtype=np.float32)
    split_inverse = inverse.reshape(2, length, 2, parts_z, rows_z)
    split_forward = forward.reshape(2, parts_z, rows_z, 2, length)
    order = np.arange(length).reshape(places, bands, planes).transpose(1, 0, 2).reshape(-1)
    inv_x = rounded(inverse[:, order], 2 * length)
    inv_y = rounded(inverse, 2 * length)
    inv_z = rounded(np.einsum("fzcsl,nm->scnlmfz", split_inverse, pick), 4 * length)
    fwd_z = rounded(np.einsum("cslfz,nm->nfzscml", split_forward, pick), 4 * length)
    fwd_y = rounded(forward, 2 * length)
    fwd_x = rounded(np.einsum("rkcx->xcrk", forward[..., order]), length)
    first_y = lax.axis_index("gy") * rows_y
    first_z = lax.axis_index("gz") * rows_z
    band = lax.axis_index("band") % bands

    params = pltpu.CompilerParams(vmem_limit_bytes=vmem_bytes)

    def cost(microseconds):
        return pl.CostEstimate(
            flops=int(microseconds * 1.0e9), bytes_accessed=int(microseconds * 1.0e6), transcendentals=0
        )

    steps = 2
    span = rows_y // steps
    whole = lambda *shape: pl.BlockSpec(shape, lambda i: (0,) * len(shape))
    orbitals_spec = pl.BlockSpec((2, span, rows_z, 2 * length), lambda i: (0, i, 0, 0))
    mask_spec = pl.BlockSpec((span, rows_z, length), lambda i: (i, 0, 0))
    channels_spec = pl.BlockSpec((kinds, span, rows_z, length), lambda i: (0, i, 0, 0))
    phase_spec = pl.BlockSpec((2 * atoms, span * rows_z), lambda i: (0, i))
    chunks_spec = pl.BlockSpec((bands * places, planes, span, 128), lambda i: (0, 0, i, 0))
    chunk_shape = (bands * places, planes, rows_y, 128)
    smem_spec = pl.BlockSpec(memory_space=pltpu.SMEM)

    def exchange(chunks):
        return lax.all_to_all(
            chunks, ("band", "gy", "gz"), split_axis=0, concat_axis=0, tiled=True, axis_index_groups=groups
        )

    spread = pl.pallas_call(
        spread_kernel,
        grid=(steps,),
        in_specs=[orbitals_spec, mask_spec, smem_spec, whole(2 * length, 2 * length)],
        out_specs=chunks_spec,
        out_shape=jax.ShapeDtypeStruct(chunk_shape, bf16),
        scratch_shapes=[pltpu.VMEM((length * span, 128), f32)],
        compiler_params=params,
        cost_estimate=cost(4),
        name="spread",
    )(orbitals, cutoff_mask, occupations, inv_x)
    potential_part = lax.dynamic_slice_in_dim(potential, band * planes, planes, 0)

    spread, positions = lax.optimization_barrier((spread, positions))
    arrived = exchange(spread)

    cos_y, sin_y = axis_phase(positions[:, 1], frequencies(first_y, rows_y, length))
    cos_z, sin_z = axis_phase(positions[:, 2], frequencies(first_z, rows_z, length))
    cos_x, sin_x = axis_phase(positions[:, 0], frequencies(0, length, length))
    cos_yz = cos_y[:, :, None] * cos_z[:, None, :] - sin_y[:, :, None] * sin_z[:, None, :]
    sin_yz = sin_y[:, :, None] * cos_z[:, None, :] + cos_y[:, :, None] * sin_z[:, None, :]
    phase = jnp.concatenate([cos_yz, sin_yz], axis=0).astype(bf16).reshape(2 * atoms, rows_y * rows_z)
    wave = jnp.concatenate([cos_x, sin_x], axis=0)
    chosen = (proj_atom[None, :] == jnp.arange(atoms, dtype=jnp.int32)[:, None])[:, None, :] & (
        proj_chan[None, :] == jnp.arange(kinds, dtype=jnp.int32)[:, None]
    )[None, :, :]
    strength = jnp.sum(jnp.where(chosen, coupling[None, None, :], 0.0), axis=2)
    strength = jnp.pad(jnp.repeat(strength, 4, axis=1), ((0, 0), (0, 128 - 4 * kinds)))

    overlap = pl.pallas_call(
        overlap_kernel,
        grid=(steps,),
        in_specs=[orbitals_spec, mask_spec, channels_spec, phase_spec, whole(2 * atoms, length)],
        out_specs=whole(atoms, 128),
        out_shape=jax.ShapeDtypeStruct((atoms, 128), f32),
        scratch_shapes=[pltpu.VMEM((2 * atoms, kinds * 4 * length), f32)],
        compiler_params=params,
        cost_estimate=cost(0.1),
        name="overlap",
    )(orbitals, cutoff_mask, channels, phase, wave)
    overlap = sum_over(overlap, "gz", (1, 2, 3))
    arrived, overlap = lax.optimization_barrier((arrived, overlap))
    overlap = sum_over(overlap, "gy", (1, 2, 3))

    rows = planes * rows_y
    band_spec = pl.BlockSpec((places, rows, 128), lambda i: (i, 0, 0))
    density, folded = pl.pallas_call(
        field_kernel,
        grid=(bands,),
        in_specs=[
            band_spec,
            whole(planes, length, length),
            whole(4 * length, 4 * length),
            whole(2 * length, 2 * length),
            whole(4 * length, 4 * length),
            whole(2 * length, 2 * length),
        ],
        out_specs=[whole(planes * length, length), band_spec],
        out_shape=[
            jax.ShapeDtypeStruct((planes * length, length), bf16),
            jax.ShapeDtypeStruct((bands * places, rows, 128), bf16),
        ],
        scratch_shapes=[pltpu.VMEM((planes * length, length), f32)],
        compiler_params=params,
        cost_estimate=cost(6),
        name="field",
    )(arrived.reshape(bands * places, rows, 128), potential_part, inv_z, inv_y, fwd_z, fwd_y)
    returned = exchange(folded.reshape(chunk_shape))

    base = pl.pallas_call(
        base_kernel,
        grid=(steps,),
        in_specs=[
            smem_spec,
            whole(atoms, 128),
            orbitals_spec,
            mask_spec,
            channels_spec,
            phase_spec,
            whole(2 * atoms, length),
            whole(atoms, 128),
        ],
        out_specs=orbitals_spec,
        out_shape=jax.ShapeDtypeStruct(orbitals.shape, f32),
        scratch_shapes=[pltpu.VMEM((2 * atoms, kinds * 4 * length), bf16)],
        compiler_params=params,
        cost_estimate=cost(0.1),
        name="base",
    )(
        jnp.stack([first_y, first_z]).astype(jnp.int32),
        overlap,
        orbitals,
        cutoff_mask,
        channels,
        phase,
        wave,
        strength,
    )
    half = planes // 2 * length
    upper = lax.axis_index("band") // bands % 2
    mine = lax.dynamic_slice_in_dim(density, upper * half, half, 0)
    theirs = lax.dynamic_slice_in_dim(density, (1 - upper) * half, half, 0)
    near = lax.ppermute(theirs, "band", partners("band", bands))
    mine = (mine.astype(f32) + near.astype(f32)).astype(bf16)
    far = [lax.ppermute(mine, "band", partners("band", d * bands)) for d in (2, 4, 6) if d < outer]
    far, base = lax.optimization_barrier((far, base))
    if far:
        far = [part.astype(f32) for part in far]
        mine = ((mine.astype(f32) + far[0]) + (far[1] + far[2])).astype(bf16)
    copies = [lax.ppermute(mine, "band", partners("band", d)) for d in (1, 2, 3)]
    applied = pl.pallas_call(
        apply_kernel,
        grid=(steps,),
        in_specs=[chunks_spec, orbitals_spec, mask_spec, smem_spec, whole(length, 4 * length)],
        out_specs=orbitals_spec,
        out_shape=jax.ShapeDtypeStruct(orbitals.shape, bf16),
        scratch_shapes=[pltpu.VMEM((length * span, 128), f32)],
        compiler_params=params,
        cost_estimate=cost(4),
        name="apply",
    )(returned, base, cutoff_mask, occupations, fwd_x)
    copies, applied = lax.optimization_barrier((copies, applied))
    odd, high = band != 0, upper != 0
    pieces = [mine] + copies
    pieces = [jnp.where(odd, pieces[j ^ 1], pieces[j]) for j in range(4)]
    pieces = [jnp.where(high, pieces[j ^ 2], pieces[j]) for j in range(4)]
    density = jnp.concatenate([pieces[0], pieces[2], pieces[1], pieces[3]], axis=0)
    return (applied, density.astype(f32).reshape(potential.shape))


def solution(mesh):
    placed = (
        P("band", "gy", "gz", None),
        P(("gy", "gz"), None, None),
        P("gy", "gz", None),
        P(None, "gy", "gz", None),
        P(),
        P(),
        P(),
        P(),
        P("band"),
    )
    return jax.shard_map(
        shards,
        mesh=mesh,
        in_specs=placed,
        out_specs=(P("band", "gy", "gz", None), P(("gy", "gz"), None, None)),
        check_vma=False,
    )
```

```python
import functools
import math

import jax
import jax.numpy as jnp
import ml_dtypes
import numpy as np
from jax import lax
from jax.experimental import pallas as pl
from jax.experimental.pallas import tpu as pltpu
from jax.sharding import PartitionSpec as P

kinetic_scale = 1.0 / 1024.0
vmem_bytes = 63 * 1024 * 1024
bf16 = jnp.bfloat16
f32 = jnp.float32


def dft_table(length, sign_value):
    grid_index = np.arange(length)
    product = grid_index[:, None] * grid_index[None, :] % length
    phase_angle = np.float32(2.0 * math.pi / length) * product.astype(np.float32)
    cosine_part = np.cos(phase_angle) / np.float32(math.sqrt(length))
    sine_part = sign_value * np.sin(phase_angle) / np.float32(math.sqrt(length))
    upper_rows = np.stack([cosine_part, -sine_part], axis=1)
    lower_rows = np.stack([sine_part, cosine_part], axis=1)
    return np.stack([upper_rows, lower_rows], axis=0).astype(np.float32)


def rounded(table, rows):
    return jnp.asarray(np.ascontiguousarray(table).reshape(rows, -1).astype(ml_dtypes.bfloat16))


def frequencies(first_index, span, length):
    grid_index = first_index + jnp.arange(span, dtype=jnp.int32)
    return jnp.where(grid_index >= length // 2, grid_index - length, grid_index).astype(f32)


def axis_phase(coordinate, freq):
    phase_angle = 2.0 * math.pi * (coordinate[:, None] * freq[None, :])
    return (jnp.cos(phase_angle), jnp.sin(phase_angle))


def dot(left, right):
    return jnp.dot(left, right, preferred_element_type=f32)


def dot_nt(left, right):
    return lax.dot_general(left, right, (((1,), (1,)), ((), ())), preferred_element_type=f32)


def dot_tn(left, right):
    return lax.dot_general(left, right, (((0,), (0,)), ((), ())), preferred_element_type=f32)


def root_weights(weight_ref, shape, axis, span):
    index = lax.broadcasted_iota(jnp.int32, shape, axis)
    return jnp.sqrt(jnp.where(index // span % 2 == 0, weight_ref[0], weight_ref[1]))


def spread_kernel(orbitals_ref, mask_ref, weight_ref, table_ref, out_ref, work_ref):
    rows_y, rows_z, length = mask_ref.shape
    mask = jnp.where(mask_ref[...] != 0, 1.0, 0.0).astype(bf16)
    mask = jnp.concatenate([mask, mask], axis=2)
    lane = lax.broadcasted_iota(jnp.int32, (length, 128), 1)
    roots = root_weights(weight_ref, (1, 128), 1, rows_z)
    spreads = []
    for pair in range(0, rows_y, 2):
        rows = []
        for y in (pair, pair + 1):
            both = jnp.concatenate([orbitals_ref[0, y] * mask[y], orbitals_ref[1, y] * mask[y]], axis=0)
            rows += [both, both]
        spreads.append(dot_nt(table_ref[...], jnp.concatenate(rows, axis=0)))
    for y in range(rows_y):
        spread = spreads[y // 2][:, y % 2 * 128 : y % 2 * 128 + 128]
        tile = jnp.where(lane < 64, spread[:length], spread[length:])
        work_ref[pl.ds(y, length, stride=rows_y), :] = tile * roots
    out_ref[...] = work_ref[...].reshape(out_ref.shape).astype(bf16)


def overlap_kernel(orbitals_ref, mask_ref, channels_ref, phase_ref, wave_ref, out_ref, sums_ref):
    step = pl.program_id(0)
    rows = mask_ref.shape[0] * mask_ref.shape[1]
    length = mask_ref.shape[2]
    atoms = wave_ref.shape[0] // 2
    kinds = channels_ref.shape[0]
    mask = jnp.where(mask_ref[...] != 0, 1.0, 0.0).astype(bf16)
    orbs = [orbitals_ref[n].reshape(rows, 2 * length) for n in range(2)]
    columns = []
    for c in range(kinds):
        radial = (channels_ref[c] * mask).reshape(rows, length)
        radial = jnp.concatenate([radial, radial], axis=1)
        columns += [radial * orbs[0], radial * orbs[1]]
    part = dot(phase_ref[...], jnp.concatenate(columns, axis=1))

    @pl.when(step == 0)
    def first():
        sums_ref[...] = part

    @pl.when(step > 0)
    def later():
        sums_ref[...] += part

    @pl.when(step == pl.num_programs(0) - 1)
    def last():
        cos_x, sin_x = wave_ref[:atoms], wave_ref[atoms:]
        lane = lax.broadcasted_iota(jnp.int32, (atoms, 128), 1)
        total = jnp.zeros((atoms, 128), f32)
        for pair in range(kinds * 2):
            base = pair * 2 * length
            real_cols = slice(base, base + length)
            imag_cols = slice(base + length, base + 2 * length)
            real = sums_ref[:atoms, real_cols] - sums_ref[atoms:, imag_cols]
            imag = sums_ref[atoms:, real_cols] + sums_ref[:atoms, imag_cols]
            real_over = jnp.sum(real * cos_x - imag * sin_x, axis=1, keepdims=True)
            imag_over = jnp.sum(real * sin_x + imag * cos_x, axis=1, keepdims=True)
            total = jnp.where(lane == 2 * pair, real_over, total)
            total = jnp.where(lane == 2 * pair + 1, imag_over, total)
        high = total.astype(bf16).astype(f32)
        out_ref[...] = jnp.concatenate([high, total - high], axis=0).astype(bf16)


def field_kernel(
    arrived_ref,
    potential_ref,
    overlap_ref,
    inv_z_ref,
    inv_y_ref,
    fwd_z_ref,
    fwd_y_ref,
    mine_ref,
    theirs_ref,
    out_ref,
    sums_ref,
):
    step = pl.program_id(0)
    planes, length = potential_ref.shape[:2]
    parts = arrived_ref.shape[0] // 4
    rows = arrived_ref.shape[1] // planes
    columns = jnp.concatenate(
        [jnp.concatenate([arrived_ref[sy * 4 + sz] for sz in range(4)], axis=1) for sy in range(parts)],
        axis=0,
    )
    halfway = dot(columns, inv_z_ref[...]).astype(bf16)
    stacked = []
    for x in range(planes):
        first = [(sy * planes + x) * rows for sy in range(parts)]
        plane = jnp.concatenate([halfway[start : start + rows] for start in first], axis=0)
        real = jnp.concatenate([plane[:, 0:128], plane[:, 256:384]], axis=1)
        imag = jnp.concatenate([plane[:, 128:256], plane[:, 384:512]], axis=1)
        stacked.append(jnp.concatenate([real, imag], axis=0))
    fields = [dot(inv_y_ref[...], block) for block in stacked]
    scaled = []
    for x, field in enumerate(fields):
        real, imag = field[:length], field[length:]
        square = real * real + imag * imag
        density = square[:, :length] + square[:, length:]
        here = slice(x * length, (x + 1) * length)
        sums_ref[here, :] = jnp.where(step == 0, density, sums_ref[here, :] + density)
        potential = jnp.concatenate([potential_ref[x], potential_ref[x]], axis=1)
        potential = jnp.concatenate([potential, potential], axis=0)
        scaled.append((potential * field).astype(bf16))
    folded = [dot(fwd_y_ref[...], block).astype(bf16) for block in scaled]
    back = []
    for block in folded:
        real, imag = block[:length], block[length:]
        back.append(
            jnp.concatenate([real[:, :length], imag[:, :length], real[:, length:], imag[:, length:]], axis=1)
        )
    back = dot(jnp.concatenate(back, axis=0), fwd_z_ref[...]).astype(bf16)
    span = rows // 2
    for x in range(planes):
        for sy in range(parts):
            for half in range(2):
                start = x * length + sy * rows + half * span
                row = (half * planes + x) * span
                for sz in range(4):
                    out_ref[sy * 4 + sz, row : row + span, :] = back[
                        start : start + span, sz * 128 : sz * 128 + 128
                    ]
    for place in range(out_ref.shape[0]):
        out_ref[place, planes * rows :, :] = overlap_ref[...]

    @pl.when(step == pl.num_programs(0) - 1)
    def last():
        half = planes // 2 * length
        low, high = sums_ref[:half, :].astype(bf16), sums_ref[half:, :].astype(bf16)
        upper = lax.axis_index("band") // 2 % 2
        mine_ref[...] = jnp.where(upper == 0, low, high)
        theirs_ref[...] = jnp.where(upper == 0, high, low)


def apply_kernel(
    returned_ref,
    overlap_ref,
    orbitals_ref,
    mask_ref,
    channels_ref,
    phase_ref,
    wave_ref,
    strength_ref,
    weight_ref,
    table_ref,
    out_ref,
    factor_ref,
    work_ref,
):
    step = pl.program_id(0)
    rows_y, rows_z, length = mask_ref.shape
    atoms = wave_ref.shape[0] // 2
    kinds = channels_ref.shape[0]

    work_ref[...] = returned_ref[...].astype(f32).reshape(work_ref.shape)
    planes = [work_ref[pl.ds(y, length, stride=rows_y), :].astype(bf16) for y in range(rows_y)]
    local = [dot_tn(jnp.concatenate(planes[y : y + 2], axis=1), table_ref[...]) for y in range(0, rows_y, 2)]

    @pl.when(step == 0)
    def factors():
        cos_x, sin_x = wave_ref[:atoms], wave_ref[atoms:]
        sources = overlap_ref.shape[0] // 2
        even = jnp.sum(overlap_ref[:sources].astype(f32), axis=0)
        odd = jnp.sum(overlap_ref[sources:].astype(f32), axis=0)
        summed = jnp.where(lax.axis_index("band") % 2 == 0, even, odd)
        coef = (summed[:atoms] + summed[atoms:]) * strength_ref[...]
        for pair in range(kinds * 2):
            coef_real = coef[:, 2 * pair : 2 * pair + 1]
            coef_imag = coef[:, 2 * pair + 1 : 2 * pair + 2]
            real = cos_x * coef_real + sin_x * coef_imag
            imag = cos_x * coef_imag - sin_x * coef_real
            base = pair * 2 * length
            factor_ref[:, base : base + length] = jnp.concatenate([real, imag], axis=0).astype(bf16)
            factor_ref[:, base + length : base + 2 * length] = jnp.concatenate(
                [imag, -real], axis=0
            ).astype(bf16)

    extra = dot_tn(phase_ref[...], factor_ref[...])

    def squared(start, axis):
        index = start + lax.broadcasted_iota(jnp.int32, mask_ref.shape, axis)
        wave = jnp.where(index >= length // 2, index - length, index)
        return wave * wave

    first_y = lax.axis_index("gy") * (rows_y * pl.num_programs(0)) + step * rows_y
    energy = squared(first_y, 0) + squared(lax.axis_index("gz") * rows_z, 1) + squared(0, 2)
    energy = kinetic_scale * 0.5 * energy.astype(f32)
    inside = mask_ref[...] != 0
    scale = 1.0 / root_weights(weight_ref, (2 * rows_z, 1), 0, rows_z)
    for y in range(rows_y):
        block = local[y // 2][y % 2 * 128 : y % 2 * 128 + 128]
        both = scale * (block[:64, : 2 * length] + block[64:, 2 * length :])
        radials = [channels_ref[c, y].astype(f32) for c in range(kinds)]
        for n in range(2):
            for part in range(2):
                cols = slice(part * length, part * length + length)
                total = both[n * rows_z : (n + 1) * rows_z, cols]
                total = total + energy[y] * orbitals_ref[n, y, :, cols].astype(f32)
                for c in range(kinds):
                    base = ((c * 2 + n) * 2 + part) * length
                    total = total + radials[c] * extra[y * rows_z : (y + 1) * rows_z, base : base + length]
                out_ref[n, y, :, cols] = jnp.where(inside[y], total, 0.0).astype(bf16)


def partners(axis, distance):
    return [(i, i ^ distance) for i in range(lax.axis_size(axis))]


def shards(
    orbitals,
    potential,
    cutoff_mask,
    channels,
    positions,
    proj_atom,
    proj_chan,
    coupling,
    occupations,
):
    rows_y, rows_z, length = cutoff_mask.shape
    parts_y = lax.axis_size("gy")
    parts_z = lax.axis_size("gz")
    parts_band = lax.axis_size("band")
    places = parts_y * parts_z
    bands = 2
    outer = parts_band // bands
    thin = length // places
    planes = thin // bands
    atoms = positions.shape[0]
    kinds = channels.shape[0]
    groups = [
        [(first * bands + b) * places + place for b in range(bands) for place in range(places)]
        for first in range(outer)
    ]
    inverse = dft_table(length, 1.0)
    forward = dft_table(length, -1.0)
    pick = np.eye(2, dtype=np.float32)
    split_inverse = inverse.reshape(2, length, 2, parts_z, rows_z)
    split_forward = forward.reshape(2, parts_z, rows_z, 2, length)
    order = np.arange(length).reshape(places, bands, planes).transpose(1, 0, 2).reshape(-1)
    inv_x = rounded(inverse[:, order], 2 * length)
    inv_y = rounded(inverse, 2 * length)
    inv_z = rounded(np.einsum("fzcsl,nm->scnlmfz", split_inverse, pick), 4 * length)
    fwd_z = rounded(np.einsum("cslfz,nm->nfzscml", split_forward, pick), 4 * length)
    fwd_y = rounded(forward, 2 * length)
    fwd_x = rounded(np.einsum("rkcx->xcrk", forward[..., order]), length)
    first_y = lax.axis_index("gy") * rows_y
    first_z = lax.axis_index("gz") * rows_z
    band = lax.axis_index("band") % bands

    params = pltpu.CompilerParams(vmem_limit_bytes=vmem_bytes)

    def cost(microseconds):
        return pl.CostEstimate(
            flops=int(microseconds * 1.0e9), bytes_accessed=int(microseconds * 1.0e6), transcendentals=0
        )

    steps = 2
    span = rows_y // steps
    whole = lambda *shape: pl.BlockSpec(shape, lambda i: (0,) * len(shape))
    orbitals_spec = pl.BlockSpec((2, span, rows_z, 2 * length), lambda i: (0, i, 0, 0))
    mask_spec = pl.BlockSpec((span, rows_z, length), lambda i: (i, 0, 0))
    channels_spec = pl.BlockSpec((kinds, span, rows_z, length), lambda i: (0, i, 0, 0))
    phase_spec = pl.BlockSpec((2 * atoms, span * rows_z), lambda i: (0, i))
    chunks_spec = pl.BlockSpec((bands * places, planes, span, 128), lambda i: (0, 0, i, 0))
    chunk_shape = (bands * places, planes, rows_y, 128)
    smem_spec = pl.BlockSpec(memory_space=pltpu.SMEM)

    def exchange(chunks):
        return lax.all_to_all(
            chunks, ("band", "gy", "gz"), split_axis=0, concat_axis=0, tiled=True, axis_index_groups=groups
        )

    spread = pl.pallas_call(
        spread_kernel,
        grid=(steps,),
        in_specs=[orbitals_spec, mask_spec, smem_spec, whole(2 * length, 2 * length)],
        out_specs=chunks_spec,
        out_shape=jax.ShapeDtypeStruct(chunk_shape, bf16),
        scratch_shapes=[pltpu.VMEM((length * span, 128), f32)],
        compiler_params=params,
        cost_estimate=cost(4),
        name="spread",
    )(orbitals, cutoff_mask, occupations, inv_x)
    potential_part = lax.dynamic_slice_in_dim(potential, band * planes, planes, 0)

    spread, positions = lax.optimization_barrier((spread, positions))
    arrived = exchange(spread)

    cos_y, sin_y = axis_phase(positions[:, 1], frequencies(first_y, rows_y, length))
    cos_z, sin_z = axis_phase(positions[:, 2], frequencies(first_z, rows_z, length))
    cos_x, sin_x = axis_phase(positions[:, 0], frequencies(0, length, length))
    cos_yz = cos_y[:, :, None] * cos_z[:, None, :] - sin_y[:, :, None] * sin_z[:, None, :]
    sin_yz = sin_y[:, :, None] * cos_z[:, None, :] + cos_y[:, :, None] * sin_z[:, None, :]
    phase = jnp.concatenate([cos_yz, sin_yz], axis=0).astype(bf16).reshape(2 * atoms, rows_y * rows_z)
    wave = jnp.concatenate([cos_x, sin_x], axis=0)
    chosen = (proj_atom[None, :] == jnp.arange(atoms, dtype=jnp.int32)[:, None])[:, None, :] & (
        proj_chan[None, :] == jnp.arange(kinds, dtype=jnp.int32)[:, None]
    )[None, :, :]
    strength = jnp.sum(jnp.where(chosen, coupling[None, None, :], 0.0), axis=2)
    strength = jnp.pad(jnp.repeat(strength, 4, axis=1), ((0, 0), (0, 128 - 4 * kinds)))

    overlap = pl.pallas_call(
        overlap_kernel,
        grid=(steps,),
        in_specs=[orbitals_spec, mask_spec, channels_spec, phase_spec, whole(2 * atoms, length)],
        out_specs=whole(2 * atoms, 128),
        out_shape=jax.ShapeDtypeStruct((2 * atoms, 128), bf16),
        scratch_shapes=[pltpu.VMEM((2 * atoms, kinds * 4 * length), f32)],
        compiler_params=params,
        cost_estimate=cost(0.1),
        name="overlap",
    )(orbitals, cutoff_mask, channels, phase, wave)
    arrived, strength, overlap = lax.optimization_barrier((arrived, strength, overlap))

    rows = planes * rows_y
    half = planes // 2 * length
    mine, theirs, folded = pl.pallas_call(
        field_kernel,
        grid=(bands,),
        in_specs=[
            pl.BlockSpec((places, rows, 128), lambda i: (i, 0, 0)),
            whole(planes, length, length),
            whole(2 * atoms, 128),
            whole(4 * length, 4 * length),
            whole(2 * length, 2 * length),
            whole(4 * length, 4 * length),
            whole(2 * length, 2 * length),
        ],
        out_specs=[
            whole(half, length),
            whole(half, length),
            pl.BlockSpec((places, rows + 2 * atoms, 128), lambda i: (i, 0, 0)),
        ],
        out_shape=[
            jax.ShapeDtypeStruct((half, length), bf16),
            jax.ShapeDtypeStruct((half, length), bf16),
            jax.ShapeDtypeStruct((bands * places, rows + 2 * atoms, 128), bf16),
        ],
        scratch_shapes=[pltpu.VMEM((planes * length, length), f32)],
        compiler_params=params,
        cost_estimate=cost(6),
        name="field",
    )(arrived.reshape(bands * places, rows, 128), potential_part, overlap, inv_z, inv_y, fwd_z, fwd_y)
    returned = exchange(folded)

    upper = lax.axis_index("band") // bands % 2
    near = lax.ppermute(theirs, "band", partners("band", bands))
    mine = (mine.astype(f32) + near.astype(f32)).astype(bf16)
    for distance in (2, 6):
        if distance < outer:
            got = lax.ppermute(mine, "band", partners("band", distance * bands))
            mine = (mine.astype(f32) + got.astype(f32)).astype(bf16)
    near = lax.ppermute(mine, "band", partners("band", bands))
    mine = jnp.where(upper == 0, jnp.stack([mine, near]), jnp.stack([near, mine]))
    other = lax.ppermute(mine, "band", partners("band", 1))
    applied = pl.pallas_call(
        apply_kernel,
        grid=(steps,),
        in_specs=[
            pl.BlockSpec((bands * places, planes * span, 128), lambda i: (0, i, 0)),
            pl.BlockSpec((bands * places, 2 * atoms, 128), lambda i: (0, rows // (2 * atoms), 0)),
            orbitals_spec,
            mask_spec,
            channels_spec,
            phase_spec,
            whole(2 * atoms, length),
            whole(atoms, 128),
            smem_spec,
            whole(length, 4 * length),
        ],
        out_specs=orbitals_spec,
        out_shape=jax.ShapeDtypeStruct(orbitals.shape, bf16),
        scratch_shapes=[
            pltpu.VMEM((2 * atoms, kinds * 4 * length), bf16),
            pltpu.VMEM((length * span, 128), f32),
        ],
        compiler_params=params,
        cost_estimate=cost(4),
        name="apply",
    )(returned, returned, orbitals, cutoff_mask, channels, phase, wave, strength, occupations, fwd_x)
    other, applied = lax.optimization_barrier((other, applied))
    density = jnp.where(band == 0, jnp.stack([mine, other]), jnp.stack([other, mine]))
    return (applied, density.astype(f32).reshape(potential.shape))


def solution(mesh):
    placed = (
        P("band", "gy", "gz", None),
        P(("gy", "gz"), None, None),
        P("gy", "gz", None),
        P(None, "gy", "gz", None),
        P(),
        P(),
        P(),
        P(),
        P("band"),
    )
    return jax.shard_map(
        shards,
        mesh=mesh,
        in_specs=placed,
        out_specs=(P("band", "gy", "gz", None), P(("gy", "gz"), None, None)),
        check_vma=False,
    )
```

```python
import functools
import math

import jax
import jax.numpy as jnp
import ml_dtypes
import numpy as np
from jax import lax
from jax.experimental import pallas as pl
from jax.experimental.pallas import tpu as pltpu
from jax.sharding import PartitionSpec as P

kinetic_scale = 1.0 / 1024.0
vmem_bytes = 63 * 1024 * 1024
bf16 = jnp.bfloat16
f32 = jnp.float32


def dft_table(length, sign_value):
    grid_index = np.arange(length)
    product = grid_index[:, None] * grid_index[None, :] % length
    phase_angle = np.float32(2.0 * math.pi / length) * product.astype(np.float32)
    cosine_part = np.cos(phase_angle) / np.float32(math.sqrt(length))
    sine_part = sign_value * np.sin(phase_angle) / np.float32(math.sqrt(length))
    upper_rows = np.stack([cosine_part, -sine_part], axis=1)
    lower_rows = np.stack([sine_part, cosine_part], axis=1)
    return np.stack([upper_rows, lower_rows], axis=0).astype(np.float32)


def rounded(table, rows):
    return jnp.asarray(np.ascontiguousarray(table).reshape(rows, -1).astype(ml_dtypes.bfloat16))


def frequencies(first_index, span, length):
    grid_index = first_index + jnp.arange(span, dtype=jnp.int32)
    return jnp.where(grid_index >= length // 2, grid_index - length, grid_index).astype(f32)


def axis_phase(coordinate, freq):
    phase_angle = 2.0 * math.pi * (coordinate[:, None] * freq[None, :])
    return (jnp.cos(phase_angle), jnp.sin(phase_angle))


def dot(left, right):
    return jnp.dot(left, right, preferred_element_type=f32)


def dot_nt(left, right):
    return lax.dot_general(left, right, (((1,), (1,)), ((), ())), preferred_element_type=f32)


def dot_tn(left, right):
    return lax.dot_general(left, right, (((0,), (0,)), ((), ())), preferred_element_type=f32)


def root_weights(weight_ref, shape, axis, span):
    index = lax.broadcasted_iota(jnp.int32, shape, axis)
    return jnp.sqrt(jnp.where(index // span % 2 == 0, weight_ref[0], weight_ref[1]))


def spread_kernel(orbitals_ref, mask_ref, weight_ref, table_ref, out_ref, work_ref):
    rows_y, rows_z, length = mask_ref.shape
    mask = jnp.where(mask_ref[...] != 0, 1.0, 0.0).astype(bf16)
    mask = jnp.concatenate([mask, mask], axis=2)
    lane = lax.broadcasted_iota(jnp.int32, (length, 128), 1)
    roots = root_weights(weight_ref, (1, 128), 1, rows_z)
    spreads = []
    for pair in range(0, rows_y, 2):
        rows = []
        for y in (pair, pair + 1):
            both = jnp.concatenate([orbitals_ref[0, y] * mask[y], orbitals_ref[1, y] * mask[y]], axis=0)
            rows += [both, both]
        spreads.append(dot_nt(table_ref[...], jnp.concatenate(rows, axis=0)))
    for y in range(rows_y):
        spread = spreads[y // 2][:, y % 2 * 128 : y % 2 * 128 + 128]
        tile = jnp.where(lane < 64, spread[:length], spread[length:])
        work_ref[pl.ds(y, length, stride=rows_y), :] = tile * roots
    out_ref[...] = work_ref[...].reshape(out_ref.shape).astype(bf16)


def overlap_kernel(orbitals_ref, mask_ref, channels_ref, phase_ref, wave_ref, out_ref, sums_ref):
    step = pl.program_id(0)
    rows = mask_ref.shape[0] * mask_ref.shape[1]
    length = mask_ref.shape[2]
    atoms = wave_ref.shape[0] // 2
    kinds = channels_ref.shape[0]
    mask = jnp.where(mask_ref[...] != 0, 1.0, 0.0).astype(bf16)
    orbs = [orbitals_ref[n].reshape(rows, 2 * length) for n in range(2)]
    columns = []
    for c in range(kinds):
        radial = (channels_ref[c] * mask).reshape(rows, length)
        radial = jnp.concatenate([radial, radial], axis=1)
        columns += [radial * orbs[0], radial * orbs[1]]
    part = dot(phase_ref[...], jnp.concatenate(columns, axis=1))

    @pl.when(step == 0)
    def first():
        sums_ref[...] = part

    @pl.when(step > 0)
    def later():
        sums_ref[...] += part

    @pl.when(step == pl.num_programs(0) - 1)
    def last():
        cos_x, sin_x = wave_ref[:atoms], wave_ref[atoms:]
        lane = lax.broadcasted_iota(jnp.int32, (atoms, 128), 1)
        total = jnp.zeros((atoms, 128), f32)
        for pair in range(kinds * 2):
            base = pair * 2 * length
            real_cols = slice(base, base + length)
            imag_cols = slice(base + length, base + 2 * length)
            real = sums_ref[:atoms, real_cols] - sums_ref[atoms:, imag_cols]
            imag = sums_ref[atoms:, real_cols] + sums_ref[:atoms, imag_cols]
            real_over = jnp.sum(real * cos_x - imag * sin_x, axis=1, keepdims=True)
            imag_over = jnp.sum(real * sin_x + imag * cos_x, axis=1, keepdims=True)
            total = jnp.where(lane == 2 * pair, real_over, total)
            total = jnp.where(lane == 2 * pair + 1, imag_over, total)
        high = total.astype(bf16).astype(f32)
        out_ref[...] = jnp.concatenate([high, total - high], axis=0).astype(bf16)


def field_kernel(
    arrived_ref,
    potential_ref,
    overlap_ref,
    inv_z_ref,
    inv_y_ref,
    fwd_z_ref,
    fwd_y_ref,
    mine_ref,
    theirs_ref,
    out_ref,
    sums_ref,
):
    step = pl.program_id(0)
    planes, length = potential_ref.shape[:2]
    parts = arrived_ref.shape[0] // 4
    rows = arrived_ref.shape[1] // planes
    columns = jnp.concatenate(
        [jnp.concatenate([arrived_ref[sy * 4 + sz] for sz in range(4)], axis=1) for sy in range(parts)],
        axis=0,
    )
    halfway = dot(columns, inv_z_ref[...]).astype(bf16)
    stacked = []
    for x in range(planes):
        first = [(sy * planes + x) * rows for sy in range(parts)]
        plane = jnp.concatenate([halfway[start : start + rows] for start in first], axis=0)
        real = jnp.concatenate([plane[:, 0:128], plane[:, 256:384]], axis=1)
        imag = jnp.concatenate([plane[:, 128:256], plane[:, 384:512]], axis=1)
        stacked.append(jnp.concatenate([real, imag], axis=0))
    fields = [dot(inv_y_ref[...], block) for block in stacked]
    scaled = []
    for x, field in enumerate(fields):
        real, imag = field[:length], field[length:]
        square = real * real + imag * imag
        density = square[:, :length] + square[:, length:]
        here = slice(x * length, (x + 1) * length)
        sums_ref[here, :] = jnp.where(step == 0, density, sums_ref[here, :] + density)
        potential = jnp.concatenate([potential_ref[x], potential_ref[x]], axis=1)
        potential = jnp.concatenate([potential, potential], axis=0)
        scaled.append((potential * field).astype(bf16))
    folded = [dot(fwd_y_ref[...], block).astype(bf16) for block in scaled]
    back = []
    for block in folded:
        real, imag = block[:length], block[length:]
        back.append(
            jnp.concatenate([real[:, :length], imag[:, :length], real[:, length:], imag[:, length:]], axis=1)
        )
    back = dot(jnp.concatenate(back, axis=0), fwd_z_ref[...]).astype(bf16)
    span = rows // 2
    for x in range(planes):
        for sy in range(parts):
            for half in range(2):
                start = x * length + sy * rows + half * span
                row = (half * planes + x) * span
                for sz in range(4):
                    out_ref[sy * 4 + sz, row : row + span, :] = back[
                        start : start + span, sz * 128 : sz * 128 + 128
                    ]
    for place in range(out_ref.shape[0]):
        out_ref[place, planes * rows :, :] = overlap_ref[...]

    @pl.when(step == pl.num_programs(0) - 1)
    def last():
        half = planes // 2 * length
        low, high = sums_ref[:half, :].astype(bf16), sums_ref[half:, :].astype(bf16)
        upper = lax.axis_index("band") // 2 % 2
        mine_ref[...] = jnp.where(upper == 0, low, high)
        theirs_ref[...] = jnp.where(upper == 0, high, low)


def apply_kernel(
    returned_ref,
    overlap_ref,
    orbitals_ref,
    mask_ref,
    channels_ref,
    phase_ref,
    wave_ref,
    strength_ref,
    weight_ref,
    table_ref,
    out_ref,
    factor_ref,
    work_ref,
):
    step = pl.program_id(0)
    rows_y, rows_z, length = mask_ref.shape
    atoms = wave_ref.shape[0] // 2
    kinds = channels_ref.shape[0]

    work_ref[...] = returned_ref[...].astype(f32).reshape(work_ref.shape)
    planes = [work_ref[pl.ds(y, length, stride=rows_y), :].astype(bf16) for y in range(rows_y)]
    local = [dot_tn(jnp.concatenate(planes[y : y + 2], axis=1), table_ref[...]) for y in range(0, rows_y, 2)]

    @pl.when(step == 0)
    def factors():
        cos_x, sin_x = wave_ref[:atoms], wave_ref[atoms:]
        sources = overlap_ref.shape[0] // 2
        even = jnp.sum(overlap_ref[:sources].astype(f32), axis=0)
        odd = jnp.sum(overlap_ref[sources:].astype(f32), axis=0)
        summed = jnp.where(lax.axis_index("band") % 2 == 0, even, odd)
        coef = (summed[:atoms] + summed[atoms:]) * strength_ref[...]
        for pair in range(kinds * 2):
            coef_real = coef[:, 2 * pair : 2 * pair + 1]
            coef_imag = coef[:, 2 * pair + 1 : 2 * pair + 2]
            real = cos_x * coef_real + sin_x * coef_imag
            imag = cos_x * coef_imag - sin_x * coef_real
            base = pair * 2 * length
            factor_ref[:, base : base + length] = jnp.concatenate([real, imag], axis=0).astype(bf16)
            factor_ref[:, base + length : base + 2 * length] = jnp.concatenate(
                [imag, -real], axis=0
            ).astype(bf16)

    extra = dot_tn(phase_ref[...], factor_ref[...])

    def squared(start, axis):
        index = start + lax.broadcasted_iota(jnp.int32, mask_ref.shape, axis)
        wave = jnp.where(index >= length // 2, index - length, index)
        return wave * wave

    first_y = lax.axis_index("gy") * (rows_y * pl.num_programs(0)) + step * rows_y
    energy = squared(first_y, 0) + squared(lax.axis_index("gz") * rows_z, 1) + squared(0, 2)
    energy = kinetic_scale * 0.5 * energy.astype(f32)
    inside = mask_ref[...] != 0
    scale = 1.0 / root_weights(weight_ref, (2 * rows_z, 1), 0, rows_z)
    for y in range(rows_y):
        block = local[y // 2][y % 2 * 128 : y % 2 * 128 + 128]
        both = scale * (block[:64, : 2 * length] + block[64:, 2 * length :])
        radials = [channels_ref[c, y].astype(f32) for c in range(kinds)]
        for n in range(2):
            for part in range(2):
                cols = slice(part * length, part * length + length)
                total = both[n * rows_z : (n + 1) * rows_z, cols]
                total = total + energy[y] * orbitals_ref[n, y, :, cols].astype(f32)
                for c in range(kinds):
                    base = ((c * 2 + n) * 2 + part) * length
                    total = total + radials[c] * extra[y * rows_z : (y + 1) * rows_z, base : base + length]
                out_ref[n, y, :, cols] = jnp.where(inside[y], total, 0.0).astype(bf16)


def strength_kernel(atom_ref, kind_ref, coupling_ref, out_ref):
    row = lax.broadcasted_iota(jnp.int32, out_ref.shape, 0)
    kind = lax.broadcasted_iota(jnp.int32, out_ref.shape, 1) // 4
    total = jnp.zeros(out_ref.shape, f32)
    for p in range(coupling_ref.shape[0]):
        total += jnp.where((row == atom_ref[p]) & (kind == kind_ref[p]), coupling_ref[p], 0.0)
    out_ref[...] = total


def partners(axis, distance):
    return [(i, i ^ distance) for i in range(lax.axis_size(axis))]


def shards(
    orbitals,
    potential,
    cutoff_mask,
    channels,
    positions,
    proj_atom,
    proj_chan,
    coupling,
    occupations,
):
    rows_y, rows_z, length = cutoff_mask.shape
    parts_y = lax.axis_size("gy")
    parts_z = lax.axis_size("gz")
    parts_band = lax.axis_size("band")
    places = parts_y * parts_z
    bands = 2
    outer = parts_band // bands
    thin = length // places
    planes = thin // bands
    atoms = positions.shape[0]
    kinds = channels.shape[0]
    groups = [
        [(first * bands + b) * places + place for b in range(bands) for place in range(places)]
        for first in range(outer)
    ]
    inverse = dft_table(length, 1.0)
    forward = dft_table(length, -1.0)
    pick = np.eye(2, dtype=np.float32)
    split_inverse = inverse.reshape(2, length, 2, parts_z, rows_z)
    split_forward = forward.reshape(2, parts_z, rows_z, 2, length)
    order = np.arange(length).reshape(places, bands, planes).transpose(1, 0, 2).reshape(-1)
    inv_x = rounded(inverse[:, order], 2 * length)
    inv_y = rounded(inverse, 2 * length)
    inv_z = rounded(np.einsum("fzcsl,nm->scnlmfz", split_inverse, pick), 4 * length)
    fwd_z = rounded(np.einsum("cslfz,nm->nfzscml", split_forward, pick), 4 * length)
    fwd_y = rounded(forward, 2 * length)
    fwd_x = rounded(np.einsum("rkcx->xcrk", forward[..., order]), length)
    first_y = lax.axis_index("gy") * rows_y
    first_z = lax.axis_index("gz") * rows_z
    band = lax.axis_index("band") % bands

    params = pltpu.CompilerParams(vmem_limit_bytes=vmem_bytes)

    def cost(microseconds):
        return pl.CostEstimate(
            flops=int(microseconds * 1.0e9), bytes_accessed=int(microseconds * 1.0e6), transcendentals=0
        )

    steps = 2
    span = rows_y // steps
    whole = lambda *shape: pl.BlockSpec(shape, lambda i: (0,) * len(shape))
    orbitals_spec = pl.BlockSpec((2, span, rows_z, 2 * length), lambda i: (0, i, 0, 0))
    mask_spec = pl.BlockSpec((span, rows_z, length), lambda i: (i, 0, 0))
    channels_spec = pl.BlockSpec((kinds, span, rows_z, length), lambda i: (0, i, 0, 0))
    phase_spec = pl.BlockSpec((2 * atoms, span * rows_z), lambda i: (0, i))
    chunks_spec = pl.BlockSpec((bands * places, planes, span, 128), lambda i: (0, 0, i, 0))
    chunk_shape = (bands * places, planes, rows_y, 128)
    smem_spec = pl.BlockSpec(memory_space=pltpu.SMEM)

    def exchange(chunks):
        return lax.all_to_all(
            chunks, ("band", "gy", "gz"), split_axis=0, concat_axis=0, tiled=True, axis_index_groups=groups
        )

    spread = pl.pallas_call(
        spread_kernel,
        grid=(steps,),
        in_specs=[orbitals_spec, mask_spec, smem_spec, whole(2 * length, 2 * length)],
        out_specs=chunks_spec,
        out_shape=jax.ShapeDtypeStruct(chunk_shape, bf16),
        scratch_shapes=[pltpu.VMEM((length * span, 128), f32)],
        compiler_params=params,
        cost_estimate=cost(4),
        name="spread",
    )(orbitals, cutoff_mask, occupations, inv_x)
    potential_part = lax.dynamic_slice_in_dim(potential, band * planes, planes, 0)

    spread, positions = lax.optimization_barrier((spread, positions))
    arrived = exchange(spread)

    cos_y, sin_y = axis_phase(positions[:, 1], frequencies(first_y, rows_y, length))
    cos_z, sin_z = axis_phase(positions[:, 2], frequencies(first_z, rows_z, length))
    cos_x, sin_x = axis_phase(positions[:, 0], frequencies(0, length, length))
    cos_yz = cos_y[:, :, None] * cos_z[:, None, :] - sin_y[:, :, None] * sin_z[:, None, :]
    sin_yz = sin_y[:, :, None] * cos_z[:, None, :] + cos_y[:, :, None] * sin_z[:, None, :]
    phase = jnp.concatenate([cos_yz, sin_yz], axis=0).astype(bf16).reshape(2 * atoms, rows_y * rows_z)
    wave = jnp.concatenate([cos_x, sin_x], axis=0)
    overlap = pl.pallas_call(
        overlap_kernel,
        grid=(steps,),
        in_specs=[orbitals_spec, mask_spec, channels_spec, phase_spec, whole(2 * atoms, length)],
        out_specs=whole(2 * atoms, 128),
        out_shape=jax.ShapeDtypeStruct((2 * atoms, 128), bf16),
        scratch_shapes=[pltpu.VMEM((2 * atoms, kinds * 4 * length), f32)],
        compiler_params=params,
        cost_estimate=cost(0.1),
        name="overlap",
    )(orbitals, cutoff_mask, channels, phase, wave)
    arrived, overlap = lax.optimization_barrier((arrived, overlap))

    rows = planes * rows_y
    half = planes // 2 * length
    mine, theirs, folded = pl.pallas_call(
        field_kernel,
        grid=(bands,),
        in_specs=[
            pl.BlockSpec((places, rows, 128), lambda i: (i, 0, 0)),
            whole(planes, length, length),
            whole(2 * atoms, 128),
            whole(4 * length, 4 * length),
            whole(2 * length, 2 * length),
            whole(4 * length, 4 * length),
            whole(2 * length, 2 * length),
        ],
        out_specs=[
            whole(half, length),
            whole(half, length),
            pl.BlockSpec((places, rows + 2 * atoms, 128), lambda i: (i, 0, 0)),
        ],
        out_shape=[
            jax.ShapeDtypeStruct((half, length), bf16),
            jax.ShapeDtypeStruct((half, length), bf16),
            jax.ShapeDtypeStruct((bands * places, rows + 2 * atoms, 128), bf16),
        ],
        scratch_shapes=[pltpu.VMEM((planes * length, length), f32)],
        compiler_params=params,
        cost_estimate=cost(6),
        name="field",
    )(arrived.reshape(bands * places, rows, 128), potential_part, overlap, inv_z, inv_y, fwd_z, fwd_y)
    folded, coupling = lax.optimization_barrier((folded, coupling))
    strength = pl.pallas_call(
        strength_kernel,
        in_specs=[smem_spec] * 3,
        out_shape=jax.ShapeDtypeStruct((atoms, 128), f32),
        compiler_params=params,
        cost_estimate=cost(5),
        name="strength",
    )(proj_atom, proj_chan, coupling)
    returned = exchange(folded)

    near = lax.ppermute(theirs, "band", partners("band", bands))
    mine = (mine.astype(f32) + near.astype(f32)).astype(bf16)
    for distance in (2, 6):
        if distance < outer:
            got = lax.ppermute(mine, "band", partners("band", distance * bands))
            mine = (mine.astype(f32) + got.astype(f32)).astype(bf16)
    copies = [lax.ppermute(mine, "band", partners("band", d)) for d in (1, 2, 3)]
    applied = pl.pallas_call(
        apply_kernel,
        grid=(steps,),
        in_specs=[
            pl.BlockSpec((bands * places, planes * span, 128), lambda i: (0, i, 0)),
            pl.BlockSpec((bands * places, 2 * atoms, 128), lambda i: (0, rows // (2 * atoms), 0)),
            orbitals_spec,
            mask_spec,
            channels_spec,
            phase_spec,
            whole(2 * atoms, length),
            whole(atoms, 128),
            smem_spec,
            whole(length, 4 * length),
        ],
        out_specs=orbitals_spec,
        out_shape=jax.ShapeDtypeStruct(orbitals.shape, bf16),
        scratch_shapes=[
            pltpu.VMEM((2 * atoms, kinds * 4 * length), bf16),
            pltpu.VMEM((length * span, 128), f32),
        ],
        compiler_params=params,
        cost_estimate=cost(4),
        name="apply",
    )(returned, returned, orbitals, cutoff_mask, channels, phase, wave, strength, occupations, fwd_x)
    copies, applied = lax.optimization_barrier((copies, applied))
    place = lax.axis_index("band") % 4
    pieces = [mine] + copies
    pieces = [jnp.where(place & 1 != 0, pieces[j ^ 1], pieces[j]) for j in range(4)]
    pieces = [jnp.where(place & 2 != 0, pieces[j ^ 2], pieces[j]) for j in range(4)]
    density = jnp.concatenate([pieces[0], pieces[2], pieces[1], pieces[3]], axis=0)
    return (applied, density.astype(f32).reshape(potential.shape))


def solution(mesh):
    placed = (
        P("band", "gy", "gz", None),
        P(("gy", "gz"), None, None),
        P("gy", "gz", None),
        P(None, "gy", "gz", None),
        P(),
        P(),
        P(),
        P(),
        P("band"),
    )
    return jax.shard_map(
        shards,
        mesh=mesh,
        in_specs=placed,
        out_specs=(P("band", "gy", "gz", None), P(("gy", "gz"), None, None)),
        check_vma=False,
    )
```

```python
import functools
import math

import jax
import jax.numpy as jnp
import ml_dtypes
import numpy as np
from jax import lax
from jax.experimental import pallas as pl
from jax.experimental.pallas import tpu as pltpu
from jax.sharding import PartitionSpec as P

kinetic_scale = 1.0 / 1024.0
vmem_bytes = 63 * 1024 * 1024
bf16 = jnp.bfloat16
f32 = jnp.float32


def dft_table(length, sign_value):
    grid_index = np.arange(length)
    product = grid_index[:, None] * grid_index[None, :] % length
    phase_angle = np.float32(2.0 * math.pi / length) * product.astype(np.float32)
    cosine_part = np.cos(phase_angle) / np.float32(math.sqrt(length))
    sine_part = sign_value * np.sin(phase_angle) / np.float32(math.sqrt(length))
    upper_rows = np.stack([cosine_part, -sine_part], axis=1)
    lower_rows = np.stack([sine_part, cosine_part], axis=1)
    return np.stack([upper_rows, lower_rows], axis=0).astype(np.float32)


def rounded(table, rows):
    return jnp.asarray(np.ascontiguousarray(table).reshape(rows, -1).astype(ml_dtypes.bfloat16))


def frequencies(first_index, span, length):
    grid_index = first_index + jnp.arange(span, dtype=jnp.int32)
    return jnp.where(grid_index >= length // 2, grid_index - length, grid_index).astype(f32)


def axis_phase(coordinate, freq):
    phase_angle = 2.0 * math.pi * (coordinate[:, None] * freq[None, :])
    return (jnp.cos(phase_angle), jnp.sin(phase_angle))


def dot(left, right):
    return jnp.dot(left, right, preferred_element_type=f32)


def dot_nt(left, right):
    return lax.dot_general(left, right, (((1,), (1,)), ((), ())), preferred_element_type=f32)


def dot_tn(left, right):
    return lax.dot_general(left, right, (((0,), (0,)), ((), ())), preferred_element_type=f32)


def root_weights(weight_ref, shape, axis, span):
    index = lax.broadcasted_iota(jnp.int32, shape, axis)
    return jnp.sqrt(jnp.where(index // span % 2 == 0, weight_ref[0], weight_ref[1]))


def spread_kernel(orbitals_ref, mask_ref, weight_ref, table_ref, out_ref, work_ref):
    rows_y, rows_z, length = mask_ref.shape
    mask = jnp.where(mask_ref[...] != 0, 1.0, 0.0).astype(bf16)
    mask = jnp.concatenate([mask, mask], axis=2)
    lane = lax.broadcasted_iota(jnp.int32, (length, 128), 1)
    roots = root_weights(weight_ref, (1, 128), 1, rows_z)
    spreads = []
    for pair in range(0, rows_y, 2):
        rows = []
        for y in (pair, pair + 1):
            both = jnp.concatenate([orbitals_ref[0, y] * mask[y], orbitals_ref[1, y] * mask[y]], axis=0)
            rows += [both, both]
        spreads.append(dot_nt(table_ref[...], jnp.concatenate(rows, axis=0)))
    for y in range(rows_y):
        spread = spreads[y // 2][:, y % 2 * 128 : y % 2 * 128 + 128]
        tile = jnp.where(lane < 64, spread[:length], spread[length:])
        work_ref[pl.ds(y, length, stride=rows_y), :] = tile * roots
    out_ref[...] = work_ref[...].reshape(out_ref.shape).astype(bf16)


def overlap_kernel(orbitals_ref, mask_ref, channels_ref, phase_ref, wave_ref, out_ref, sums_ref):
    step = pl.program_id(0)
    rows = mask_ref.shape[0] * mask_ref.shape[1]
    length = mask_ref.shape[2]
    atoms = wave_ref.shape[0] // 2
    kinds = channels_ref.shape[0]
    mask = jnp.where(mask_ref[...] != 0, 1.0, 0.0).astype(bf16)
    orbs = [orbitals_ref[n].reshape(rows, 2 * length) for n in range(2)]
    columns = []
    for c in range(kinds):
        radial = (channels_ref[c] * mask).reshape(rows, length)
        radial = jnp.concatenate([radial, radial], axis=1)
        columns += [radial * orbs[0], radial * orbs[1]]
    part = dot(phase_ref[...], jnp.concatenate(columns, axis=1))

    @pl.when(step == 0)
    def first():
        sums_ref[...] = part

    @pl.when(step > 0)
    def later():
        sums_ref[...] += part

    @pl.when(step == pl.num_programs(0) - 1)
    def last():
        cos_x, sin_x = wave_ref[:atoms], wave_ref[atoms:]
        lane = lax.broadcasted_iota(jnp.int32, (atoms, 128), 1)
        total = jnp.zeros((atoms, 128), f32)
        for pair in range(kinds * 2):
            base = pair * 2 * length
            real_cols = slice(base, base + length)
            imag_cols = slice(base + length, base + 2 * length)
            real = sums_ref[:atoms, real_cols] - sums_ref[atoms:, imag_cols]
            imag = sums_ref[atoms:, real_cols] + sums_ref[:atoms, imag_cols]
            real_over = jnp.sum(real * cos_x - imag * sin_x, axis=1, keepdims=True)
            imag_over = jnp.sum(real * sin_x + imag * cos_x, axis=1, keepdims=True)
            total = jnp.where(lane == 2 * pair, real_over, total)
            total = jnp.where(lane == 2 * pair + 1, imag_over, total)
        high = total.astype(bf16).astype(f32)
        out_ref[...] = jnp.concatenate([high, total - high], axis=0).astype(bf16)


def field_kernel(
    arrived_ref,
    potential_ref,
    overlap_ref,
    inv_z_ref,
    inv_y_ref,
    fwd_z_ref,
    fwd_y_ref,
    mine_ref,
    theirs_ref,
    out_ref,
    sums_ref,
):
    step = pl.program_id(0)
    planes, length = potential_ref.shape[:2]
    parts = arrived_ref.shape[0] // 4
    rows = arrived_ref.shape[1] // planes
    columns = jnp.concatenate(
        [jnp.concatenate([arrived_ref[sy * 4 + sz] for sz in range(4)], axis=1) for sy in range(parts)],
        axis=0,
    )
    halfway = dot(columns, inv_z_ref[...]).astype(bf16)
    stacked = []
    for x in range(planes):
        first = [(sy * planes + x) * rows for sy in range(parts)]
        plane = jnp.concatenate([halfway[start : start + rows] for start in first], axis=0)
        real = jnp.concatenate([plane[:, 0:128], plane[:, 256:384]], axis=1)
        imag = jnp.concatenate([plane[:, 128:256], plane[:, 384:512]], axis=1)
        stacked.append(jnp.concatenate([real, imag], axis=0))
    fields = [dot(inv_y_ref[...], block) for block in stacked]
    scaled = []
    for x, field in enumerate(fields):
        real, imag = field[:length], field[length:]
        square = real * real + imag * imag
        density = square[:, :length] + square[:, length:]
        here = slice(x * length, (x + 1) * length)
        sums_ref[here, :] = jnp.where(step == 0, density, sums_ref[here, :] + density)
        potential = jnp.concatenate([potential_ref[x], potential_ref[x]], axis=1)
        potential = jnp.concatenate([potential, potential], axis=0)
        scaled.append((potential * field).astype(bf16))
    folded = [dot(fwd_y_ref[...], block).astype(bf16) for block in scaled]
    back = []
    for block in folded:
        real, imag = block[:length], block[length:]
        back.append(
            jnp.concatenate([real[:, :length], imag[:, :length], real[:, length:], imag[:, length:]], axis=1)
        )
    back = dot(jnp.concatenate(back, axis=0), fwd_z_ref[...]).astype(bf16)
    span = rows // 2
    for x in range(planes):
        for sy in range(parts):
            for half in range(2):
                start = x * length + sy * rows + half * span
                row = (half * planes + x) * span
                for sz in range(4):
                    out_ref[sy * 4 + sz, row : row + span, :] = back[
                        start : start + span, sz * 128 : sz * 128 + 128
                    ]
    for place in range(out_ref.shape[0]):
        out_ref[place, planes * rows :, :] = overlap_ref[...]

    @pl.when(step == pl.num_programs(0) - 1)
    def last():
        half = planes // 2 * length
        low, high = sums_ref[:half, :].astype(bf16), sums_ref[half:, :].astype(bf16)
        upper = lax.axis_index("band") // 2 % 2
        mine_ref[...] = jnp.where(upper == 0, low, high)
        theirs_ref[...] = jnp.where(upper == 0, high, low)


def apply_kernel(
    returned_ref,
    overlap_ref,
    orbitals_ref,
    mask_ref,
    channels_ref,
    phase_ref,
    wave_ref,
    strength_ref,
    weight_ref,
    table_ref,
    out_ref,
    factor_ref,
    work_ref,
):
    step = pl.program_id(0)
    rows_y, rows_z, length = mask_ref.shape
    atoms = wave_ref.shape[0] // 2
    kinds = channels_ref.shape[0]

    work_ref[...] = returned_ref[...].astype(f32).reshape(work_ref.shape)
    planes = [work_ref[pl.ds(y, length, stride=rows_y), :].astype(bf16) for y in range(rows_y)]
    local = [dot_tn(jnp.concatenate(planes[y : y + 2], axis=1), table_ref[...]) for y in range(0, rows_y, 2)]

    @pl.when(step == 0)
    def factors():
        cos_x, sin_x = wave_ref[:atoms], wave_ref[atoms:]
        sources = overlap_ref.shape[0] // 2
        even = jnp.sum(overlap_ref[:sources].astype(f32), axis=0)
        odd = jnp.sum(overlap_ref[sources:].astype(f32), axis=0)
        summed = jnp.where(lax.axis_index("band") % 2 == 0, even, odd)
        coef = (summed[:atoms] + summed[atoms:]) * strength_ref[...]
        for pair in range(kinds * 2):
            coef_real = coef[:, 2 * pair : 2 * pair + 1]
            coef_imag = coef[:, 2 * pair + 1 : 2 * pair + 2]
            real = cos_x * coef_real + sin_x * coef_imag
            imag = cos_x * coef_imag - sin_x * coef_real
            base = pair * 2 * length
            factor_ref[:, base : base + length] = jnp.concatenate([real, imag], axis=0).astype(bf16)
            factor_ref[:, base + length : base + 2 * length] = jnp.concatenate(
                [imag, -real], axis=0
            ).astype(bf16)

    extra = dot_tn(phase_ref[...], factor_ref[...])

    def squared(start, axis):
        index = start + lax.broadcasted_iota(jnp.int32, mask_ref.shape, axis)
        wave = jnp.where(index >= length // 2, index - length, index)
        return wave * wave

    first_y = lax.axis_index("gy") * (rows_y * pl.num_programs(0)) + step * rows_y
    energy = squared(first_y, 0) + squared(lax.axis_index("gz") * rows_z, 1) + squared(0, 2)
    energy = kinetic_scale * 0.5 * energy.astype(f32)
    inside = mask_ref[...] != 0
    scale = 1.0 / root_weights(weight_ref, (2 * rows_z, 1), 0, rows_z)
    for y in range(rows_y):
        block = local[y // 2][y % 2 * 128 : y % 2 * 128 + 128]
        both = scale * (block[:64, : 2 * length] + block[64:, 2 * length :])
        radials = [channels_ref[c, y].astype(f32) for c in range(kinds)]
        for n in range(2):
            for part in range(2):
                cols = slice(part * length, part * length + length)
                total = both[n * rows_z : (n + 1) * rows_z, cols]
                total = total + energy[y] * orbitals_ref[n, y, :, cols].astype(f32)
                for c in range(kinds):
                    base = ((c * 2 + n) * 2 + part) * length
                    total = total + radials[c] * extra[y * rows_z : (y + 1) * rows_z, base : base + length]
                out_ref[n, y, :, cols] = jnp.where(inside[y], total, 0.0).astype(bf16)


def strength_kernel(atom_ref, kind_ref, coupling_ref, out_ref):
    row = lax.broadcasted_iota(jnp.int32, out_ref.shape, 0)
    kind = lax.broadcasted_iota(jnp.int32, out_ref.shape, 1) // 4
    total = jnp.zeros(out_ref.shape, f32)
    for p in range(coupling_ref.shape[0]):
        total += jnp.where((row == atom_ref[p]) & (kind == kind_ref[p]), coupling_ref[p], 0.0)
    out_ref[...] = total


def partners(axis, distance):
    return [(i, i ^ distance) for i in range(lax.axis_size(axis))]


def shards(
    orbitals,
    potential,
    cutoff_mask,
    channels,
    positions,
    proj_atom,
    proj_chan,
    coupling,
    occupations,
):
    rows_y, rows_z, length = cutoff_mask.shape
    parts_y = lax.axis_size("gy")
    parts_z = lax.axis_size("gz")
    parts_band = lax.axis_size("band")
    places = parts_y * parts_z
    bands = 2
    outer = parts_band // bands
    thin = length // places
    planes = thin // bands
    atoms = positions.shape[0]
    kinds = channels.shape[0]
    groups = [
        [(first * bands + b) * places + place for b in range(bands) for place in range(places)]
        for first in range(outer)
    ]
    inverse = dft_table(length, 1.0)
    forward = dft_table(length, -1.0)
    pick = np.eye(2, dtype=np.float32)
    split_inverse = inverse.reshape(2, length, 2, parts_z, rows_z)
    split_forward = forward.reshape(2, parts_z, rows_z, 2, length)
    order = np.arange(length).reshape(places, bands, planes).transpose(1, 0, 2).reshape(-1)
    inv_x = rounded(inverse[:, order], 2 * length)
    inv_y = rounded(inverse, 2 * length)
    inv_z = rounded(np.einsum("fzcsl,nm->scnlmfz", split_inverse, pick), 4 * length)
    fwd_z = rounded(np.einsum("cslfz,nm->nfzscml", split_forward, pick), 4 * length)
    fwd_y = rounded(forward, 2 * length)
    fwd_x = rounded(np.einsum("rkcx->xcrk", forward[..., order]), length)
    first_y = lax.axis_index("gy") * rows_y
    first_z = lax.axis_index("gz") * rows_z
    band = lax.axis_index("band") % bands

    params = pltpu.CompilerParams(vmem_limit_bytes=vmem_bytes)

    def cost(microseconds):
        return pl.CostEstimate(
            flops=int(microseconds * 1.0e9), bytes_accessed=int(microseconds * 1.0e6), transcendentals=0
        )

    steps = 2
    span = rows_y // steps
    whole = lambda *shape: pl.BlockSpec(shape, lambda i: (0,) * len(shape))
    orbitals_spec = pl.BlockSpec((2, span, rows_z, 2 * length), lambda i: (0, i, 0, 0))
    mask_spec = pl.BlockSpec((span, rows_z, length), lambda i: (i, 0, 0))
    channels_spec = pl.BlockSpec((kinds, span, rows_z, length), lambda i: (0, i, 0, 0))
    phase_spec = pl.BlockSpec((2 * atoms, span * rows_z), lambda i: (0, i))
    chunks_spec = pl.BlockSpec((bands * places, planes, span, 128), lambda i: (0, 0, i, 0))
    chunk_shape = (bands * places, planes, rows_y, 128)
    smem_spec = pl.BlockSpec(memory_space=pltpu.SMEM)

    def exchange(chunks):
        return lax.all_to_all(
            chunks, ("band", "gy", "gz"), split_axis=0, concat_axis=0, tiled=True, axis_index_groups=groups
        )

    spread = pl.pallas_call(
        spread_kernel,
        grid=(steps,),
        in_specs=[orbitals_spec, mask_spec, smem_spec, whole(2 * length, 2 * length)],
        out_specs=chunks_spec,
        out_shape=jax.ShapeDtypeStruct(chunk_shape, bf16),
        scratch_shapes=[pltpu.VMEM((length * span, 128), f32)],
        compiler_params=params,
        cost_estimate=cost(4),
        name="spread",
    )(orbitals, cutoff_mask, occupations, inv_x)
    potential_part = lax.dynamic_slice_in_dim(potential, band * planes, planes, 0)

    spread, positions = lax.optimization_barrier((spread, positions))
    arrived = exchange(spread)

    cos_y, sin_y = axis_phase(positions[:, 1], frequencies(first_y, rows_y, length))
    cos_z, sin_z = axis_phase(positions[:, 2], frequencies(first_z, rows_z, length))
    cos_x, sin_x = axis_phase(positions[:, 0], frequencies(0, length, length))
    cos_yz = cos_y[:, :, None] * cos_z[:, None, :] - sin_y[:, :, None] * sin_z[:, None, :]
    sin_yz = sin_y[:, :, None] * cos_z[:, None, :] + cos_y[:, :, None] * sin_z[:, None, :]
    phase = jnp.concatenate([cos_yz, sin_yz], axis=0).astype(bf16).reshape(2 * atoms, rows_y * rows_z)
    wave = jnp.concatenate([cos_x, sin_x], axis=0)
    positions, coupling = lax.optimization_barrier((positions, coupling))
    strength = pl.pallas_call(
        strength_kernel,
        in_specs=[smem_spec] * 3,
        out_shape=jax.ShapeDtypeStruct((atoms, 128), f32),
        compiler_params=params,
        cost_estimate=cost(0.1),
        name="strength",
    )(proj_atom, proj_chan, coupling)
    overlap = pl.pallas_call(
        overlap_kernel,
        grid=(steps,),
        in_specs=[orbitals_spec, mask_spec, channels_spec, phase_spec, whole(2 * atoms, length)],
        out_specs=whole(2 * atoms, 128),
        out_shape=jax.ShapeDtypeStruct((2 * atoms, 128), bf16),
        scratch_shapes=[pltpu.VMEM((2 * atoms, kinds * 4 * length), f32)],
        compiler_params=params,
        cost_estimate=cost(0.1),
        name="overlap",
    )(orbitals, cutoff_mask, channels, phase, wave)
    arrived, overlap, strength = lax.optimization_barrier((arrived, overlap, strength))

    rows = planes * rows_y
    half = planes // 2 * length
    mine, theirs, folded = pl.pallas_call(
        field_kernel,
        grid=(bands,),
        in_specs=[
            pl.BlockSpec((places, rows, 128), lambda i: (i, 0, 0)),
            whole(planes, length, length),
            whole(2 * atoms, 128),
            whole(4 * length, 4 * length),
            whole(2 * length, 2 * length),
            whole(4 * length, 4 * length),
            whole(2 * length, 2 * length),
        ],
        out_specs=[
            whole(half, length),
            whole(half, length),
            pl.BlockSpec((places, rows + 2 * atoms, 128), lambda i: (i, 0, 0)),
        ],
        out_shape=[
            jax.ShapeDtypeStruct((half, length), bf16),
            jax.ShapeDtypeStruct((half, length), bf16),
            jax.ShapeDtypeStruct((bands * places, rows + 2 * atoms, 128), bf16),
        ],
        scratch_shapes=[pltpu.VMEM((planes * length, length), f32)],
        compiler_params=params,
        cost_estimate=cost(6),
        name="field",
    )(arrived.reshape(bands * places, rows, 128), potential_part, overlap, inv_z, inv_y, fwd_z, fwd_y)
    returned = exchange(folded)

    near = lax.ppermute(theirs, "band", partners("band", bands))
    mine = (mine.astype(f32) + near.astype(f32)).astype(bf16)
    got = lax.ppermute(mine, "band", partners("band", 2 * bands))
    mine = (mine.astype(f32) + got.astype(f32)).astype(bf16)
    far, near, both = [lax.ppermute(mine, "band", partners("band", d * bands)) for d in (6, 1, 7)]
    mine = (mine.astype(f32) + far.astype(f32)).astype(bf16)
    near = (near.astype(f32) + both.astype(f32)).astype(bf16)
    upper = lax.axis_index("band") // bands % 2
    mine = jnp.where(upper == 0, jnp.stack([mine, near]), jnp.stack([near, mine]))
    other = lax.ppermute(mine, "band", partners("band", 1))
    applied = pl.pallas_call(
        apply_kernel,
        grid=(steps,),
        in_specs=[
            pl.BlockSpec((bands * places, planes * span, 128), lambda i: (0, i, 0)),
            pl.BlockSpec((bands * places, 2 * atoms, 128), lambda i: (0, rows // (2 * atoms), 0)),
            orbitals_spec,
            mask_spec,
            channels_spec,
            phase_spec,
            whole(2 * atoms, length),
            whole(atoms, 128),
            smem_spec,
            whole(length, 4 * length),
        ],
        out_specs=orbitals_spec,
        out_shape=jax.ShapeDtypeStruct(orbitals.shape, bf16),
        scratch_shapes=[
            pltpu.VMEM((2 * atoms, kinds * 4 * length), bf16),
            pltpu.VMEM((length * span, 128), f32),
        ],
        compiler_params=params,
        cost_estimate=cost(4),
        name="apply",
    )(returned, returned, orbitals, cutoff_mask, channels, phase, wave, strength, occupations, fwd_x)
    other, applied = lax.optimization_barrier((other, applied))
    density = jnp.where(band == 0, jnp.stack([mine, other]), jnp.stack([other, mine]))
    return (applied, density.astype(f32).reshape(potential.shape))


def solution(mesh):
    placed = (
        P("band", "gy", "gz", None),
        P(("gy", "gz"), None, None),
        P("gy", "gz", None),
        P(None, "gy", "gz", None),
        P(),
        P(),
        P(),
        P(),
        P("band"),
    )
    return jax.shard_map(
        shards,
        mesh=mesh,
        in_specs=placed,
        out_specs=(P("band", "gy", "gz", None), P(("gy", "gz"), None, None)),
        check_vma=False,
    )
```

```python
import functools
import math

import jax
import jax.numpy as jnp
import ml_dtypes
import numpy as np
from jax import lax
from jax.experimental import pallas as pl
from jax.experimental.pallas import tpu as pltpu
from jax.sharding import PartitionSpec as P

kinetic_scale = 1.0 / 1024.0
vmem_bytes = 63 * 1024 * 1024
bf16 = jnp.bfloat16
f32 = jnp.float32


def dft_table(length, sign_value):
    grid_index = np.arange(length)
    product = grid_index[:, None] * grid_index[None, :] % length
    phase_angle = np.float32(2.0 * math.pi / length) * product.astype(np.float32)
    cosine_part = np.cos(phase_angle) / np.float32(math.sqrt(length))
    sine_part = sign_value * np.sin(phase_angle) / np.float32(math.sqrt(length))
    upper_rows = np.stack([cosine_part, -sine_part], axis=1)
    lower_rows = np.stack([sine_part, cosine_part], axis=1)
    return np.stack([upper_rows, lower_rows], axis=0).astype(np.float32)


def rounded(table, rows):
    return jnp.asarray(np.ascontiguousarray(table).reshape(rows, -1).astype(ml_dtypes.bfloat16))


def frequencies(first_index, span, length):
    grid_index = first_index + jnp.arange(span, dtype=jnp.int32)
    return jnp.where(grid_index >= length // 2, grid_index - length, grid_index).astype(f32)


def axis_phase(coordinate, freq):
    phase_angle = 2.0 * math.pi * (coordinate[:, None] * freq[None, :])
    return (jnp.cos(phase_angle), jnp.sin(phase_angle))


def dot(left, right):
    return jnp.dot(left, right, preferred_element_type=f32)


def dot_nt(left, right):
    return lax.dot_general(left, right, (((1,), (1,)), ((), ())), preferred_element_type=f32)


def dot_tn(left, right):
    return lax.dot_general(left, right, (((0,), (0,)), ((), ())), preferred_element_type=f32)


def root_weights(weight_ref, shape, axis, span):
    index = lax.broadcasted_iota(jnp.int32, shape, axis)
    return jnp.sqrt(jnp.where(index // span % 2 == 0, weight_ref[0], weight_ref[1]))


def spread_kernel(orbitals_ref, mask_ref, weight_ref, table_ref, out_ref, work_ref):
    rows_y, rows_z, length = mask_ref.shape
    mask = jnp.where(mask_ref[...] != 0, 1.0, 0.0).astype(bf16)
    mask = jnp.concatenate([mask, mask], axis=2)
    lane = lax.broadcasted_iota(jnp.int32, (length, 128), 1)
    roots = root_weights(weight_ref, (1, 128), 1, rows_z)
    spreads = []
    for pair in range(0, rows_y, 2):
        rows = []
        for y in (pair, pair + 1):
            both = jnp.concatenate([orbitals_ref[0, y] * mask[y], orbitals_ref[1, y] * mask[y]], axis=0)
            rows += [both, both]
        spreads.append(dot_nt(table_ref[...], jnp.concatenate(rows, axis=0)))
    for y in range(rows_y):
        spread = spreads[y // 2][:, y % 2 * 128 : y % 2 * 128 + 128]
        tile = jnp.where(lane < 64, spread[:length], spread[length:])
        work_ref[pl.ds(y, length, stride=rows_y), :] = tile * roots
    out_ref[...] = work_ref[...].reshape(out_ref.shape).astype(bf16)


def overlap_kernel(orbitals_ref, mask_ref, channels_ref, phase_ref, wave_ref, out_ref, sums_ref):
    step = pl.program_id(0)
    rows = mask_ref.shape[0] * mask_ref.shape[1]
    length = mask_ref.shape[2]
    atoms = wave_ref.shape[0] // 2
    kinds = channels_ref.shape[0]
    mask = jnp.where(mask_ref[...] != 0, 1.0, 0.0).astype(bf16)
    orbs = [orbitals_ref[n].reshape(rows, 2 * length) for n in range(2)]
    columns = []
    for c in range(kinds):
        radial = (channels_ref[c] * mask).reshape(rows, length)
        radial = jnp.concatenate([radial, radial], axis=1)
        columns += [radial * orbs[0], radial * orbs[1]]
    part = dot(phase_ref[...], jnp.concatenate(columns, axis=1))

    @pl.when(step == 0)
    def first():
        sums_ref[...] = part

    @pl.when(step > 0)
    def later():
        sums_ref[...] += part

    @pl.when(step == pl.num_programs(0) - 1)
    def last():
        cos_x, sin_x = wave_ref[:atoms], wave_ref[atoms:]
        lane = lax.broadcasted_iota(jnp.int32, (atoms, 128), 1)
        total = jnp.zeros((atoms, 128), f32)
        for pair in range(kinds * 2):
            base = pair * 2 * length
            real_cols = slice(base, base + length)
            imag_cols = slice(base + length, base + 2 * length)
            real = sums_ref[:atoms, real_cols] - sums_ref[atoms:, imag_cols]
            imag = sums_ref[atoms:, real_cols] + sums_ref[:atoms, imag_cols]
            real_over = jnp.sum(real * cos_x - imag * sin_x, axis=1, keepdims=True)
            imag_over = jnp.sum(real * sin_x + imag * cos_x, axis=1, keepdims=True)
            total = jnp.where(lane == 2 * pair, real_over, total)
            total = jnp.where(lane == 2 * pair + 1, imag_over, total)
        high = total.astype(bf16).astype(f32)
        out_ref[...] = jnp.concatenate([high, total - high], axis=0).astype(bf16)


def field_kernel(
    arrived_ref,
    potential_ref,
    overlap_ref,
    inv_z_ref,
    inv_y_ref,
    fwd_z_ref,
    fwd_y_ref,
    mine_ref,
    theirs_ref,
    out_ref,
    sums_ref,
):
    step = pl.program_id(0)
    planes, length = potential_ref.shape[:2]
    parts = arrived_ref.shape[0] // 4
    rows = arrived_ref.shape[1] // planes
    columns = jnp.concatenate(
        [jnp.concatenate([arrived_ref[sy * 4 + sz] for sz in range(4)], axis=1) for sy in range(parts)],
        axis=0,
    )
    halfway = dot(columns, inv_z_ref[...]).astype(bf16)
    stacked = []
    for x in range(planes):
        first = [(sy * planes + x) * rows for sy in range(parts)]
        plane = jnp.concatenate([halfway[start : start + rows] for start in first], axis=0)
        real = jnp.concatenate([plane[:, 0:128], plane[:, 256:384]], axis=1)
        imag = jnp.concatenate([plane[:, 128:256], plane[:, 384:512]], axis=1)
        stacked.append(jnp.concatenate([real, imag], axis=0))
    fields = [dot(inv_y_ref[...], block) for block in stacked]
    scaled = []
    for x, field in enumerate(fields):
        real, imag = field[:length], field[length:]
        square = real * real + imag * imag
        density = square[:, :length] + square[:, length:]
        here = slice(x * length, (x + 1) * length)
        sums_ref[here, :] = jnp.where(step == 0, density, sums_ref[here, :] + density)
        potential = jnp.concatenate([potential_ref[x], potential_ref[x]], axis=1)
        potential = jnp.concatenate([potential, potential], axis=0)
        scaled.append((potential * field).astype(bf16))
    folded = [dot(fwd_y_ref[...], block).astype(bf16) for block in scaled]
    back = []
    for block in folded:
        real, imag = block[:length], block[length:]
        back.append(
            jnp.concatenate([real[:, :length], imag[:, :length], real[:, length:], imag[:, length:]], axis=1)
        )
    back = dot(jnp.concatenate(back, axis=0), fwd_z_ref[...]).astype(bf16)
    span = rows // 2
    for x in range(planes):
        for sy in range(parts):
            for half in range(2):
                start = x * length + sy * rows + half * span
                row = (half * planes + x) * span
                for sz in range(4):
                    out_ref[sy * 4 + sz, row : row + span, :] = back[
                        start : start + span, sz * 128 : sz * 128 + 128
                    ]
    for place in range(out_ref.shape[0]):
        out_ref[place, planes * rows :, :] = overlap_ref[...]

    @pl.when(step == pl.num_programs(0) - 1)
    def last():
        half = planes // 2 * length
        low, high = sums_ref[:half, :].astype(bf16), sums_ref[half:, :].astype(bf16)
        upper = lax.axis_index("band") // 2 % 2
        mine_ref[...] = jnp.where(upper == 0, low, high)
        theirs_ref[...] = jnp.where(upper == 0, high, low)


def apply_kernel(
    returned_ref,
    overlap_ref,
    orbitals_ref,
    mask_ref,
    channels_ref,
    phase_ref,
    wave_ref,
    strength_ref,
    weight_ref,
    table_ref,
    out_ref,
    factor_ref,
    work_ref,
):
    step = pl.program_id(0)
    rows_y, rows_z, length = mask_ref.shape
    atoms = wave_ref.shape[0] // 2
    kinds = channels_ref.shape[0]

    work_ref[...] = returned_ref[...].astype(f32).reshape(work_ref.shape)
    planes = [work_ref[pl.ds(y, length, stride=rows_y), :].astype(bf16) for y in range(rows_y)]
    local = [dot_tn(jnp.concatenate(planes[y : y + 2], axis=1), table_ref[...]) for y in range(0, rows_y, 2)]

    @pl.when(step == 0)
    def factors():
        cos_x, sin_x = wave_ref[:atoms], wave_ref[atoms:]
        sources = overlap_ref.shape[0] // 2
        even = jnp.sum(overlap_ref[:sources].astype(f32), axis=0)
        odd = jnp.sum(overlap_ref[sources:].astype(f32), axis=0)
        summed = jnp.where(lax.axis_index("band") % 2 == 0, even, odd)
        coef = (summed[:atoms] + summed[atoms:]) * strength_ref[...]
        for pair in range(kinds * 2):
            coef_real = coef[:, 2 * pair : 2 * pair + 1]
            coef_imag = coef[:, 2 * pair + 1 : 2 * pair + 2]
            real = cos_x * coef_real + sin_x * coef_imag
            imag = cos_x * coef_imag - sin_x * coef_real
            base = pair * 2 * length
            factor_ref[:, base : base + length] = jnp.concatenate([real, imag], axis=0).astype(bf16)
            factor_ref[:, base + length : base + 2 * length] = jnp.concatenate(
                [imag, -real], axis=0
            ).astype(bf16)

    extra = dot_tn(phase_ref[...], factor_ref[...])

    def squared(start, axis):
        index = start + lax.broadcasted_iota(jnp.int32, mask_ref.shape, axis)
        wave = jnp.where(index >= length // 2, index - length, index)
        return wave * wave

    first_y = lax.axis_index("gy") * (rows_y * pl.num_programs(0)) + step * rows_y
    energy = squared(first_y, 0) + squared(lax.axis_index("gz") * rows_z, 1) + squared(0, 2)
    energy = kinetic_scale * 0.5 * energy.astype(f32)
    inside = mask_ref[...] != 0
    scale = 1.0 / root_weights(weight_ref, (2 * rows_z, 1), 0, rows_z)
    for y in range(rows_y):
        block = local[y // 2][y % 2 * 128 : y % 2 * 128 + 128]
        both = scale * (block[:64, : 2 * length] + block[64:, 2 * length :])
        radials = [channels_ref[c, y].astype(f32) for c in range(kinds)]
        for n in range(2):
            for part in range(2):
                cols = slice(part * length, part * length + length)
                total = both[n * rows_z : (n + 1) * rows_z, cols]
                total = total + energy[y] * orbitals_ref[n, y, :, cols].astype(f32)
                for c in range(kinds):
                    base = ((c * 2 + n) * 2 + part) * length
                    total = total + radials[c] * extra[y * rows_z : (y + 1) * rows_z, base : base + length]
                out_ref[n, y, :, cols] = jnp.where(inside[y], total, 0.0).astype(bf16)


def strength_kernel(atom_ref, kind_ref, coupling_ref, out_ref):
    row = lax.broadcasted_iota(jnp.int32, out_ref.shape, 0)
    kind = lax.broadcasted_iota(jnp.int32, out_ref.shape, 1) // 4
    total = jnp.zeros(out_ref.shape, f32)
    for p in range(coupling_ref.shape[0]):
        total += jnp.where((row == atom_ref[p]) & (kind == kind_ref[p]), coupling_ref[p], 0.0)
    out_ref[...] = total


def partners(axis, distance):
    return [(i, i ^ distance) for i in range(lax.axis_size(axis))]


def shards(
    orbitals,
    potential,
    cutoff_mask,
    channels,
    positions,
    proj_atom,
    proj_chan,
    coupling,
    occupations,
):
    rows_y, rows_z, length = cutoff_mask.shape
    parts_y = lax.axis_size("gy")
    parts_z = lax.axis_size("gz")
    parts_band = lax.axis_size("band")
    places = parts_y * parts_z
    bands = 2
    outer = parts_band // bands
    thin = length // places
    planes = thin // bands
    atoms = positions.shape[0]
    kinds = channels.shape[0]
    groups = [
        [(first * bands + b) * places + place for b in range(bands) for place in range(places)]
        for first in range(outer)
    ]
    inverse = dft_table(length, 1.0)
    forward = dft_table(length, -1.0)
    pick = np.eye(2, dtype=np.float32)
    split_inverse = inverse.reshape(2, length, 2, parts_z, rows_z)
    split_forward = forward.reshape(2, parts_z, rows_z, 2, length)
    order = np.arange(length).reshape(places, bands, planes).transpose(1, 0, 2).reshape(-1)
    inv_x = rounded(inverse[:, order], 2 * length)
    inv_y = rounded(inverse, 2 * length)
    inv_z = rounded(np.einsum("fzcsl,nm->scnlmfz", split_inverse, pick), 4 * length)
    fwd_z = rounded(np.einsum("cslfz,nm->nfzscml", split_forward, pick), 4 * length)
    fwd_y = rounded(forward, 2 * length)
    fwd_x = rounded(np.einsum("rkcx->xcrk", forward[..., order]), length)
    first_y = lax.axis_index("gy") * rows_y
    first_z = lax.axis_index("gz") * rows_z
    band = lax.axis_index("band") % bands

    params = pltpu.CompilerParams(vmem_limit_bytes=vmem_bytes)

    def cost(microseconds):
        return pl.CostEstimate(
            flops=int(microseconds * 1.0e9), bytes_accessed=int(microseconds * 1.0e6), transcendentals=0
        )

    steps = 2
    span = rows_y // steps
    whole = lambda *shape: pl.BlockSpec(shape, lambda i: (0,) * len(shape))
    orbitals_spec = pl.BlockSpec((2, span, rows_z, 2 * length), lambda i: (0, i, 0, 0))
    mask_spec = pl.BlockSpec((span, rows_z, length), lambda i: (i, 0, 0))
    channels_spec = pl.BlockSpec((kinds, span, rows_z, length), lambda i: (0, i, 0, 0))
    phase_spec = pl.BlockSpec((2 * atoms, span * rows_z), lambda i: (0, i))
    chunks_spec = pl.BlockSpec((bands * places, planes, span, 128), lambda i: (0, 0, i, 0))
    chunk_shape = (bands * places, planes, rows_y, 128)
    smem_spec = pl.BlockSpec(memory_space=pltpu.SMEM)

    def exchange(chunks):
        return lax.all_to_all(
            chunks, ("band", "gy", "gz"), split_axis=0, concat_axis=0, tiled=True, axis_index_groups=groups
        )

    spread = pl.pallas_call(
        spread_kernel,
        grid=(steps,),
        in_specs=[orbitals_spec, mask_spec, smem_spec, whole(2 * length, 2 * length)],
        out_specs=chunks_spec,
        out_shape=jax.ShapeDtypeStruct(chunk_shape, bf16),
        scratch_shapes=[pltpu.VMEM((length * span, 128), f32)],
        compiler_params=params,
        cost_estimate=cost(4),
        name="spread",
    )(orbitals, cutoff_mask, occupations, inv_x)
    potential_part = lax.dynamic_slice_in_dim(potential, band * planes, planes, 0)

    spread, positions = lax.optimization_barrier((spread, positions))
    arrived = exchange(spread)

    cos_y, sin_y = axis_phase(positions[:, 1], frequencies(first_y, rows_y, length))
    cos_z, sin_z = axis_phase(positions[:, 2], frequencies(first_z, rows_z, length))
    cos_x, sin_x = axis_phase(positions[:, 0], frequencies(0, length, length))
    cos_yz = cos_y[:, :, None] * cos_z[:, None, :] - sin_y[:, :, None] * sin_z[:, None, :]
    sin_yz = sin_y[:, :, None] * cos_z[:, None, :] + cos_y[:, :, None] * sin_z[:, None, :]
    phase = jnp.concatenate([cos_yz, sin_yz], axis=0).astype(bf16).reshape(2 * atoms, rows_y * rows_z)
    wave = jnp.concatenate([cos_x, sin_x], axis=0)
    overlap = pl.pallas_call(
        overlap_kernel,
        grid=(steps,),
        in_specs=[orbitals_spec, mask_spec, channels_spec, phase_spec, whole(2 * atoms, length)],
        out_specs=whole(2 * atoms, 128),
        out_shape=jax.ShapeDtypeStruct((2 * atoms, 128), bf16),
        scratch_shapes=[pltpu.VMEM((2 * atoms, kinds * 4 * length), f32)],
        compiler_params=params,
        cost_estimate=cost(0.1),
        name="overlap",
    )(orbitals, cutoff_mask, channels, phase, wave)
    arrived, overlap = lax.optimization_barrier((arrived, overlap))

    rows = planes * rows_y
    half = planes // 2 * length
    mine, theirs, folded = pl.pallas_call(
        field_kernel,
        grid=(bands,),
        in_specs=[
            pl.BlockSpec((places, rows, 128), lambda i: (i, 0, 0)),
            whole(planes, length, length),
            whole(2 * atoms, 128),
            whole(4 * length, 4 * length),
            whole(2 * length, 2 * length),
            whole(4 * length, 4 * length),
            whole(2 * length, 2 * length),
        ],
        out_specs=[
            whole(half, length),
            whole(half, length),
            pl.BlockSpec((places, rows + 2 * atoms, 128), lambda i: (i, 0, 0)),
        ],
        out_shape=[
            jax.ShapeDtypeStruct((half, length), bf16),
            jax.ShapeDtypeStruct((half, length), bf16),
            jax.ShapeDtypeStruct((bands * places, rows + 2 * atoms, 128), bf16),
        ],
        scratch_shapes=[pltpu.VMEM((planes * length, length), f32)],
        compiler_params=params,
        cost_estimate=cost(6),
        name="field",
    )(arrived.reshape(bands * places, rows, 128), potential_part, overlap, inv_z, inv_y, fwd_z, fwd_y)
    folded, coupling = lax.optimization_barrier((folded, coupling))
    strength = pl.pallas_call(
        strength_kernel,
        in_specs=[smem_spec] * 3,
        out_shape=jax.ShapeDtypeStruct((atoms, 128), f32),
        compiler_params=params,
        cost_estimate=cost(10),
        name="strength",
    )(proj_atom, proj_chan, coupling)
    returned = exchange(folded)

    near = lax.ppermute(theirs, "band", partners("band", bands))
    mine = (mine.astype(f32) + near.astype(f32)).astype(bf16)
    got = lax.ppermute(mine, "band", partners("band", 2 * bands))
    mine = (mine.astype(f32) + got.astype(f32)).astype(bf16)
    far, near, both = [lax.ppermute(mine, "band", partners("band", d * bands)) for d in (6, 1, 7)]
    applied = pl.pallas_call(
        apply_kernel,
        grid=(steps,),
        in_specs=[
            pl.BlockSpec((bands * places, planes * span, 128), lambda i: (0, i, 0)),
            pl.BlockSpec((bands * places, 2 * atoms, 128), lambda i: (0, rows // (2 * atoms), 0)),
            orbitals_spec,
            mask_spec,
            channels_spec,
            phase_spec,
            whole(2 * atoms, length),
            whole(atoms, 128),
            smem_spec,
            whole(length, 4 * length),
        ],
        out_specs=orbitals_spec,
        out_shape=jax.ShapeDtypeStruct(orbitals.shape, bf16),
        scratch_shapes=[
            pltpu.VMEM((2 * atoms, kinds * 4 * length), bf16),
            pltpu.VMEM((length * span, 128), f32),
        ],
        compiler_params=params,
        cost_estimate=cost(4),
        name="apply",
    )(returned, returned, orbitals, cutoff_mask, channels, phase, wave, strength, occupations, fwd_x)
    far, near, both, applied = lax.optimization_barrier((far, near, both, applied))
    mine = (mine.astype(f32) + far.astype(f32)).astype(bf16)
    near = (near.astype(f32) + both.astype(f32)).astype(bf16)
    upper = lax.axis_index("band") // bands % 2
    mine = jnp.where(upper == 0, jnp.stack([mine, near]), jnp.stack([near, mine]))
    other = lax.ppermute(mine, "band", partners("band", 1))
    density = jnp.where(band == 0, jnp.stack([mine, other]), jnp.stack([other, mine]))
    return (applied, density.astype(f32).reshape(potential.shape))


def solution(mesh):
    placed = (
        P("band", "gy", "gz", None),
        P(("gy", "gz"), None, None),
        P("gy", "gz", None),
        P(None, "gy", "gz", None),
        P(),
        P(),
        P(),
        P(),
        P("band"),
    )
    return jax.shard_map(
        shards,
        mesh=mesh,
        in_specs=placed,
        out_specs=(P("band", "gy", "gz", None), P(("gy", "gz"), None, None)),
        check_vma=False,
    )
```

```python
import functools
import math

import jax
import jax.numpy as jnp
import ml_dtypes
import numpy as np
from jax import lax
from jax.experimental import pallas as pl
from jax.experimental.pallas import tpu as pltpu
from jax.sharding import PartitionSpec as P

kinetic_scale = 1.0 / 1024.0
vmem_bytes = 63 * 1024 * 1024
bf16 = jnp.bfloat16
f32 = jnp.float32


def dft_table(length, sign_value):
    grid_index = np.arange(length)
    product = grid_index[:, None] * grid_index[None, :] % length
    phase_angle = np.float32(2.0 * math.pi / length) * product.astype(np.float32)
    cosine_part = np.cos(phase_angle) / np.float32(math.sqrt(length))
    sine_part = sign_value * np.sin(phase_angle) / np.float32(math.sqrt(length))
    upper_rows = np.stack([cosine_part, -sine_part], axis=1)
    lower_rows = np.stack([sine_part, cosine_part], axis=1)
    return np.stack([upper_rows, lower_rows], axis=0).astype(np.float32)


def rounded(table, rows):
    return jnp.asarray(np.ascontiguousarray(table).reshape(rows, -1).astype(ml_dtypes.bfloat16))


def frequencies(first_index, span, length):
    grid_index = first_index + jnp.arange(span, dtype=jnp.int32)
    return jnp.where(grid_index >= length // 2, grid_index - length, grid_index).astype(f32)


def axis_phase(coordinate, freq):
    phase_angle = 2.0 * math.pi * (coordinate[:, None] * freq[None, :])
    return (jnp.cos(phase_angle), jnp.sin(phase_angle))


def dot(left, right):
    return jnp.dot(left, right, preferred_element_type=f32)


def dot_nt(left, right):
    return lax.dot_general(left, right, (((1,), (1,)), ((), ())), preferred_element_type=f32)


def dot_tn(left, right):
    return lax.dot_general(left, right, (((0,), (0,)), ((), ())), preferred_element_type=f32)


def root_weights(weight_ref, shape, axis, span):
    index = lax.broadcasted_iota(jnp.int32, shape, axis)
    return jnp.sqrt(jnp.where(index // span % 2 == 0, weight_ref[0], weight_ref[1]))


def spread_kernel(orbitals_ref, mask_ref, weight_ref, table_ref, out_ref, work_ref):
    rows_y, rows_z, length = mask_ref.shape
    mask = jnp.where(mask_ref[...] != 0, 1.0, 0.0).astype(bf16)
    mask = jnp.concatenate([mask, mask], axis=2)
    lane = lax.broadcasted_iota(jnp.int32, (length, 128), 1)
    roots = root_weights(weight_ref, (1, 128), 1, rows_z)
    spreads = []
    for pair in range(0, rows_y, 2):
        rows = []
        for y in (pair, pair + 1):
            both = jnp.concatenate([orbitals_ref[0, y] * mask[y], orbitals_ref[1, y] * mask[y]], axis=0)
            rows += [both, both]
        spreads.append(dot_nt(table_ref[...], jnp.concatenate(rows, axis=0)))
    for y in range(rows_y):
        spread = spreads[y // 2][:, y % 2 * 128 : y % 2 * 128 + 128]
        tile = jnp.where(lane < 64, spread[:length], spread[length:])
        work_ref[pl.ds(y, length, stride=rows_y), :] = tile * roots
    out_ref[...] = work_ref[...].reshape(out_ref.shape).astype(bf16)


def overlap_kernel(
    orbitals_ref, mask_ref, channels_ref, phase_ref, wave_ref, out_ref, profile_ref, sums_ref
):
    step = pl.program_id(0)
    rows = mask_ref.shape[0] * mask_ref.shape[1]
    length = mask_ref.shape[2]
    atoms = wave_ref.shape[0] // 2
    kinds = channels_ref.shape[0]
    mask = jnp.where(mask_ref[...] != 0, 1.0, 0.0).astype(bf16)
    orbs = [orbitals_ref[n].reshape(rows, 2 * length) for n in range(2)]
    columns = []
    profile_ref[kinds] = mask
    for c in range(kinds):
        profile_ref[c] = channels_ref[c] * mask
        radial = profile_ref[c].reshape(rows, length)
        radial = jnp.concatenate([radial, radial], axis=1)
        columns += [radial * orbs[0], radial * orbs[1]]
    part = dot(phase_ref[...], jnp.concatenate(columns, axis=1))

    @pl.when(step == 0)
    def first():
        sums_ref[...] = part

    @pl.when(step > 0)
    def later():
        sums_ref[...] += part

    @pl.when(step == pl.num_programs(0) - 1)
    def last():
        cos_x, sin_x = wave_ref[:atoms], wave_ref[atoms:]
        lane = lax.broadcasted_iota(jnp.int32, (atoms, 128), 1)
        total = jnp.zeros((atoms, 128), f32)
        for pair in range(kinds * 2):
            base = pair * 2 * length
            real_cols = slice(base, base + length)
            imag_cols = slice(base + length, base + 2 * length)
            real = sums_ref[:atoms, real_cols] - sums_ref[atoms:, imag_cols]
            imag = sums_ref[atoms:, real_cols] + sums_ref[:atoms, imag_cols]
            real_over = jnp.sum(real * cos_x - imag * sin_x, axis=1, keepdims=True)
            imag_over = jnp.sum(real * sin_x + imag * cos_x, axis=1, keepdims=True)
            total = jnp.where(lane == 2 * pair, real_over, total)
            total = jnp.where(lane == 2 * pair + 1, imag_over, total)
        high = total.astype(bf16).astype(f32)
        out_ref[...] = jnp.concatenate([high, total - high], axis=0).astype(bf16)


def field_kernel(
    arrived_ref,
    potential_ref,
    overlap_ref,
    inv_z_ref,
    inv_y_ref,
    fwd_z_ref,
    fwd_y_ref,
    mine_ref,
    theirs_ref,
    out_ref,
    sums_ref,
):
    step = pl.program_id(0)
    planes, length = potential_ref.shape[:2]
    parts = arrived_ref.shape[0] // 4
    rows = arrived_ref.shape[1] // planes
    columns = jnp.concatenate(
        [jnp.concatenate([arrived_ref[sy * 4 + sz] for sz in range(4)], axis=1) for sy in range(parts)],
        axis=0,
    )
    halfway = dot(columns, inv_z_ref[...]).astype(bf16)
    stacked = []
    for x in range(planes):
        first = [(sy * planes + x) * rows for sy in range(parts)]
        plane = jnp.concatenate([halfway[start : start + rows] for start in first], axis=0)
        real = jnp.concatenate([plane[:, 0:128], plane[:, 256:384]], axis=1)
        imag = jnp.concatenate([plane[:, 128:256], plane[:, 384:512]], axis=1)
        stacked.append(jnp.concatenate([real, imag], axis=0))
    fields = [dot(inv_y_ref[...], block) for block in stacked]
    scaled = []
    for x, field in enumerate(fields):
        real, imag = field[:length], field[length:]
        square = real * real + imag * imag
        density = square[:, :length] + square[:, length:]
        here = slice(x * length, (x + 1) * length)
        sums_ref[here, :] = jnp.where(step == 0, density, sums_ref[here, :] + density)
        potential = jnp.concatenate([potential_ref[x], potential_ref[x]], axis=1)
        potential = jnp.concatenate([potential, potential], axis=0)
        scaled.append((potential * field).astype(bf16))
    folded = [dot(fwd_y_ref[...], block).astype(bf16) for block in scaled]
    back = []
    for block in folded:
        real, imag = block[:length], block[length:]
        back.append(
            jnp.concatenate([real[:, :length], imag[:, :length], real[:, length:], imag[:, length:]], axis=1)
        )
    back = dot(jnp.concatenate(back, axis=0), fwd_z_ref[...]).astype(bf16)
    span = rows // 2
    for x in range(planes):
        for sy in range(parts):
            for half in range(2):
                start = x * length + sy * rows + half * span
                row = (half * planes + x) * span
                for sz in range(4):
                    out_ref[sy * 4 + sz, row : row + span, :] = back[
                        start : start + span, sz * 128 : sz * 128 + 128
                    ]
    for place in range(out_ref.shape[0]):
        out_ref[place, planes * rows :, :] = overlap_ref[...]

    @pl.when(step == pl.num_programs(0) - 1)
    def last():
        half = planes // 2 * length
        low, high = sums_ref[:half, :].astype(bf16), sums_ref[half:, :].astype(bf16)
        upper = lax.axis_index("band") // 2 % 2
        mine_ref[...] = jnp.where(upper == 0, low, high)
        theirs_ref[...] = jnp.where(upper == 0, high, low)


def apply_kernel(
    returned_ref,
    overlap_ref,
    orbitals_ref,
    profile_ref,
    phase_ref,
    wave_ref,
    strength_ref,
    weight_ref,
    table_ref,
    out_ref,
    factor_ref,
    work_ref,
):
    step = pl.program_id(0)
    kinds = profile_ref.shape[0] - 1
    grid_shape = profile_ref.shape[1:]
    rows_y, rows_z, length = grid_shape
    atoms = wave_ref.shape[0] // 2

    work_ref[...] = returned_ref[...].astype(f32).reshape(work_ref.shape)
    planes = [work_ref[pl.ds(y, length, stride=rows_y), :].astype(bf16) for y in range(rows_y)]
    local = [dot_tn(jnp.concatenate(planes[y : y + 2], axis=1), table_ref[...]) for y in range(0, rows_y, 2)]

    @pl.when(step == 0)
    def factors():
        cos_x, sin_x = wave_ref[:atoms], wave_ref[atoms:]
        sources = overlap_ref.shape[0] // 2
        even = jnp.sum(overlap_ref[:sources].astype(f32), axis=0)
        odd = jnp.sum(overlap_ref[sources:].astype(f32), axis=0)
        summed = jnp.where(lax.axis_index("band") % 2 == 0, even, odd)
        coef = (summed[:atoms] + summed[atoms:]) * strength_ref[...]
        for pair in range(kinds * 2):
            coef_real = coef[:, 2 * pair : 2 * pair + 1]
            coef_imag = coef[:, 2 * pair + 1 : 2 * pair + 2]
            real = cos_x * coef_real + sin_x * coef_imag
            imag = cos_x * coef_imag - sin_x * coef_real
            base = pair * 2 * length
            factor_ref[:, base : base + length] = jnp.concatenate([real, imag], axis=0).astype(bf16)
            factor_ref[:, base + length : base + 2 * length] = jnp.concatenate(
                [imag, -real], axis=0
            ).astype(bf16)

    extra = dot_tn(phase_ref[...], factor_ref[...])

    def squared(start, axis):
        index = start + lax.broadcasted_iota(jnp.int32, grid_shape, axis)
        wave = jnp.where(index >= length // 2, index - length, index)
        return wave * wave

    first_y = lax.axis_index("gy") * (rows_y * pl.num_programs(0)) + step * rows_y
    energy = squared(first_y, 0) + squared(lax.axis_index("gz") * rows_z, 1) + squared(0, 2)
    energy = kinetic_scale * 0.5 * energy.astype(f32)
    scale = 1.0 / root_weights(weight_ref, (2 * rows_z, 1), 0, rows_z)
    for y in range(rows_y):
        block = local[y // 2][y % 2 * 128 : y % 2 * 128 + 128]
        both = scale * (block[:64, : 2 * length] + block[64:, 2 * length :])
        radials = [profile_ref[c, y].astype(f32) for c in range(kinds + 1)]
        for n in range(2):
            for part in range(2):
                cols = slice(part * length, part * length + length)
                total = both[n * rows_z : (n + 1) * rows_z, cols]
                total = total + energy[y] * orbitals_ref[n, y, :, cols].astype(f32)
                total = total * radials[kinds]
                for c in range(kinds):
                    base = ((c * 2 + n) * 2 + part) * length
                    total = total + radials[c] * extra[y * rows_z : (y + 1) * rows_z, base : base + length]
                out_ref[n, y, :, cols] = total.astype(bf16)


def strength_kernel(atom_ref, kind_ref, coupling_ref, out_ref):
    row = lax.broadcasted_iota(jnp.int32, out_ref.shape, 0)
    kind = lax.broadcasted_iota(jnp.int32, out_ref.shape, 1) // 4
    total = jnp.zeros(out_ref.shape, f32)
    for p in range(coupling_ref.shape[0]):
        total += jnp.where((row == atom_ref[p]) & (kind == kind_ref[p]), coupling_ref[p], 0.0)
    out_ref[...] = total


def partners(axis, distance):
    return [(i, i ^ distance) for i in range(lax.axis_size(axis))]


def shards(
    orbitals,
    potential,
    cutoff_mask,
    channels,
    positions,
    proj_atom,
    proj_chan,
    coupling,
    occupations,
):
    rows_y, rows_z, length = cutoff_mask.shape
    parts_y = lax.axis_size("gy")
    parts_z = lax.axis_size("gz")
    parts_band = lax.axis_size("band")
    places = parts_y * parts_z
    bands = 2
    outer = parts_band // bands
    thin = length // places
    planes = thin // bands
    atoms = positions.shape[0]
    kinds = channels.shape[0]
    groups = [
        [(first * bands + b) * places + place for b in range(bands) for place in range(places)]
        for first in range(outer)
    ]
    inverse = dft_table(length, 1.0)
    forward = dft_table(length, -1.0)
    pick = np.eye(2, dtype=np.float32)
    split_inverse = inverse.reshape(2, length, 2, parts_z, rows_z)
    split_forward = forward.reshape(2, parts_z, rows_z, 2, length)
    order = np.arange(length).reshape(places, bands, planes).transpose(1, 0, 2).reshape(-1)
    inv_x = rounded(inverse[:, order], 2 * length)
    inv_y = rounded(inverse, 2 * length)
    inv_z = rounded(np.einsum("fzcsl,nm->scnlmfz", split_inverse, pick), 4 * length)
    fwd_z = rounded(np.einsum("cslfz,nm->nfzscml", split_forward, pick), 4 * length)
    fwd_y = rounded(forward, 2 * length)
    fwd_x = rounded(np.einsum("rkcx->xcrk", forward[..., order]), length)
    first_y = lax.axis_index("gy") * rows_y
    first_z = lax.axis_index("gz") * rows_z
    band = lax.axis_index("band") % bands

    params = pltpu.CompilerParams(vmem_limit_bytes=vmem_bytes)

    def cost(microseconds):
        return pl.CostEstimate(
            flops=int(microseconds * 1.0e9), bytes_accessed=int(microseconds * 1.0e6), transcendentals=0
        )

    steps = 2
    span = rows_y // steps
    whole = lambda *shape: pl.BlockSpec(shape, lambda i: (0,) * len(shape))
    orbitals_spec = pl.BlockSpec((2, span, rows_z, 2 * length), lambda i: (0, i, 0, 0))
    mask_spec = pl.BlockSpec((span, rows_z, length), lambda i: (i, 0, 0))
    channels_spec = pl.BlockSpec((kinds, span, rows_z, length), lambda i: (0, i, 0, 0))
    phase_spec = pl.BlockSpec((2 * atoms, span * rows_z), lambda i: (0, i))
    chunks_spec = pl.BlockSpec((bands * places, planes, span, 128), lambda i: (0, 0, i, 0))
    chunk_shape = (bands * places, planes, rows_y, 128)
    smem_spec = pl.BlockSpec(memory_space=pltpu.SMEM)

    def exchange(chunks):
        return lax.all_to_all(
            chunks, ("band", "gy", "gz"), split_axis=0, concat_axis=0, tiled=True, axis_index_groups=groups
        )

    spread = pl.pallas_call(
        spread_kernel,
        grid=(steps,),
        in_specs=[orbitals_spec, mask_spec, smem_spec, whole(2 * length, 2 * length)],
        out_specs=chunks_spec,
        out_shape=jax.ShapeDtypeStruct(chunk_shape, bf16),
        scratch_shapes=[pltpu.VMEM((length * span, 128), f32)],
        compiler_params=params,
        cost_estimate=cost(4),
        name="spread",
    )(orbitals, cutoff_mask, occupations, inv_x)
    potential_part = lax.dynamic_slice_in_dim(potential, band * planes, planes, 0)

    spread, positions = lax.optimization_barrier((spread, positions))
    arrived = exchange(spread)

    cos_y, sin_y = axis_phase(positions[:, 1], frequencies(first_y, rows_y, length))
    cos_z, sin_z = axis_phase(positions[:, 2], frequencies(first_z, rows_z, length))
    cos_x, sin_x = axis_phase(positions[:, 0], frequencies(0, length, length))
    cos_yz = cos_y[:, :, None] * cos_z[:, None, :] - sin_y[:, :, None] * sin_z[:, None, :]
    sin_yz = sin_y[:, :, None] * cos_z[:, None, :] + cos_y[:, :, None] * sin_z[:, None, :]
    phase = jnp.concatenate([cos_yz, sin_yz], axis=0).astype(bf16).reshape(2 * atoms, rows_y * rows_z)
    wave = jnp.concatenate([cos_x, sin_x], axis=0)
    positions, coupling = lax.optimization_barrier((positions, coupling))
    strength = pl.pallas_call(
        strength_kernel,
        in_specs=[smem_spec] * 3,
        out_shape=jax.ShapeDtypeStruct((atoms, 128), f32),
        compiler_params=params,
        cost_estimate=cost(0.1),
        name="strength",
    )(proj_atom, proj_chan, coupling)
    profile_spec = pl.BlockSpec((kinds + 1, span, rows_z, length), lambda i: (0, i, 0, 0))
    overlap, profile = pl.pallas_call(
        overlap_kernel,
        grid=(steps,),
        in_specs=[orbitals_spec, mask_spec, channels_spec, phase_spec, whole(2 * atoms, length)],
        out_specs=[whole(2 * atoms, 128), profile_spec],
        out_shape=[
            jax.ShapeDtypeStruct((2 * atoms, 128), bf16),
            jax.ShapeDtypeStruct((kinds + 1, rows_y, rows_z, length), bf16),
        ],
        scratch_shapes=[pltpu.VMEM((2 * atoms, kinds * 4 * length), f32)],
        compiler_params=params,
        cost_estimate=cost(0.1),
        name="overlap",
    )(orbitals, cutoff_mask, channels, phase, wave)
    arrived, overlap, strength = lax.optimization_barrier((arrived, overlap, strength))

    rows = planes * rows_y
    half = planes // 2 * length
    mine, theirs, folded = pl.pallas_call(
        field_kernel,
        grid=(bands,),
        in_specs=[
            pl.BlockSpec((places, rows, 128), lambda i: (i, 0, 0)),
            whole(planes, length, length),
            whole(2 * atoms, 128),
            whole(4 * length, 4 * length),
            whole(2 * length, 2 * length),
            whole(4 * length, 4 * length),
            whole(2 * length, 2 * length),
        ],
        out_specs=[
            whole(half, length),
            whole(half, length),
            pl.BlockSpec((places, rows + 2 * atoms, 128), lambda i: (i, 0, 0)),
        ],
        out_shape=[
            jax.ShapeDtypeStruct((half, length), bf16),
            jax.ShapeDtypeStruct((half, length), bf16),
            jax.ShapeDtypeStruct((bands * places, rows + 2 * atoms, 128), bf16),
        ],
        scratch_shapes=[pltpu.VMEM((planes * length, length), f32)],
        compiler_params=params,
        cost_estimate=cost(6),
        name="field",
    )(arrived.reshape(bands * places, rows, 128), potential_part, overlap, inv_z, inv_y, fwd_z, fwd_y)
    returned = exchange(folded)

    near = lax.ppermute(theirs, "band", partners("band", bands))
    mine = (mine.astype(f32) + near.astype(f32)).astype(bf16)
    got = lax.ppermute(mine, "band", partners("band", 2 * bands))
    mine = (mine.astype(f32) + got.astype(f32)).astype(bf16)
    far, near, both = [lax.ppermute(mine, "band", partners("band", d * bands)) for d in (6, 1, 7)]
    mine = (mine.astype(f32) + far.astype(f32)).astype(bf16)
    near = (near.astype(f32) + both.astype(f32)).astype(bf16)
    upper = lax.axis_index("band") // bands % 2
    mine = jnp.where(upper == 0, jnp.stack([mine, near]), jnp.stack([near, mine]))
    other = lax.ppermute(mine, "band", partners("band", 1))
    applied = pl.pallas_call(
        apply_kernel,
        grid=(steps,),
        in_specs=[
            pl.BlockSpec((bands * places, planes * span, 128), lambda i: (0, i, 0)),
            pl.BlockSpec((bands * places, 2 * atoms, 128), lambda i: (0, rows // (2 * atoms), 0)),
            orbitals_spec,
            profile_spec,
            phase_spec,
            whole(2 * atoms, length),
            whole(atoms, 128),
            smem_spec,
            whole(length, 4 * length),
        ],
        out_specs=orbitals_spec,
        out_shape=jax.ShapeDtypeStruct(orbitals.shape, bf16),
        scratch_shapes=[
            pltpu.VMEM((2 * atoms, kinds * 4 * length), bf16),
            pltpu.VMEM((length * span, 128), f32),
        ],
        compiler_params=pltpu.CompilerParams(vmem_limit_bytes=52224 * 1024),
        cost_estimate=cost(4),
        name="apply",
    )(returned, returned, orbitals, profile, phase, wave, strength, occupations, fwd_x)
    other, applied = lax.optimization_barrier((other, applied))
    density = jnp.where(band == 0, jnp.stack([mine, other]), jnp.stack([other, mine]))
    return (applied, density.astype(f32).reshape(potential.shape))


def solution(mesh):
    placed = (
        P("band", "gy", "gz", None),
        P(("gy", "gz"), None, None),
        P("gy", "gz", None),
        P(None, "gy", "gz", None),
        P(),
        P(),
        P(),
        P(),
        P("band"),
    )
    return jax.shard_map(
        shards,
        mesh=mesh,
        in_specs=placed,
        out_specs=(P("band", "gy", "gz", None), P(("gy", "gz"), None, None)),
        check_vma=False,
    )
```

```python
import functools
import math

import jax
import jax.numpy as jnp
import ml_dtypes
import numpy as np
from jax import lax
from jax.experimental import pallas as pl
from jax.experimental.pallas import tpu as pltpu
from jax.sharding import PartitionSpec as P

kinetic_scale = 1.0 / 1024.0
vmem_bytes = 63 * 1024 * 1024
bf16 = jnp.bfloat16
f32 = jnp.float32


def dft_table(length, sign_value):
    grid_index = np.arange(length)
    product = grid_index[:, None] * grid_index[None, :] % length
    phase_angle = np.float32(2.0 * math.pi / length) * product.astype(np.float32)
    cosine_part = np.cos(phase_angle) / np.float32(math.sqrt(length))
    sine_part = sign_value * np.sin(phase_angle) / np.float32(math.sqrt(length))
    upper_rows = np.stack([cosine_part, -sine_part], axis=1)
    lower_rows = np.stack([sine_part, cosine_part], axis=1)
    return np.stack([upper_rows, lower_rows], axis=0).astype(np.float32)


def rounded(table, rows):
    return jnp.asarray(np.ascontiguousarray(table).reshape(rows, -1).astype(ml_dtypes.bfloat16))


def frequencies(first_index, span, length):
    grid_index = first_index + jnp.arange(span, dtype=jnp.int32)
    return jnp.where(grid_index >= length // 2, grid_index - length, grid_index).astype(f32)


def axis_phase(coordinate, freq):
    phase_angle = 2.0 * math.pi * (coordinate[:, None] * freq[None, :])
    return (jnp.cos(phase_angle), jnp.sin(phase_angle))


def dot(left, right):
    return jnp.dot(left, right, preferred_element_type=f32)


def dot_nt(left, right):
    return lax.dot_general(left, right, (((1,), (1,)), ((), ())), preferred_element_type=f32)


def dot_tn(left, right):
    return lax.dot_general(left, right, (((0,), (0,)), ((), ())), preferred_element_type=f32)


def root_weights(weight_ref, shape, axis, span):
    index = lax.broadcasted_iota(jnp.int32, shape, axis)
    return jnp.sqrt(jnp.where(index // span % 2 == 0, weight_ref[0], weight_ref[1]))


def spread_kernel(orbitals_ref, mask_ref, weight_ref, table_ref, out_ref, work_ref):
    rows_y, rows_z, length = mask_ref.shape
    mask = jnp.where(mask_ref[...] != 0, 1.0, 0.0).astype(bf16)
    mask = jnp.concatenate([mask, mask], axis=2)
    lane = lax.broadcasted_iota(jnp.int32, (length, 128), 1)
    roots = root_weights(weight_ref, (1, 128), 1, rows_z)
    spreads = []
    for pair in range(0, rows_y, 2):
        rows = []
        for y in (pair, pair + 1):
            both = jnp.concatenate([orbitals_ref[0, y] * mask[y], orbitals_ref[1, y] * mask[y]], axis=0)
            rows += [both, both]
        spreads.append(dot_nt(table_ref[...], jnp.concatenate(rows, axis=0)))
    for y in range(rows_y):
        spread = spreads[y // 2][:, y % 2 * 128 : y % 2 * 128 + 128]
        tile = jnp.where(lane < 64, spread[:length], spread[length:])
        work_ref[pl.ds(y, length, stride=rows_y), :] = tile * roots
    out_ref[...] = work_ref[...].reshape(out_ref.shape).astype(bf16)


def overlap_kernel(
    orbitals_ref, mask_ref, channels_ref, phase_ref, wave_ref, out_ref, profile_ref, sums_ref
):
    step = pl.program_id(0)
    rows = mask_ref.shape[0] * mask_ref.shape[1]
    length = mask_ref.shape[2]
    atoms = wave_ref.shape[0] // 2
    kinds = channels_ref.shape[0]
    mask = jnp.where(mask_ref[...] != 0, 1.0, 0.0).astype(bf16)
    orbs = [orbitals_ref[n].reshape(rows, 2 * length) for n in range(2)]
    columns = []
    profile_ref[kinds] = mask
    for c in range(kinds):
        profile_ref[c] = channels_ref[c] * mask
        radial = profile_ref[c].reshape(rows, length)
        radial = jnp.concatenate([radial, radial], axis=1)
        columns += [radial * orbs[0], radial * orbs[1]]
    part = dot(phase_ref[...], jnp.concatenate(columns, axis=1))

    @pl.when(step == 0)
    def first():
        sums_ref[...] = part

    @pl.when(step > 0)
    def later():
        sums_ref[...] += part

    @pl.when(step == pl.num_programs(0) - 1)
    def last():
        cos_x, sin_x = wave_ref[:atoms], wave_ref[atoms:]
        lane = lax.broadcasted_iota(jnp.int32, (atoms, 128), 1)
        total = jnp.zeros((atoms, 128), f32)
        for pair in range(kinds * 2):
            base = pair * 2 * length
            real_cols = slice(base, base + length)
            imag_cols = slice(base + length, base + 2 * length)
            real = sums_ref[:atoms, real_cols] - sums_ref[atoms:, imag_cols]
            imag = sums_ref[atoms:, real_cols] + sums_ref[:atoms, imag_cols]
            real_over = jnp.sum(real * cos_x - imag * sin_x, axis=1, keepdims=True)
            imag_over = jnp.sum(real * sin_x + imag * cos_x, axis=1, keepdims=True)
            total = jnp.where(lane == 2 * pair, real_over, total)
            total = jnp.where(lane == 2 * pair + 1, imag_over, total)
        high = total.astype(bf16).astype(f32)
        out_ref[...] = jnp.concatenate([high, total - high], axis=0).astype(bf16)


def field_kernel(
    arrived_ref,
    potential_ref,
    overlap_ref,
    z_ref,
    inv_y_ref,
    fwd_y_ref,
    mine_ref,
    theirs_ref,
    out_ref,
    sums_ref,
):
    step = pl.program_id(0)
    planes, length = potential_ref.shape[:2]
    parts = arrived_ref.shape[0] // 4
    rows = arrived_ref.shape[1] // planes
    columns = jnp.concatenate(
        [jnp.concatenate([arrived_ref[sy * 4 + sz] for sz in range(4)], axis=1) for sy in range(parts)],
        axis=0,
    )
    halfway = dot(columns, z_ref[0]).astype(bf16)
    stacked = []
    for x in range(planes):
        first = [(sy * planes + x) * rows for sy in range(parts)]
        plane = jnp.concatenate([halfway[start : start + rows] for start in first], axis=0)
        real = jnp.concatenate([plane[:, 0:128], plane[:, 256:384]], axis=1)
        imag = jnp.concatenate([plane[:, 128:256], plane[:, 384:512]], axis=1)
        stacked.append(jnp.concatenate([real, imag], axis=0))
    fields = [dot(inv_y_ref[...], block) for block in stacked]
    scaled = []
    for x, field in enumerate(fields):
        real, imag = field[:length], field[length:]
        square = real * real + imag * imag
        density = square[:, :length] + square[:, length:]
        here = slice(x * length, (x + 1) * length)
        sums_ref[here, :] = jnp.where(step == 0, density, sums_ref[here, :] + density)
        potential = jnp.concatenate([potential_ref[x], potential_ref[x]], axis=1)
        potential = jnp.concatenate([potential, potential], axis=0)
        scaled.append((potential * field).astype(bf16))
    folded = [dot(fwd_y_ref[...], block).astype(bf16) for block in scaled]
    back = []
    for block in folded:
        real, imag = block[:length], block[length:]
        back.append(
            jnp.concatenate([real[:, :length], imag[:, :length], real[:, length:], imag[:, length:]], axis=1)
        )
    back = dot(jnp.concatenate(back, axis=0), z_ref[1]).astype(bf16)
    span = rows // 2
    for x in range(planes):
        for sy in range(parts):
            for half in range(2):
                start = x * length + sy * rows + half * span
                row = (half * planes + x) * span
                for sz in range(4):
                    out_ref[sy * 4 + sz, row : row + span, :] = back[
                        start : start + span, sz * 128 : sz * 128 + 128
                    ]
    for place in range(out_ref.shape[0]):
        out_ref[place, planes * rows :, :] = overlap_ref[...]

    @pl.when(step == pl.num_programs(0) - 1)
    def last():
        half = planes // 2 * length
        low, high = sums_ref[:half, :].astype(bf16), sums_ref[half:, :].astype(bf16)
        upper = lax.axis_index("band") // 2 % 2
        mine_ref[...] = jnp.where(upper == 0, low, high)
        theirs_ref[...] = jnp.where(upper == 0, high, low)


def apply_kernel(
    returned_ref,
    overlap_ref,
    orbitals_ref,
    profile_ref,
    phase_ref,
    wave_ref,
    strength_ref,
    weight_ref,
    table_ref,
    out_ref,
    factor_ref,
    work_ref,
):
    step = pl.program_id(0)
    kinds = profile_ref.shape[0] - 1
    grid_shape = profile_ref.shape[1:]
    rows_y, rows_z, length = grid_shape
    atoms = wave_ref.shape[0] // 2

    work_ref[...] = returned_ref[...].astype(f32).reshape(work_ref.shape)
    planes = [work_ref[pl.ds(y, length, stride=rows_y), :].astype(bf16) for y in range(rows_y)]
    local = [dot_tn(jnp.concatenate(planes[y : y + 2], axis=1), table_ref[...]) for y in range(0, rows_y, 2)]

    @pl.when(step == 0)
    def factors():
        cos_x, sin_x = wave_ref[:atoms], wave_ref[atoms:]
        sources = overlap_ref.shape[0] // 2
        even = jnp.sum(overlap_ref[:sources].astype(f32), axis=0)
        odd = jnp.sum(overlap_ref[sources:].astype(f32), axis=0)
        summed = jnp.where(lax.axis_index("band") % 2 == 0, even, odd)
        coef = (summed[:atoms] + summed[atoms:]) * strength_ref[...]
        for pair in range(kinds * 2):
            coef_real = coef[:, 2 * pair : 2 * pair + 1]
            coef_imag = coef[:, 2 * pair + 1 : 2 * pair + 2]
            real = cos_x * coef_real + sin_x * coef_imag
            imag = cos_x * coef_imag - sin_x * coef_real
            base = pair * 2 * length
            factor_ref[:, base : base + length] = jnp.concatenate([real, imag], axis=0).astype(bf16)
            factor_ref[:, base + length : base + 2 * length] = jnp.concatenate(
                [imag, -real], axis=0
            ).astype(bf16)

    extra = dot_tn(phase_ref[...], factor_ref[...])

    def squared(start, axis):
        index = start + lax.broadcasted_iota(jnp.int32, grid_shape, axis)
        wave = jnp.where(index >= length // 2, index - length, index)
        return wave * wave

    first_y = lax.axis_index("gy") * (rows_y * pl.num_programs(0)) + step * rows_y
    energy = squared(first_y, 0) + squared(lax.axis_index("gz") * rows_z, 1) + squared(0, 2)
    energy = kinetic_scale * 0.5 * energy.astype(f32)
    scale = 1.0 / root_weights(weight_ref, (2 * rows_z, 1), 0, rows_z)
    for y in range(rows_y):
        block = local[y // 2][y % 2 * 128 : y % 2 * 128 + 128]
        both = scale * (block[:64, : 2 * length] + block[64:, 2 * length :])
        radials = [profile_ref[c, y].astype(f32) for c in range(kinds + 1)]
        for n in range(2):
            for part in range(2):
                cols = slice(part * length, part * length + length)
                total = both[n * rows_z : (n + 1) * rows_z, cols]
                total = total + energy[y] * orbitals_ref[n, y, :, cols].astype(f32)
                total = total * radials[kinds]
                for c in range(kinds):
                    base = ((c * 2 + n) * 2 + part) * length
                    total = total + radials[c] * extra[y * rows_z : (y + 1) * rows_z, base : base + length]
                out_ref[n, y, :, cols] = total.astype(bf16)


def strength_kernel(atom_ref, kind_ref, coupling_ref, out_ref):
    row = lax.broadcasted_iota(jnp.int32, out_ref.shape, 0)
    kind = lax.broadcasted_iota(jnp.int32, out_ref.shape, 1) // 4
    total = jnp.zeros(out_ref.shape, f32)
    for p in range(coupling_ref.shape[0]):
        total += jnp.where((row == atom_ref[p]) & (kind == kind_ref[p]), coupling_ref[p], 0.0)
    out_ref[...] = total


def partners(axis, distance):
    return [(i, i ^ distance) for i in range(lax.axis_size(axis))]


def shards(
    orbitals,
    potential,
    cutoff_mask,
    channels,
    positions,
    proj_atom,
    proj_chan,
    coupling,
    occupations,
):
    rows_y, rows_z, length = cutoff_mask.shape
    parts_y = lax.axis_size("gy")
    parts_z = lax.axis_size("gz")
    parts_band = lax.axis_size("band")
    places = parts_y * parts_z
    bands = 2
    outer = parts_band // bands
    thin = length // places
    planes = thin // bands
    atoms = positions.shape[0]
    kinds = channels.shape[0]
    groups = [
        [(first * bands + b) * places + place for b in range(bands) for place in range(places)]
        for first in range(outer)
    ]
    inverse = dft_table(length, 1.0)
    forward = dft_table(length, -1.0)
    pick = np.eye(2, dtype=np.float32)
    split_inverse = inverse.reshape(2, length, 2, parts_z, rows_z)
    split_forward = forward.reshape(2, parts_z, rows_z, 2, length)
    order = np.arange(length).reshape(places, bands, planes).transpose(1, 0, 2).reshape(-1)
    inv_x = rounded(inverse[:, order], 2 * length)
    inv_y = rounded(inverse, 2 * length)
    inv_z = np.einsum("fzcsl,nm->scnlmfz", split_inverse, pick).reshape(4 * length, 4 * length)
    fwd_z = np.einsum("cslfz,nm->nfzscml", split_forward, pick).reshape(4 * length, 4 * length)
    both_z = rounded(np.stack([inv_z, fwd_z]), 8 * length).reshape(2, 4 * length, 4 * length)
    fwd_y = rounded(forward, 2 * length)
    fwd_x = rounded(np.einsum("rkcx->xcrk", forward[..., order]), length)
    first_y = lax.axis_index("gy") * rows_y
    first_z = lax.axis_index("gz") * rows_z
    band = lax.axis_index("band") % bands

    params = pltpu.CompilerParams(vmem_limit_bytes=vmem_bytes)

    def cost(microseconds):
        return pl.CostEstimate(
            flops=int(microseconds * 1.0e9), bytes_accessed=int(microseconds * 1.0e6), transcendentals=0
        )

    steps = 2
    span = rows_y // steps
    whole = lambda *shape: pl.BlockSpec(shape, lambda i: (0,) * len(shape))
    orbitals_spec = pl.BlockSpec((2, span, rows_z, 2 * length), lambda i: (0, i, 0, 0))
    mask_spec = pl.BlockSpec((span, rows_z, length), lambda i: (i, 0, 0))
    channels_spec = pl.BlockSpec((kinds, span, rows_z, length), lambda i: (0, i, 0, 0))
    phase_spec = pl.BlockSpec((2 * atoms, span * rows_z), lambda i: (0, i))
    chunks_spec = pl.BlockSpec((bands * places, planes, span, 128), lambda i: (0, 0, i, 0))
    chunk_shape = (bands * places, planes, rows_y, 128)
    smem_spec = pl.BlockSpec(memory_space=pltpu.SMEM)

    def exchange(chunks):
        return lax.all_to_all(
            chunks, ("band", "gy", "gz"), split_axis=0, concat_axis=0, tiled=True, axis_index_groups=groups
        )

    spread = pl.pallas_call(
        spread_kernel,
        grid=(steps,),
        in_specs=[orbitals_spec, mask_spec, smem_spec, whole(2 * length, 2 * length)],
        out_specs=chunks_spec,
        out_shape=jax.ShapeDtypeStruct(chunk_shape, bf16),
        scratch_shapes=[pltpu.VMEM((length * span, 128), f32)],
        compiler_params=params,
        cost_estimate=cost(4),
        name="spread",
    )(orbitals, cutoff_mask, occupations, inv_x)
    potential_part = lax.dynamic_slice_in_dim(potential, band * planes, planes, 0)

    spread, positions = lax.optimization_barrier((spread, positions))
    arrived = exchange(spread)

    cos_y, sin_y = axis_phase(positions[:, 1], frequencies(first_y, rows_y, length))
    cos_z, sin_z = axis_phase(positions[:, 2], frequencies(first_z, rows_z, length))
    cos_x, sin_x = axis_phase(positions[:, 0], frequencies(0, length, length))
    cos_yz = cos_y[:, :, None] * cos_z[:, None, :] - sin_y[:, :, None] * sin_z[:, None, :]
    sin_yz = sin_y[:, :, None] * cos_z[:, None, :] + cos_y[:, :, None] * sin_z[:, None, :]
    phase = jnp.concatenate([cos_yz, sin_yz], axis=0).astype(bf16).reshape(2 * atoms, rows_y * rows_z)
    wave = jnp.concatenate([cos_x, sin_x], axis=0)
    positions, coupling = lax.optimization_barrier((positions, coupling))
    strength = pl.pallas_call(
        strength_kernel,
        in_specs=[smem_spec] * 3,
        out_shape=jax.ShapeDtypeStruct((atoms, 128), f32),
        compiler_params=pltpu.CompilerParams(vmem_limit_bytes=16384 * 1024),
        cost_estimate=cost(0.1),
        name="strength",
    )(proj_atom, proj_chan, coupling)
    profile_spec = pl.BlockSpec((kinds + 1, span, rows_z, length), lambda i: (0, i, 0, 0))
    overlap, profile = pl.pallas_call(
        overlap_kernel,
        grid=(steps,),
        in_specs=[orbitals_spec, mask_spec, channels_spec, phase_spec, whole(2 * atoms, length)],
        out_specs=[whole(2 * atoms, 128), profile_spec],
        out_shape=[
            jax.ShapeDtypeStruct((2 * atoms, 128), bf16),
            jax.ShapeDtypeStruct((kinds + 1, rows_y, rows_z, length), bf16),
        ],
        scratch_shapes=[pltpu.VMEM((2 * atoms, kinds * 4 * length), f32)],
        compiler_params=pltpu.CompilerParams(vmem_limit_bytes=32768 * 1024),
        cost_estimate=cost(0.1),
        name="overlap",
    )(orbitals, cutoff_mask, channels, phase, wave)
    arrived, overlap, strength = lax.optimization_barrier((arrived, overlap, strength))

    rows = planes * rows_y
    half = planes // 2 * length
    mine, theirs, folded = pl.pallas_call(
        field_kernel,
        grid=(bands,),
        in_specs=[
            pl.BlockSpec((places, rows, 128), lambda i: (i, 0, 0)),
            whole(planes, length, length),
            whole(2 * atoms, 128),
            whole(2, 4 * length, 4 * length),
            whole(2 * length, 2 * length),
            whole(2 * length, 2 * length),
        ],
        out_specs=[
            whole(half, length),
            whole(half, length),
            pl.BlockSpec((places, rows + 2 * atoms, 128), lambda i: (i, 0, 0)),
        ],
        out_shape=[
            jax.ShapeDtypeStruct((half, length), bf16),
            jax.ShapeDtypeStruct((half, length), bf16),
            jax.ShapeDtypeStruct((bands * places, rows + 2 * atoms, 128), bf16),
        ],
        scratch_shapes=[pltpu.VMEM((planes * length, length), f32)],
        compiler_params=pltpu.CompilerParams(vmem_limit_bytes=53248 * 1024),
        cost_estimate=cost(6),
        name="field",
    )(arrived.reshape(bands * places, rows, 128), potential_part, overlap, both_z, inv_y, fwd_y)
    returned = exchange(folded)

    near = lax.ppermute(theirs, "band", partners("band", bands))
    mine = (mine.astype(f32) + near.astype(f32)).astype(bf16)
    got = lax.ppermute(mine, "band", partners("band", 2 * bands))
    mine = (mine.astype(f32) + got.astype(f32)).astype(bf16)
    far, near, both = [lax.ppermute(mine, "band", partners("band", d * bands)) for d in (6, 1, 7)]
    mine = (mine.astype(f32) + far.astype(f32)).astype(bf16)
    near = (near.astype(f32) + both.astype(f32)).astype(bf16)
    upper = lax.axis_index("band") // bands % 2
    mine = jnp.where(upper == 0, jnp.stack([mine, near]), jnp.stack([near, mine]))
    other = lax.ppermute(mine, "band", partners("band", 1))
    applied = pl.pallas_call(
        apply_kernel,
        grid=(steps,),
        in_specs=[
            pl.BlockSpec((bands * places, planes * span, 128), lambda i: (0, i, 0)),
            pl.BlockSpec((bands * places, 2 * atoms, 128), lambda i: (0, rows // (2 * atoms), 0)),
            orbitals_spec,
            profile_spec,
            phase_spec,
            whole(2 * atoms, length),
            whole(atoms, 128),
            smem_spec,
            whole(length, 4 * length),
        ],
        out_specs=orbitals_spec,
        out_shape=jax.ShapeDtypeStruct(orbitals.shape, bf16),
        scratch_shapes=[
            pltpu.VMEM((2 * atoms, kinds * 4 * length), bf16),
            pltpu.VMEM((length * span, 128), f32),
        ],
        compiler_params=pltpu.CompilerParams(vmem_limit_bytes=52224 * 1024),
        cost_estimate=cost(4),
        name="apply",
    )(returned, returned, orbitals, profile, phase, wave, strength, occupations, fwd_x)
    other, applied = lax.optimization_barrier((other, applied))
    density = jnp.where(band == 0, jnp.stack([mine, other]), jnp.stack([other, mine]))
    return (applied, density.astype(f32).reshape(potential.shape))


def solution(mesh):
    placed = (
        P("band", "gy", "gz", None),
        P(("gy", "gz"), None, None),
        P("gy", "gz", None),
        P(None, "gy", "gz", None),
        P(),
        P(),
        P(),
        P(),
        P("band"),
    )
    return jax.shard_map(
        shards,
        mesh=mesh,
        in_specs=placed,
        out_specs=(P("band", "gy", "gz", None), P(("gy", "gz"), None, None)),
        check_vma=False,
    )
```

```python
import functools
import math

import jax
import jax.numpy as jnp
import ml_dtypes
import numpy as np
from jax import lax
from jax.experimental import pallas as pl
from jax.experimental.pallas import tpu as pltpu
from jax.sharding import PartitionSpec as P

kinetic_scale = 1.0 / 1024.0
vmem_bytes = 63 * 1024 * 1024
bf16 = jnp.bfloat16
f32 = jnp.float32


def dft_table(length, sign_value):
    grid_index = np.arange(length)
    product = grid_index[:, None] * grid_index[None, :] % length
    phase_angle = np.float32(2.0 * math.pi / length) * product.astype(np.float32)
    cosine_part = np.cos(phase_angle) / np.float32(math.sqrt(length))
    sine_part = sign_value * np.sin(phase_angle) / np.float32(math.sqrt(length))
    upper_rows = np.stack([cosine_part, -sine_part], axis=1)
    lower_rows = np.stack([sine_part, cosine_part], axis=1)
    return np.stack([upper_rows, lower_rows], axis=0).astype(np.float32)


def rounded(table, rows):
    return jnp.asarray(np.ascontiguousarray(table).reshape(rows, -1).astype(ml_dtypes.bfloat16))


def frequencies(first_index, span, length):
    grid_index = first_index + jnp.arange(span, dtype=jnp.int32)
    return jnp.where(grid_index >= length // 2, grid_index - length, grid_index).astype(f32)


def axis_phase(coordinate, freq):
    phase_angle = 2.0 * math.pi * (coordinate[:, None] * freq[None, :])
    return (jnp.cos(phase_angle), jnp.sin(phase_angle))


def dot(left, right):
    return jnp.dot(left, right, preferred_element_type=f32)


def dot_nt(left, right):
    return lax.dot_general(left, right, (((1,), (1,)), ((), ())), preferred_element_type=f32)


def dot_tn(left, right):
    return lax.dot_general(left, right, (((0,), (0,)), ((), ())), preferred_element_type=f32)


def root_weights(weight_ref, shape, axis, span):
    index = lax.broadcasted_iota(jnp.int32, shape, axis)
    return jnp.sqrt(jnp.where(index // span % 2 == 0, weight_ref[0], weight_ref[1]))


def spread_kernel(orbitals_ref, mask_ref, weight_ref, table_ref, out_ref, work_ref):
    rows_y, rows_z, length = mask_ref.shape
    mask = jnp.where(mask_ref[...] != 0, 1.0, 0.0).astype(bf16)
    mask = jnp.concatenate([mask, mask], axis=2)
    lane = lax.broadcasted_iota(jnp.int32, (length, 128), 1)
    roots = root_weights(weight_ref, (1, 128), 1, rows_z)
    spreads = []
    for pair in range(0, rows_y, 2):
        rows = []
        for y in (pair, pair + 1):
            both = jnp.concatenate([orbitals_ref[0, y] * mask[y], orbitals_ref[1, y] * mask[y]], axis=0)
            rows += [both, both]
        spreads.append(dot_nt(table_ref[...], jnp.concatenate(rows, axis=0)))
    for y in range(rows_y):
        spread = spreads[y // 2][:, y % 2 * 128 : y % 2 * 128 + 128]
        tile = jnp.where(lane < 64, spread[:length], spread[length:])
        work_ref[pl.ds(y, length, stride=rows_y), :] = tile * roots
    out_ref[...] = work_ref[...].reshape(out_ref.shape).astype(bf16)


def overlap_kernel(
    orbitals_ref, mask_ref, channels_ref, phase_ref, wave_ref, out_ref, profile_ref, sums_ref
):
    step = pl.program_id(0)
    rows = mask_ref.shape[0] * mask_ref.shape[1]
    length = mask_ref.shape[2]
    atoms = wave_ref.shape[0] // 2
    kinds = channels_ref.shape[0]
    mask = jnp.where(mask_ref[...] != 0, 1.0, 0.0).astype(bf16)
    orbs = [orbitals_ref[n].reshape(rows, 2 * length) for n in range(2)]
    columns = []
    profile_ref[kinds] = mask
    for c in range(kinds):
        profile_ref[c] = channels_ref[c] * mask
        radial = profile_ref[c].reshape(rows, length)
        radial = jnp.concatenate([radial, radial], axis=1)
        columns += [radial * orbs[0], radial * orbs[1]]
    part = dot(phase_ref[...], jnp.concatenate(columns, axis=1))

    @pl.when(step == 0)
    def first():
        sums_ref[...] = part

    @pl.when(step > 0)
    def later():
        sums_ref[...] += part

    @pl.when(step == pl.num_programs(0) - 1)
    def last():
        cos_x, sin_x = wave_ref[:atoms], wave_ref[atoms:]
        lane = lax.broadcasted_iota(jnp.int32, (atoms, 128), 1)
        total = jnp.zeros((atoms, 128), f32)
        for pair in range(kinds * 2):
            base = pair * 2 * length
            real_cols = slice(base, base + length)
            imag_cols = slice(base + length, base + 2 * length)
            real = sums_ref[:atoms, real_cols] - sums_ref[atoms:, imag_cols]
            imag = sums_ref[atoms:, real_cols] + sums_ref[:atoms, imag_cols]
            real_over = jnp.sum(real * cos_x - imag * sin_x, axis=1, keepdims=True)
            imag_over = jnp.sum(real * sin_x + imag * cos_x, axis=1, keepdims=True)
            total = jnp.where(lane == 2 * pair, real_over, total)
            total = jnp.where(lane == 2 * pair + 1, imag_over, total)
        high = total.astype(bf16).astype(f32)
        out_ref[...] = jnp.concatenate([high, total - high], axis=0).astype(bf16)


def field_kernel(
    arrived_ref,
    potential_ref,
    overlap_ref,
    z_ref,
    inv_y_ref,
    fwd_y_ref,
    mine_ref,
    theirs_ref,
    out_ref,
):
    planes, length = potential_ref.shape[:2]
    parts = 4
    places = 4 * parts
    bands = arrived_ref.shape[0] // places
    rows = arrived_ref.shape[1] // planes
    span = rows // 2
    halfway = []
    for b in range(bands):
        columns = jnp.concatenate(
            [
                jnp.concatenate([arrived_ref[b * places + sy * 4 + sz] for sz in range(4)], axis=1)
                for sy in range(parts)
            ],
            axis=0,
        )
        halfway.append(dot(columns, z_ref[0]).astype(bf16))
    fields = []
    for b in range(bands):
        for x in range(planes):
            first = [(sy * planes + x) * rows for sy in range(parts)]
            plane = jnp.concatenate([halfway[b][start : start + rows] for start in first], axis=0)
            real = jnp.concatenate([plane[:, 0:128], plane[:, 256:384]], axis=1)
            imag = jnp.concatenate([plane[:, 128:256], plane[:, 384:512]], axis=1)
            fields.append(dot(inv_y_ref[...], jnp.concatenate([real, imag], axis=0)))
    density = []
    scaled = []
    for x in range(planes):
        square = [fields[b * planes + x] * fields[b * planes + x] for b in range(bands)]
        square = sum(s[:length] + s[length:] for s in square)
        density.append((square[:, :length] + square[:, length:]).astype(bf16))
    for b in range(bands):
        for x in range(planes):
            potential = jnp.concatenate([potential_ref[x], potential_ref[x]], axis=1)
            potential = jnp.concatenate([potential, potential], axis=0)
            scaled.append((potential * fields[b * planes + x]).astype(bf16))
    folded = [dot(fwd_y_ref[...], block).astype(bf16) for block in scaled]
    for b in range(bands):
        back = []
        for block in folded[b * planes : (b + 1) * planes]:
            real, imag = block[:length], block[length:]
            back.append(
                jnp.concatenate([real[:, :length], imag[:, :length], real[:, length:], imag[:, length:]], axis=1)
            )
        back = dot(jnp.concatenate(back, axis=0), z_ref[1]).astype(bf16)
        for x in range(planes):
            for sy in range(parts):
                for half in range(2):
                    start = x * length + sy * rows + half * span
                    row = (half * planes + x) * span
                    for sz in range(4):
                        out_ref[b * places + sy * 4 + sz, row : row + span, :] = back[
                            start : start + span, sz * 128 : sz * 128 + 128
                        ]
    for place in range(out_ref.shape[0]):
        out_ref[place, planes * rows :, :] = overlap_ref[...]
    upper = lax.axis_index("band") // 2 % 2
    half = planes // 2
    for x in range(half):
        here = slice(x * length, (x + 1) * length)
        mine_ref[here, :] = jnp.where(upper == 0, density[x], density[half + x])
        theirs_ref[here, :] = jnp.where(upper == 0, density[half + x], density[x])


def apply_kernel(
    returned_ref,
    overlap_ref,
    orbitals_ref,
    profile_ref,
    phase_ref,
    wave_ref,
    strength_ref,
    weight_ref,
    table_ref,
    out_ref,
    factor_ref,
    work_ref,
):
    step = pl.program_id(0)
    kinds = profile_ref.shape[0] - 1
    grid_shape = profile_ref.shape[1:]
    rows_y, rows_z, length = grid_shape
    atoms = wave_ref.shape[0] // 2

    work_ref[...] = returned_ref[...].astype(f32).reshape(work_ref.shape)
    planes = [work_ref[pl.ds(y, length, stride=rows_y), :].astype(bf16) for y in range(rows_y)]
    local = [dot_tn(jnp.concatenate(planes[y : y + 2], axis=1), table_ref[...]) for y in range(0, rows_y, 2)]

    @pl.when(step == 0)
    def factors():
        cos_x, sin_x = wave_ref[:atoms], wave_ref[atoms:]
        sources = overlap_ref.shape[0] // 2
        even = jnp.sum(overlap_ref[:sources].astype(f32), axis=0)
        odd = jnp.sum(overlap_ref[sources:].astype(f32), axis=0)
        summed = jnp.where(lax.axis_index("band") % 2 == 0, even, odd)
        coef = (summed[:atoms] + summed[atoms:]) * strength_ref[...]
        for pair in range(kinds * 2):
            coef_real = coef[:, 2 * pair : 2 * pair + 1]
            coef_imag = coef[:, 2 * pair + 1 : 2 * pair + 2]
            real = cos_x * coef_real + sin_x * coef_imag
            imag = cos_x * coef_imag - sin_x * coef_real
            base = pair * 2 * length
            factor_ref[:, base : base + length] = jnp.concatenate([real, imag], axis=0).astype(bf16)
            factor_ref[:, base + length : base + 2 * length] = jnp.concatenate(
                [imag, -real], axis=0
            ).astype(bf16)

    extra = dot_tn(phase_ref[...], factor_ref[...])

    def squared(start, axis):
        index = start + lax.broadcasted_iota(jnp.int32, grid_shape, axis)
        wave = jnp.where(index >= length // 2, index - length, index)
        return wave * wave

    first_y = lax.axis_index("gy") * (rows_y * pl.num_programs(0)) + step * rows_y
    energy = squared(first_y, 0) + squared(lax.axis_index("gz") * rows_z, 1) + squared(0, 2)
    energy = kinetic_scale * 0.5 * energy.astype(f32)
    scale = 1.0 / root_weights(weight_ref, (2 * rows_z, 1), 0, rows_z)
    for y in range(rows_y):
        block = local[y // 2][y % 2 * 128 : y % 2 * 128 + 128]
        both = scale * (block[:64, : 2 * length] + block[64:, 2 * length :])
        radials = [profile_ref[c, y].astype(f32) for c in range(kinds + 1)]
        for n in range(2):
            for part in range(2):
                cols = slice(part * length, part * length + length)
                total = both[n * rows_z : (n + 1) * rows_z, cols]
                total = total + energy[y] * orbitals_ref[n, y, :, cols].astype(f32)
                total = total * radials[kinds]
                for c in range(kinds):
                    base = ((c * 2 + n) * 2 + part) * length
                    total = total + radials[c] * extra[y * rows_z : (y + 1) * rows_z, base : base + length]
                out_ref[n, y, :, cols] = total.astype(bf16)


def strength_kernel(atom_ref, kind_ref, coupling_ref, out_ref):
    row = lax.broadcasted_iota(jnp.int32, out_ref.shape, 0)
    kind = lax.broadcasted_iota(jnp.int32, out_ref.shape, 1) // 4
    total = jnp.zeros(out_ref.shape, f32)
    for p in range(coupling_ref.shape[0]):
        total += jnp.where((row == atom_ref[p]) & (kind == kind_ref[p]), coupling_ref[p], 0.0)
    out_ref[...] = total


def partners(axis, distance):
    return [(i, i ^ distance) for i in range(lax.axis_size(axis))]


def shards(
    orbitals,
    potential,
    cutoff_mask,
    channels,
    positions,
    proj_atom,
    proj_chan,
    coupling,
    occupations,
):
    rows_y, rows_z, length = cutoff_mask.shape
    parts_y = lax.axis_size("gy")
    parts_z = lax.axis_size("gz")
    parts_band = lax.axis_size("band")
    places = parts_y * parts_z
    bands = 2
    outer = parts_band // bands
    thin = length // places
    planes = thin // bands
    atoms = positions.shape[0]
    kinds = channels.shape[0]
    groups = [
        [(first * bands + b) * places + place for b in range(bands) for place in range(places)]
        for first in range(outer)
    ]
    inverse = dft_table(length, 1.0)
    forward = dft_table(length, -1.0)
    pick = np.eye(2, dtype=np.float32)
    split_inverse = inverse.reshape(2, length, 2, parts_z, rows_z)
    split_forward = forward.reshape(2, parts_z, rows_z, 2, length)
    order = np.arange(length).reshape(places, bands, planes).transpose(1, 0, 2).reshape(-1)
    inv_x = rounded(inverse[:, order], 2 * length)
    inv_y = rounded(inverse, 2 * length)
    inv_z = np.einsum("fzcsl,nm->scnlmfz", split_inverse, pick).reshape(4 * length, 4 * length)
    fwd_z = np.einsum("cslfz,nm->nfzscml", split_forward, pick).reshape(4 * length, 4 * length)
    both_z = rounded(np.stack([inv_z, fwd_z]), 8 * length).reshape(2, 4 * length, 4 * length)
    fwd_y = rounded(forward, 2 * length)
    fwd_x = rounded(np.einsum("rkcx->xcrk", forward[..., order]), length)
    first_y = lax.axis_index("gy") * rows_y
    first_z = lax.axis_index("gz") * rows_z
    band = lax.axis_index("band") % bands

    params = pltpu.CompilerParams(vmem_limit_bytes=vmem_bytes)

    def cost(microseconds):
        return pl.CostEstimate(
            flops=int(microseconds * 1.0e9), bytes_accessed=int(microseconds * 1.0e6), transcendentals=0
        )

    steps = 2
    span = rows_y // steps
    whole = lambda *shape: pl.BlockSpec(shape, lambda i: (0,) * len(shape))
    orbitals_spec = pl.BlockSpec((2, span, rows_z, 2 * length), lambda i: (0, i, 0, 0))
    mask_spec = pl.BlockSpec((span, rows_z, length), lambda i: (i, 0, 0))
    channels_spec = pl.BlockSpec((kinds, span, rows_z, length), lambda i: (0, i, 0, 0))
    phase_spec = pl.BlockSpec((2 * atoms, span * rows_z), lambda i: (0, i))
    chunks_spec = pl.BlockSpec((bands * places, planes, span, 128), lambda i: (0, 0, i, 0))
    chunk_shape = (bands * places, planes, rows_y, 128)
    smem_spec = pl.BlockSpec(memory_space=pltpu.SMEM)

    def exchange(chunks):
        return lax.all_to_all(
            chunks, ("band", "gy", "gz"), split_axis=0, concat_axis=0, tiled=True, axis_index_groups=groups
        )

    spread = pl.pallas_call(
        spread_kernel,
        grid=(steps,),
        in_specs=[orbitals_spec, mask_spec, smem_spec, whole(2 * length, 2 * length)],
        out_specs=chunks_spec,
        out_shape=jax.ShapeDtypeStruct(chunk_shape, bf16),
        scratch_shapes=[pltpu.VMEM((length * span, 128), f32)],
        compiler_params=params,
        cost_estimate=cost(4),
        name="spread",
    )(orbitals, cutoff_mask, occupations, inv_x)
    potential_part = lax.dynamic_slice_in_dim(potential, band * planes, planes, 0)

    spread, positions = lax.optimization_barrier((spread, positions))
    arrived = exchange(spread)

    cos_y, sin_y = axis_phase(positions[:, 1], frequencies(first_y, rows_y, length))
    cos_z, sin_z = axis_phase(positions[:, 2], frequencies(first_z, rows_z, length))
    cos_x, sin_x = axis_phase(positions[:, 0], frequencies(0, length, length))
    cos_yz = cos_y[:, :, None] * cos_z[:, None, :] - sin_y[:, :, None] * sin_z[:, None, :]
    sin_yz = sin_y[:, :, None] * cos_z[:, None, :] + cos_y[:, :, None] * sin_z[:, None, :]
    phase = jnp.concatenate([cos_yz, sin_yz], axis=0).astype(bf16).reshape(2 * atoms, rows_y * rows_z)
    wave = jnp.concatenate([cos_x, sin_x], axis=0)
    positions, coupling = lax.optimization_barrier((positions, coupling))
    strength = pl.pallas_call(
        strength_kernel,
        in_specs=[smem_spec] * 3,
        out_shape=jax.ShapeDtypeStruct((atoms, 128), f32),
        compiler_params=pltpu.CompilerParams(vmem_limit_bytes=16384 * 1024),
        cost_estimate=cost(0.1),
        name="strength",
    )(proj_atom, proj_chan, coupling)
    profile_spec = pl.BlockSpec((kinds + 1, span, rows_z, length), lambda i: (0, i, 0, 0))
    overlap, profile = pl.pallas_call(
        overlap_kernel,
        grid=(steps,),
        in_specs=[orbitals_spec, mask_spec, channels_spec, phase_spec, whole(2 * atoms, length)],
        out_specs=[whole(2 * atoms, 128), profile_spec],
        out_shape=[
            jax.ShapeDtypeStruct((2 * atoms, 128), bf16),
            jax.ShapeDtypeStruct((kinds + 1, rows_y, rows_z, length), bf16),
        ],
        scratch_shapes=[pltpu.VMEM((2 * atoms, kinds * 4 * length), f32)],
        compiler_params=pltpu.CompilerParams(vmem_limit_bytes=32768 * 1024),
        cost_estimate=cost(0.1),
        name="overlap",
    )(orbitals, cutoff_mask, channels, phase, wave)
    arrived, overlap, strength = lax.optimization_barrier((arrived, overlap, strength))

    rows = planes * rows_y
    half = planes // 2 * length
    mine, theirs, folded = pl.pallas_call(
        field_kernel,
        grid=(1,),
        in_specs=[
            whole(bands * places, rows, 128),
            whole(planes, length, length),
            whole(2 * atoms, 128),
            whole(2, 4 * length, 4 * length),
            whole(2 * length, 2 * length),
            whole(2 * length, 2 * length),
        ],
        out_specs=[
            whole(half, length),
            whole(half, length),
            whole(bands * places, rows + 2 * atoms, 128),
        ],
        out_shape=[
            jax.ShapeDtypeStruct((half, length), bf16),
            jax.ShapeDtypeStruct((half, length), bf16),
            jax.ShapeDtypeStruct((bands * places, rows + 2 * atoms, 128), bf16),
        ],
        compiler_params=pltpu.CompilerParams(vmem_limit_bytes=53248 * 1024),
        cost_estimate=cost(6),
        name="field",
    )(arrived.reshape(bands * places, rows, 128), potential_part, overlap, both_z, inv_y, fwd_y)
    returned = exchange(folded)

    near = lax.ppermute(theirs, "band", partners("band", bands))
    mine = (mine.astype(f32) + near.astype(f32)).astype(bf16)
    got = lax.ppermute(mine, "band", partners("band", 2 * bands))
    mine = (mine.astype(f32) + got.astype(f32)).astype(bf16)
    far, near, both = [lax.ppermute(mine, "band", partners("band", d * bands)) for d in (6, 1, 7)]
    mine = (mine.astype(f32) + far.astype(f32)).astype(bf16)
    near = (near.astype(f32) + both.astype(f32)).astype(bf16)
    upper = lax.axis_index("band") // bands % 2
    mine = jnp.where(upper == 0, jnp.stack([mine, near]), jnp.stack([near, mine]))
    other = lax.ppermute(mine, "band", partners("band", 1))
    applied = pl.pallas_call(
        apply_kernel,
        grid=(steps,),
        in_specs=[
            pl.BlockSpec((bands * places, planes * span, 128), lambda i: (0, i, 0)),
            pl.BlockSpec((bands * places, 2 * atoms, 128), lambda i: (0, rows // (2 * atoms), 0)),
            orbitals_spec,
            profile_spec,
            phase_spec,
            whole(2 * atoms, length),
            whole(atoms, 128),
            smem_spec,
            whole(length, 4 * length),
        ],
        out_specs=orbitals_spec,
        out_shape=jax.ShapeDtypeStruct(orbitals.shape, bf16),
        scratch_shapes=[
            pltpu.VMEM((2 * atoms, kinds * 4 * length), bf16),
            pltpu.VMEM((length * span, 128), f32),
        ],
        compiler_params=pltpu.CompilerParams(vmem_limit_bytes=52224 * 1024),
        cost_estimate=cost(4),
        name="apply",
    )(returned, returned, orbitals, profile, phase, wave, strength, occupations, fwd_x)
    other, applied = lax.optimization_barrier((other, applied))
    density = jnp.where(band == 0, jnp.stack([mine, other]), jnp.stack([other, mine]))
    return (applied, density.astype(f32).reshape(potential.shape))


def solution(mesh):
    placed = (
        P("band", "gy", "gz", None),
        P(("gy", "gz"), None, None),
        P("gy", "gz", None),
        P(None, "gy", "gz", None),
        P(),
        P(),
        P(),
        P(),
        P("band"),
    )
    return jax.shard_map(
        shards,
        mesh=mesh,
        in_specs=placed,
        out_specs=(P("band", "gy", "gz", None), P(("gy", "gz"), None, None)),
        check_vma=False,
    )
```

```python
import functools
import math

import jax
import jax.numpy as jnp
import ml_dtypes
import numpy as np
from jax import lax
from jax.experimental import pallas as pl
from jax.experimental.pallas import tpu as pltpu
from jax.sharding import PartitionSpec as P

kinetic_scale = 1.0 / 1024.0
vmem_bytes = 63 * 1024 * 1024
bf16 = jnp.bfloat16
f32 = jnp.float32


def dft_table(length, sign_value):
    grid_index = np.arange(length)
    product = grid_index[:, None] * grid_index[None, :] % length
    phase_angle = np.float32(2.0 * math.pi / length) * product.astype(np.float32)
    cosine_part = np.cos(phase_angle) / np.float32(math.sqrt(length))
    sine_part = sign_value * np.sin(phase_angle) / np.float32(math.sqrt(length))
    upper_rows = np.stack([cosine_part, -sine_part], axis=1)
    lower_rows = np.stack([sine_part, cosine_part], axis=1)
    return np.stack([upper_rows, lower_rows], axis=0).astype(np.float32)


def rounded(table, rows):
    return jnp.asarray(np.ascontiguousarray(table).reshape(rows, -1).astype(ml_dtypes.bfloat16))


def frequencies(first_index, span, length):
    grid_index = first_index + jnp.arange(span, dtype=jnp.int32)
    return jnp.where(grid_index >= length // 2, grid_index - length, grid_index).astype(f32)


def axis_phase(coordinate, freq):
    phase_angle = 2.0 * math.pi * (coordinate[:, None] * freq[None, :])
    return (jnp.cos(phase_angle), jnp.sin(phase_angle))


def dot(left, right):
    return jnp.dot(left, right, preferred_element_type=f32)


def dot_nt(left, right):
    return lax.dot_general(left, right, (((1,), (1,)), ((), ())), preferred_element_type=f32)


def dot_tn(left, right):
    return lax.dot_general(left, right, (((0,), (0,)), ((), ())), preferred_element_type=f32)


def root_weights(weight_ref, shape, axis, span):
    index = lax.broadcasted_iota(jnp.int32, shape, axis)
    return jnp.sqrt(jnp.where(index // span % 2 == 0, weight_ref[0], weight_ref[1]))


def spread_kernel(orbitals_ref, mask_ref, weight_ref, table_ref, out_ref, work_ref):
    rows_y, rows_z, length = mask_ref.shape
    mask = jnp.where(mask_ref[...] != 0, 1.0, 0.0).astype(bf16)
    mask = jnp.concatenate([mask, mask], axis=2)
    lane = lax.broadcasted_iota(jnp.int32, (length, 128), 1)
    roots = root_weights(weight_ref, (1, 128), 1, rows_z)
    spreads = []
    for pair in range(0, rows_y, 2):
        rows = []
        for y in (pair, pair + 1):
            both = jnp.concatenate([orbitals_ref[0, y] * mask[y], orbitals_ref[1, y] * mask[y]], axis=0)
            rows += [both, both]
        spreads.append(dot_nt(table_ref[...], jnp.concatenate(rows, axis=0)))
    for y in range(rows_y):
        spread = spreads[y // 2][:, y % 2 * 128 : y % 2 * 128 + 128]
        tile = jnp.where(lane < 64, spread[:length], spread[length:])
        work_ref[pl.ds(y, length, stride=rows_y), :] = tile * roots
    out_ref[...] = work_ref[...].reshape(out_ref.shape).astype(bf16)


def overlap_kernel(
    orbitals_ref, mask_ref, channels_ref, phase_ref, wave_ref, out_ref, profile_ref, sums_ref
):
    step = pl.program_id(0)
    rows = mask_ref.shape[0] * mask_ref.shape[1]
    length = mask_ref.shape[2]
    atoms = wave_ref.shape[0] // 2
    kinds = channels_ref.shape[0]
    mask = jnp.where(mask_ref[...] != 0, 1.0, 0.0).astype(bf16)
    orbs = [orbitals_ref[n].reshape(rows, 2 * length) for n in range(2)]
    columns = []
    profile_ref[kinds] = mask
    for c in range(kinds):
        profile_ref[c] = channels_ref[c] * mask
        radial = profile_ref[c].reshape(rows, length)
        radial = jnp.concatenate([radial, radial], axis=1)
        columns += [radial * orbs[0], radial * orbs[1]]
    part = dot(phase_ref[...], jnp.concatenate(columns, axis=1))

    @pl.when(step == 0)
    def first():
        sums_ref[...] = part

    @pl.when(step > 0)
    def later():
        sums_ref[...] += part

    @pl.when(step == pl.num_programs(0) - 1)
    def last():
        cos_x, sin_x = wave_ref[:atoms], wave_ref[atoms:]
        lane = lax.broadcasted_iota(jnp.int32, (atoms, 128), 1)
        total = jnp.zeros((atoms, 128), f32)
        for pair in range(kinds * 2):
            base = pair * 2 * length
            real_cols = slice(base, base + length)
            imag_cols = slice(base + length, base + 2 * length)
            real = sums_ref[:atoms, real_cols] - sums_ref[atoms:, imag_cols]
            imag = sums_ref[atoms:, real_cols] + sums_ref[:atoms, imag_cols]
            real_over = jnp.sum(real * cos_x - imag * sin_x, axis=1, keepdims=True)
            imag_over = jnp.sum(real * sin_x + imag * cos_x, axis=1, keepdims=True)
            total = jnp.where(lane == 2 * pair, real_over, total)
            total = jnp.where(lane == 2 * pair + 1, imag_over, total)
        high = total.astype(bf16).astype(f32)
        out_ref[...] = jnp.concatenate([high, total - high], axis=0).astype(bf16)


def field_kernel(
    arrived_ref,
    potential_ref,
    overlap_ref,
    z_ref,
    inv_y_ref,
    fwd_y_ref,
    mine_ref,
    theirs_ref,
    out_ref,
    tables_ref,
    chunks_ref,
    loads,
    stores,
):
    planes, length = potential_ref.shape[:2]
    parts = 4
    places = 4 * parts
    tables = [pltpu.make_async_copy(z_ref.at[i], tables_ref.at[i], loads.at[i]) for i in range(2)]
    for table in tables:
        table.start()
    bands = arrived_ref.shape[0] // places
    rows = arrived_ref.shape[1] // planes
    span = rows // 2
    for place in range(out_ref.shape[0]):
        chunks_ref[place, planes * rows :, :] = overlap_ref[...]
    tables[0].wait()
    halfway = []
    for b in range(bands):
        columns = jnp.concatenate(
            [
                jnp.concatenate([arrived_ref[b * places + sy * 4 + sz] for sz in range(4)], axis=1)
                for sy in range(parts)
            ],
            axis=0,
        )
        halfway.append(dot(columns, tables_ref[0]).astype(bf16))
    fields = []
    for b in range(bands):
        for x in range(planes):
            first = [(sy * planes + x) * rows for sy in range(parts)]
            plane = jnp.concatenate([halfway[b][start : start + rows] for start in first], axis=0)
            real = jnp.concatenate([plane[:, 0:128], plane[:, 256:384]], axis=1)
            imag = jnp.concatenate([plane[:, 128:256], plane[:, 384:512]], axis=1)
            fields.append(dot(inv_y_ref[...], jnp.concatenate([real, imag], axis=0)))
    density = []
    scaled = []
    for x in range(planes):
        square = [fields[b * planes + x] * fields[b * planes + x] for b in range(bands)]
        square = sum(s[:length] + s[length:] for s in square)
        density.append((square[:, :length] + square[:, length:]).astype(bf16))
    for b in range(bands):
        for x in range(planes):
            potential = jnp.concatenate([potential_ref[x], potential_ref[x]], axis=1)
            potential = jnp.concatenate([potential, potential], axis=0)
            scaled.append((potential * fields[b * planes + x]).astype(bf16))
    folded = [dot(fwd_y_ref[...], block).astype(bf16) for block in scaled]
    tables[1].wait()
    copies = []
    for b in range(bands):
        back = []
        for block in folded[b * planes : (b + 1) * planes]:
            real, imag = block[:length], block[length:]
            back.append(
                jnp.concatenate([real[:, :length], imag[:, :length], real[:, length:], imag[:, length:]], axis=1)
            )
        back = dot(jnp.concatenate(back, axis=0), tables_ref[1]).astype(bf16)
        for x in range(planes):
            for sy in range(parts):
                for half in range(2):
                    start = x * length + sy * rows + half * span
                    row = (half * planes + x) * span
                    for sz in range(4):
                        chunks_ref[b * places + sy * 4 + sz, row : row + span, :] = back[
                            start : start + span, sz * 128 : sz * 128 + 128
                        ]
        here = pl.ds(b * places, places)
        copies.append(pltpu.make_async_copy(chunks_ref.at[here], out_ref.at[here], stores.at[b]))
        copies[b].start()
    upper = lax.axis_index("band") // 2 % 2
    half = planes // 2
    for x in range(half):
        here = slice(x * length, (x + 1) * length)
        mine_ref[here, :] = jnp.where(upper == 0, density[x], density[half + x])
        theirs_ref[here, :] = jnp.where(upper == 0, density[half + x], density[x])
    for copy in copies:
        copy.wait()


def apply_kernel(
    returned_ref,
    overlap_ref,
    orbitals_ref,
    profile_ref,
    phase_ref,
    wave_ref,
    strength_ref,
    weight_ref,
    table_ref,
    out_ref,
    factor_ref,
    work_ref,
):
    step = pl.program_id(0)
    kinds = profile_ref.shape[0] - 1
    grid_shape = profile_ref.shape[1:]
    rows_y, rows_z, length = grid_shape
    atoms = wave_ref.shape[0] // 2

    work_ref[...] = returned_ref[...].astype(f32).reshape(work_ref.shape)
    planes = [work_ref[pl.ds(y, length, stride=rows_y), :].astype(bf16) for y in range(rows_y)]
    local = [dot_tn(jnp.concatenate(planes[y : y + 2], axis=1), table_ref[...]) for y in range(0, rows_y, 2)]

    @pl.when(step == 0)
    def factors():
        cos_x, sin_x = wave_ref[:atoms], wave_ref[atoms:]
        sources = overlap_ref.shape[0] // 2
        even = jnp.sum(overlap_ref[:sources].astype(f32), axis=0)
        odd = jnp.sum(overlap_ref[sources:].astype(f32), axis=0)
        summed = jnp.where(lax.axis_index("band") % 2 == 0, even, odd)
        coef = (summed[:atoms] + summed[atoms:]) * strength_ref[...]
        for pair in range(kinds * 2):
            coef_real = coef[:, 2 * pair : 2 * pair + 1]
            coef_imag = coef[:, 2 * pair + 1 : 2 * pair + 2]
            real = cos_x * coef_real + sin_x * coef_imag
            imag = cos_x * coef_imag - sin_x * coef_real
            base = pair * 2 * length
            factor_ref[:, base : base + length] = jnp.concatenate([real, imag], axis=0).astype(bf16)
            factor_ref[:, base + length : base + 2 * length] = jnp.concatenate(
                [imag, -real], axis=0
            ).astype(bf16)

    extra = dot_tn(phase_ref[...], factor_ref[...])

    def squared(start, axis):
        index = start + lax.broadcasted_iota(jnp.int32, grid_shape, axis)
        wave = jnp.where(index >= length // 2, index - length, index)
        return wave * wave

    first_y = lax.axis_index("gy") * (rows_y * pl.num_programs(0)) + step * rows_y
    energy = squared(first_y, 0) + squared(lax.axis_index("gz") * rows_z, 1) + squared(0, 2)
    energy = kinetic_scale * 0.5 * energy.astype(f32)
    scale = 1.0 / root_weights(weight_ref, (2 * rows_z, 1), 0, rows_z)
    for y in range(rows_y):
        block = local[y // 2][y % 2 * 128 : y % 2 * 128 + 128]
        both = scale * (block[:64, : 2 * length] + block[64:, 2 * length :])
        radials = [profile_ref[c, y].astype(f32) for c in range(kinds + 1)]
        for n in range(2):
            for part in range(2):
                cols = slice(part * length, part * length + length)
                total = both[n * rows_z : (n + 1) * rows_z, cols]
                total = total + energy[y] * orbitals_ref[n, y, :, cols].astype(f32)
                total = total * radials[kinds]
                for c in range(kinds):
                    base = ((c * 2 + n) * 2 + part) * length
                    total = total + radials[c] * extra[y * rows_z : (y + 1) * rows_z, base : base + length]
                out_ref[n, y, :, cols] = total.astype(bf16)


def strength_kernel(atom_ref, kind_ref, coupling_ref, out_ref):
    row = lax.broadcasted_iota(jnp.int32, out_ref.shape, 0)
    kind = lax.broadcasted_iota(jnp.int32, out_ref.shape, 1) // 4
    total = jnp.zeros(out_ref.shape, f32)
    for p in range(coupling_ref.shape[0]):
        total += jnp.where((row == atom_ref[p]) & (kind == kind_ref[p]), coupling_ref[p], 0.0)
    out_ref[...] = total


def partners(axis, distance):
    return [(i, i ^ distance) for i in range(lax.axis_size(axis))]


def shards(
    orbitals,
    potential,
    cutoff_mask,
    channels,
    positions,
    proj_atom,
    proj_chan,
    coupling,
    occupations,
):
    rows_y, rows_z, length = cutoff_mask.shape
    parts_y = lax.axis_size("gy")
    parts_z = lax.axis_size("gz")
    parts_band = lax.axis_size("band")
    places = parts_y * parts_z
    bands = 2
    outer = parts_band // bands
    thin = length // places
    planes = thin // bands
    atoms = positions.shape[0]
    kinds = channels.shape[0]
    groups = [
        [(first * bands + b) * places + place for b in range(bands) for place in range(places)]
        for first in range(outer)
    ]
    inverse = dft_table(length, 1.0)
    forward = dft_table(length, -1.0)
    pick = np.eye(2, dtype=np.float32)
    split_inverse = inverse.reshape(2, length, 2, parts_z, rows_z)
    split_forward = forward.reshape(2, parts_z, rows_z, 2, length)
    order = np.arange(length).reshape(places, bands, planes).transpose(1, 0, 2).reshape(-1)
    inv_x = rounded(inverse[:, order], 2 * length)
    inv_y = rounded(inverse, 2 * length)
    inv_z = np.einsum("fzcsl,nm->scnlmfz", split_inverse, pick).reshape(4 * length, 4 * length)
    fwd_z = np.einsum("cslfz,nm->nfzscml", split_forward, pick).reshape(4 * length, 4 * length)
    both_z = rounded(np.stack([inv_z, fwd_z]), 8 * length).reshape(2, 4 * length, 4 * length)
    fwd_y = rounded(forward, 2 * length)
    fwd_x = rounded(np.einsum("rkcx->xcrk", forward[..., order]), length)
    first_y = lax.axis_index("gy") * rows_y
    first_z = lax.axis_index("gz") * rows_z
    band = lax.axis_index("band") % bands

    params = pltpu.CompilerParams(vmem_limit_bytes=vmem_bytes)

    def cost(microseconds):
        return pl.CostEstimate(
            flops=int(microseconds * 1.0e9), bytes_accessed=int(microseconds * 1.0e6), transcendentals=0
        )

    steps = 2
    span = rows_y // steps
    whole = lambda *shape: pl.BlockSpec(shape, lambda i: (0,) * len(shape))
    orbitals_spec = pl.BlockSpec((2, span, rows_z, 2 * length), lambda i: (0, i, 0, 0))
    mask_spec = pl.BlockSpec((span, rows_z, length), lambda i: (i, 0, 0))
    channels_spec = pl.BlockSpec((kinds, span, rows_z, length), lambda i: (0, i, 0, 0))
    phase_spec = pl.BlockSpec((2 * atoms, span * rows_z), lambda i: (0, i))
    chunks_spec = pl.BlockSpec((bands * places, planes, span, 128), lambda i: (0, 0, i, 0))
    chunk_shape = (bands * places, planes, rows_y, 128)
    smem_spec = pl.BlockSpec(memory_space=pltpu.SMEM)

    def exchange(chunks):
        return lax.all_to_all(
            chunks, ("band", "gy", "gz"), split_axis=0, concat_axis=0, tiled=True, axis_index_groups=groups
        )

    spread = pl.pallas_call(
        spread_kernel,
        grid=(steps,),
        in_specs=[orbitals_spec, mask_spec, smem_spec, whole(2 * length, 2 * length)],
        out_specs=chunks_spec,
        out_shape=jax.ShapeDtypeStruct(chunk_shape, bf16),
        scratch_shapes=[pltpu.VMEM((length * span, 128), f32)],
        compiler_params=params,
        cost_estimate=cost(4),
        name="spread",
    )(orbitals, cutoff_mask, occupations, inv_x)
    potential_part = lax.dynamic_slice_in_dim(potential, band * planes, planes, 0)

    spread, positions = lax.optimization_barrier((spread, positions))
    arrived = exchange(spread)

    cos_y, sin_y = axis_phase(positions[:, 1], frequencies(first_y, rows_y, length))
    cos_z, sin_z = axis_phase(positions[:, 2], frequencies(first_z, rows_z, length))
    cos_x, sin_x = axis_phase(positions[:, 0], frequencies(0, length, length))
    cos_yz = cos_y[:, :, None] * cos_z[:, None, :] - sin_y[:, :, None] * sin_z[:, None, :]
    sin_yz = sin_y[:, :, None] * cos_z[:, None, :] + cos_y[:, :, None] * sin_z[:, None, :]
    phase = jnp.concatenate([cos_yz, sin_yz], axis=0).astype(bf16).reshape(2 * atoms, rows_y * rows_z)
    wave = jnp.concatenate([cos_x, sin_x], axis=0)
    positions, coupling = lax.optimization_barrier((positions, coupling))
    strength = pl.pallas_call(
        strength_kernel,
        in_specs=[smem_spec] * 3,
        out_shape=jax.ShapeDtypeStruct((atoms, 128), f32),
        compiler_params=pltpu.CompilerParams(vmem_limit_bytes=16384 * 1024),
        cost_estimate=cost(0.1),
        name="strength",
    )(proj_atom, proj_chan, coupling)
    profile_spec = pl.BlockSpec((kinds + 1, span, rows_z, length), lambda i: (0, i, 0, 0))
    overlap, profile = pl.pallas_call(
        overlap_kernel,
        grid=(steps,),
        in_specs=[orbitals_spec, mask_spec, channels_spec, phase_spec, whole(2 * atoms, length)],
        out_specs=[whole(2 * atoms, 128), profile_spec],
        out_shape=[
            jax.ShapeDtypeStruct((2 * atoms, 128), bf16),
            jax.ShapeDtypeStruct((kinds + 1, rows_y, rows_z, length), bf16),
        ],
        scratch_shapes=[pltpu.VMEM((2 * atoms, kinds * 4 * length), f32)],
        compiler_params=pltpu.CompilerParams(vmem_limit_bytes=32768 * 1024),
        cost_estimate=cost(0.1),
        name="overlap",
    )(orbitals, cutoff_mask, channels, phase, wave)
    arrived, overlap, strength = lax.optimization_barrier((arrived, overlap, strength))

    rows = planes * rows_y
    half = planes // 2 * length
    mine, theirs, folded = pl.pallas_call(
        field_kernel,
        grid=(1,),
        in_specs=[
            whole(bands * places, rows, 128),
            whole(planes, length, length),
            whole(2 * atoms, 128),
            pl.BlockSpec(memory_space=pl.ANY),
            whole(2 * length, 2 * length),
            whole(2 * length, 2 * length),
        ],
        out_specs=[
            whole(half, length),
            whole(half, length),
            pl.BlockSpec(memory_space=pl.ANY),
        ],
        out_shape=[
            jax.ShapeDtypeStruct((half, length), bf16),
            jax.ShapeDtypeStruct((half, length), bf16),
            jax.ShapeDtypeStruct((bands * places, rows + 2 * atoms, 128), bf16),
        ],
        scratch_shapes=[
            pltpu.VMEM((2, 4 * length, 4 * length), bf16),
            pltpu.VMEM((bands * places, rows + 2 * atoms, 128), bf16),
            pltpu.SemaphoreType.DMA((2,)),
            pltpu.SemaphoreType.DMA((bands,)),
        ],
        compiler_params=pltpu.CompilerParams(vmem_limit_bytes=53248 * 1024),
        cost_estimate=cost(6),
        name="field",
    )(arrived.reshape(bands * places, rows, 128), potential_part, overlap, both_z, inv_y, fwd_y)
    returned = exchange(folded)

    near = lax.ppermute(theirs, "band", partners("band", bands))
    mine = (mine.astype(f32) + near.astype(f32)).astype(bf16)
    got = lax.ppermute(mine, "band", partners("band", 2 * bands))
    mine = (mine.astype(f32) + got.astype(f32)).astype(bf16)
    far, near, both = [lax.ppermute(mine, "band", partners("band", d * bands)) for d in (6, 1, 7)]
    mine = (mine.astype(f32) + far.astype(f32)).astype(bf16)
    near = (near.astype(f32) + both.astype(f32)).astype(bf16)
    upper = lax.axis_index("band") // bands % 2
    mine = jnp.where(upper == 0, jnp.stack([mine, near]), jnp.stack([near, mine]))
    other = lax.ppermute(mine, "band", partners("band", 1))
    applied = pl.pallas_call(
        apply_kernel,
        grid=(steps,),
        in_specs=[
            pl.BlockSpec((bands * places, planes * span, 128), lambda i: (0, i, 0)),
            pl.BlockSpec((bands * places, 2 * atoms, 128), lambda i: (0, rows // (2 * atoms), 0)),
            orbitals_spec,
            profile_spec,
            phase_spec,
            whole(2 * atoms, length),
            whole(atoms, 128),
            smem_spec,
            whole(length, 4 * length),
        ],
        out_specs=orbitals_spec,
        out_shape=jax.ShapeDtypeStruct(orbitals.shape, bf16),
        scratch_shapes=[
            pltpu.VMEM((2 * atoms, kinds * 4 * length), bf16),
            pltpu.VMEM((length * span, 128), f32),
        ],
        compiler_params=pltpu.CompilerParams(vmem_limit_bytes=52224 * 1024),
        cost_estimate=cost(4),
        name="apply",
    )(returned, returned, orbitals, profile, phase, wave, strength, occupations, fwd_x)
    other, applied = lax.optimization_barrier((other, applied))
    density = jnp.where(band == 0, jnp.stack([mine, other]), jnp.stack([other, mine]))
    return (applied, density.astype(f32).reshape(potential.shape))


def solution(mesh):
    placed = (
        P("band", "gy", "gz", None),
        P(("gy", "gz"), None, None),
        P("gy", "gz", None),
        P(None, "gy", "gz", None),
        P(),
        P(),
        P(),
        P(),
        P("band"),
    )
    return jax.shard_map(
        shards,
        mesh=mesh,
        in_specs=placed,
        out_specs=(P("band", "gy", "gz", None), P(("gy", "gz"), None, None)),
        check_vma=False,
    )
```

```python
import functools
import math

import jax
import jax.numpy as jnp
import ml_dtypes
import numpy as np
from jax import lax
from jax.experimental import pallas as pl
from jax.experimental.pallas import tpu as pltpu
from jax.sharding import PartitionSpec as P

kinetic_scale = 1.0 / 1024.0
vmem_bytes = 63 * 1024 * 1024
bf16 = jnp.bfloat16
f32 = jnp.float32


def dft_table(length, sign_value):
    grid_index = np.arange(length)
    product = grid_index[:, None] * grid_index[None, :] % length
    phase_angle = np.float32(2.0 * math.pi / length) * product.astype(np.float32)
    cosine_part = np.cos(phase_angle) / np.float32(math.sqrt(length))
    sine_part = sign_value * np.sin(phase_angle) / np.float32(math.sqrt(length))
    upper_rows = np.stack([cosine_part, -sine_part], axis=1)
    lower_rows = np.stack([sine_part, cosine_part], axis=1)
    return np.stack([upper_rows, lower_rows], axis=0).astype(np.float32)


def rounded(table, rows):
    return jnp.asarray(np.ascontiguousarray(table).reshape(rows, -1).astype(ml_dtypes.bfloat16))


def frequencies(first_index, span, length):
    grid_index = first_index + jnp.arange(span, dtype=jnp.int32)
    return jnp.where(grid_index >= length // 2, grid_index - length, grid_index).astype(f32)


def axis_phase(coordinate, freq):
    phase_angle = 2.0 * math.pi * (coordinate[:, None] * freq[None, :])
    return (jnp.cos(phase_angle), jnp.sin(phase_angle))


def dot(left, right):
    return jnp.dot(left, right, preferred_element_type=f32)


def dot_nt(left, right):
    return lax.dot_general(left, right, (((1,), (1,)), ((), ())), preferred_element_type=f32)


def dot_tn(left, right):
    return lax.dot_general(left, right, (((0,), (0,)), ((), ())), preferred_element_type=f32)


def root_weights(weight_ref, shape, axis, span):
    index = lax.broadcasted_iota(jnp.int32, shape, axis)
    return jnp.sqrt(jnp.where(index // span % 2 == 0, weight_ref[0], weight_ref[1]))


def spread_kernel(orbitals_ref, mask_ref, weight_ref, table_ref, out_ref, work_ref):
    rows_y, rows_z, length = mask_ref.shape
    mask = jnp.where(mask_ref[...] != 0, 1.0, 0.0).astype(bf16)
    mask = jnp.concatenate([mask, mask], axis=2)
    lane = lax.broadcasted_iota(jnp.int32, (length, 128), 1)
    roots = root_weights(weight_ref, (1, 128), 1, rows_z)
    spreads = []
    for pair in range(0, rows_y, 2):
        rows = []
        for y in (pair, pair + 1):
            both = jnp.concatenate([orbitals_ref[0, y] * mask[y], orbitals_ref[1, y] * mask[y]], axis=0)
            rows += [both, both]
        spreads.append(dot_nt(table_ref[...], jnp.concatenate(rows, axis=0)))
    for y in range(rows_y):
        spread = spreads[y // 2][:, y % 2 * 128 : y % 2 * 128 + 128]
        tile = jnp.where(lane < 64, spread[:length], spread[length:])
        work_ref[pl.ds(y, length, stride=rows_y), :] = tile * roots
    out_ref[...] = work_ref[...].reshape(out_ref.shape).astype(bf16)


def overlap_kernel(
    orbitals_ref, mask_ref, channels_ref, phase_ref, wave_ref, out_ref, profile_ref, sums_ref
):
    step = pl.program_id(0)
    rows = mask_ref.shape[0] * mask_ref.shape[1]
    length = mask_ref.shape[2]
    atoms = wave_ref.shape[0] // 2
    kinds = channels_ref.shape[0]
    mask = jnp.where(mask_ref[...] != 0, 1.0, 0.0).astype(bf16)
    orbs = [orbitals_ref[n].reshape(rows, 2 * length) for n in range(2)]
    columns = []
    profile_ref[kinds] = mask
    for c in range(kinds):
        profile_ref[c] = channels_ref[c] * mask
        radial = profile_ref[c].reshape(rows, length)
        radial = jnp.concatenate([radial, radial], axis=1)
        columns += [radial * orbs[0], radial * orbs[1]]
    part = dot(phase_ref[...], jnp.concatenate(columns, axis=1))

    @pl.when(step == 0)
    def first():
        sums_ref[...] = part

    @pl.when(step > 0)
    def later():
        sums_ref[...] += part

    @pl.when(step == pl.num_programs(0) - 1)
    def last():
        cos_x, sin_x = wave_ref[:atoms], wave_ref[atoms:]
        lane = lax.broadcasted_iota(jnp.int32, (atoms, 128), 1)
        total = jnp.zeros((atoms, 128), f32)
        for pair in range(kinds * 2):
            base = pair * 2 * length
            real_cols = slice(base, base + length)
            imag_cols = slice(base + length, base + 2 * length)
            real = sums_ref[:atoms, real_cols] - sums_ref[atoms:, imag_cols]
            imag = sums_ref[atoms:, real_cols] + sums_ref[:atoms, imag_cols]
            real_over = jnp.sum(real * cos_x - imag * sin_x, axis=1, keepdims=True)
            imag_over = jnp.sum(real * sin_x + imag * cos_x, axis=1, keepdims=True)
            total = jnp.where(lane == 2 * pair, real_over, total)
            total = jnp.where(lane == 2 * pair + 1, imag_over, total)
        high = total.astype(bf16).astype(f32)
        out_ref[...] = jnp.concatenate([high, total - high], axis=0).astype(bf16)


def field_kernel(
    arrived_ref,
    potential_ref,
    overlap_ref,
    z_ref,
    inv_y_ref,
    fwd_y_ref,
    mine_ref,
    theirs_ref,
    out_ref,
    tables_ref,
    chunks_ref,
    loads,
    stores,
):
    planes, length = potential_ref.shape[:2]
    parts = 4
    places = 4 * parts
    tables = [pltpu.make_async_copy(z_ref.at[i], tables_ref.at[i], loads.at[i]) for i in range(2)]
    for table in tables:
        table.start()
    bands = arrived_ref.shape[0] // places
    rows = arrived_ref.shape[1] // planes
    span = rows // 2
    for place in range(out_ref.shape[0]):
        chunks_ref[place, planes * rows :, :] = overlap_ref[...]
    tables[0].wait()
    halfway = []
    for b in range(bands):
        columns = jnp.concatenate(
            [
                jnp.concatenate([arrived_ref[b * places + sy * 4 + sz] for sz in range(4)], axis=1)
                for sy in range(parts)
            ],
            axis=0,
        )
        halfway.append(dot(columns, tables_ref[0]).astype(bf16))
    fields = []
    for b in range(bands):
        for x in range(planes):
            first = [(sy * planes + x) * rows for sy in range(parts)]
            plane = jnp.concatenate([halfway[b][start : start + rows] for start in first], axis=0)
            real = jnp.concatenate([plane[:, 0:128], plane[:, 256:384]], axis=1)
            imag = jnp.concatenate([plane[:, 128:256], plane[:, 384:512]], axis=1)
            fields.append(dot(inv_y_ref[...], jnp.concatenate([real, imag], axis=0)))
    density = []
    scaled = []
    for x in range(planes):
        square = [fields[b * planes + x] * fields[b * planes + x] for b in range(bands)]
        square = sum(s[:length] + s[length:] for s in square)
        density.append((square[:, :length] + square[:, length:]).astype(bf16))
    for b in range(bands):
        for x in range(planes):
            potential = jnp.concatenate([potential_ref[x], potential_ref[x]], axis=1)
            potential = jnp.concatenate([potential, potential], axis=0)
            scaled.append((potential * fields[b * planes + x]).astype(bf16))
    folded = [dot(fwd_y_ref[...], block).astype(bf16) for block in scaled]
    tables[1].wait()
    copies = []
    for b in range(bands):
        back = []
        for block in folded[b * planes : (b + 1) * planes]:
            real, imag = block[:length], block[length:]
            back.append(
                jnp.concatenate([real[:, :length], imag[:, :length], real[:, length:], imag[:, length:]], axis=1)
            )
        back = dot(jnp.concatenate(back, axis=0), tables_ref[1]).astype(bf16)
        for x in range(planes):
            for sy in range(parts):
                for half in range(2):
                    start = x * length + sy * rows + half * span
                    row = (half * planes + x) * span
                    for sz in range(4):
                        chunks_ref[b * places + sy * 4 + sz, row : row + span, :] = back[
                            start : start + span, sz * 128 : sz * 128 + 128
                        ]
        here = pl.ds(b * places, places)
        copies.append(pltpu.make_async_copy(chunks_ref.at[here], out_ref.at[here], stores.at[b]))
        copies[b].start()
    upper = lax.axis_index("band") // 2 % 2
    half = planes // 2
    for x in range(half):
        here = slice(x * length, (x + 1) * length)
        mine_ref[here, :] = jnp.where(upper == 0, density[x], density[half + x])
        theirs_ref[here, :] = jnp.where(upper == 0, density[half + x], density[x])
    for copy in copies:
        copy.wait()


def apply_kernel(
    returned_ref,
    overlap_ref,
    orbitals_ref,
    profile_ref,
    phase_ref,
    wave_ref,
    strength_ref,
    weight_ref,
    table_ref,
    out_ref,
    factor_ref,
    work_ref,
):
    step = pl.program_id(0)
    kinds = profile_ref.shape[0] - 1
    grid_shape = profile_ref.shape[1:]
    rows_y, rows_z, length = grid_shape
    atoms = wave_ref.shape[0] // 2

    work_ref[...] = returned_ref[...].astype(f32).reshape(work_ref.shape)
    lane = lax.broadcasted_iota(jnp.int32, (length, 128), 1)
    local = []
    for y in range(0, rows_y, 2):
        even, odd = [work_ref[pl.ds(row, length, stride=rows_y), :] for row in (y, y + 1)]
        real = jnp.where(lane < 64, even, pltpu.roll(odd, 64, 1))
        imag = jnp.where(lane < 64, pltpu.roll(even, 64, 1), odd)
        local.append(dot_tn(jnp.concatenate([real, imag], axis=0).astype(bf16), table_ref[...]))

    @pl.when(step == 0)
    def factors():
        cos_x, sin_x = wave_ref[:atoms], wave_ref[atoms:]
        sources = overlap_ref.shape[0] // 2
        even = jnp.sum(overlap_ref[:sources].astype(f32), axis=0)
        odd = jnp.sum(overlap_ref[sources:].astype(f32), axis=0)
        summed = jnp.where(lax.axis_index("band") % 2 == 0, even, odd)
        coef = (summed[:atoms] + summed[atoms:]) * strength_ref[...]
        for pair in range(kinds * 2):
            coef_real = coef[:, 2 * pair : 2 * pair + 1]
            coef_imag = coef[:, 2 * pair + 1 : 2 * pair + 2]
            real = cos_x * coef_real + sin_x * coef_imag
            imag = cos_x * coef_imag - sin_x * coef_real
            base = pair * 2 * length
            factor_ref[:, base : base + length] = jnp.concatenate([real, imag], axis=0).astype(bf16)
            factor_ref[:, base + length : base + 2 * length] = jnp.concatenate(
                [imag, -real], axis=0
            ).astype(bf16)

    extra = dot_tn(phase_ref[...], factor_ref[...])

    def squared(start, axis):
        index = start + lax.broadcasted_iota(jnp.int32, grid_shape, axis)
        wave = jnp.where(index >= length // 2, index - length, index)
        return wave * wave

    first_y = lax.axis_index("gy") * (rows_y * pl.num_programs(0)) + step * rows_y
    energy = squared(first_y, 0) + squared(lax.axis_index("gz") * rows_z, 1) + squared(0, 2)
    energy = kinetic_scale * 0.5 * energy.astype(f32)
    scale = 1.0 / root_weights(weight_ref, (2 * rows_z, 1), 0, rows_z)
    for y in range(rows_y):
        both = scale * local[y // 2][y % 2 * 64 : y % 2 * 64 + 64]
        radials = [profile_ref[c, y].astype(f32) for c in range(kinds + 1)]
        for n in range(2):
            for part in range(2):
                cols = slice(part * length, part * length + length)
                total = both[n * rows_z : (n + 1) * rows_z, cols]
                total = total + energy[y] * orbitals_ref[n, y, :, cols].astype(f32)
                total = total * radials[kinds]
                for c in range(kinds):
                    base = ((c * 2 + n) * 2 + part) * length
                    total = total + radials[c] * extra[y * rows_z : (y + 1) * rows_z, base : base + length]
                out_ref[n, y, :, cols] = total.astype(bf16)


def strength_kernel(atom_ref, kind_ref, coupling_ref, out_ref):
    row = lax.broadcasted_iota(jnp.int32, out_ref.shape, 0)
    kind = lax.broadcasted_iota(jnp.int32, out_ref.shape, 1) // 4
    total = jnp.zeros(out_ref.shape, f32)
    for p in range(coupling_ref.shape[0]):
        total += jnp.where((row == atom_ref[p]) & (kind == kind_ref[p]), coupling_ref[p], 0.0)
    out_ref[...] = total


def partners(axis, distance):
    return [(i, i ^ distance) for i in range(lax.axis_size(axis))]


def shards(
    orbitals,
    potential,
    cutoff_mask,
    channels,
    positions,
    proj_atom,
    proj_chan,
    coupling,
    occupations,
):
    rows_y, rows_z, length = cutoff_mask.shape
    parts_y = lax.axis_size("gy")
    parts_z = lax.axis_size("gz")
    parts_band = lax.axis_size("band")
    places = parts_y * parts_z
    bands = 2
    outer = parts_band // bands
    thin = length // places
    planes = thin // bands
    atoms = positions.shape[0]
    kinds = channels.shape[0]
    groups = [
        [(first * bands + b) * places + place for b in range(bands) for place in range(places)]
        for first in range(outer)
    ]
    inverse = dft_table(length, 1.0)
    forward = dft_table(length, -1.0)
    pick = np.eye(2, dtype=np.float32)
    split_inverse = inverse.reshape(2, length, 2, parts_z, rows_z)
    split_forward = forward.reshape(2, parts_z, rows_z, 2, length)
    order = np.arange(length).reshape(places, bands, planes).transpose(1, 0, 2).reshape(-1)
    inv_x = rounded(inverse[:, order], 2 * length)
    inv_y = rounded(inverse, 2 * length)
    inv_z = np.einsum("fzcsl,nm->scnlmfz", split_inverse, pick).reshape(4 * length, 4 * length)
    fwd_z = np.einsum("cslfz,nm->nfzscml", split_forward, pick).reshape(4 * length, 4 * length)
    both_z = rounded(np.stack([inv_z, fwd_z]), 8 * length).reshape(2, 4 * length, 4 * length)
    fwd_y = rounded(forward, 2 * length)
    fwd_x = rounded(np.einsum("rkcx->cxrk", forward[..., order]), 2 * length)
    first_y = lax.axis_index("gy") * rows_y
    first_z = lax.axis_index("gz") * rows_z
    band = lax.axis_index("band") % bands

    params = pltpu.CompilerParams(vmem_limit_bytes=vmem_bytes)

    def cost(microseconds):
        return pl.CostEstimate(
            flops=int(microseconds * 1.0e9), bytes_accessed=int(microseconds * 1.0e6), transcendentals=0
        )

    steps = 2
    span = rows_y // steps
    whole = lambda *shape: pl.BlockSpec(shape, lambda i: (0,) * len(shape))
    orbitals_spec = pl.BlockSpec((2, span, rows_z, 2 * length), lambda i: (0, i, 0, 0))
    mask_spec = pl.BlockSpec((span, rows_z, length), lambda i: (i, 0, 0))
    channels_spec = pl.BlockSpec((kinds, span, rows_z, length), lambda i: (0, i, 0, 0))
    phase_spec = pl.BlockSpec((2 * atoms, span * rows_z), lambda i: (0, i))
    chunks_spec = pl.BlockSpec((bands * places, planes, span, 128), lambda i: (0, 0, i, 0))
    chunk_shape = (bands * places, planes, rows_y, 128)
    smem_spec = pl.BlockSpec(memory_space=pltpu.SMEM)

    def exchange(chunks):
        return lax.all_to_all(
            chunks, ("band", "gy", "gz"), split_axis=0, concat_axis=0, tiled=True, axis_index_groups=groups
        )

    spread = pl.pallas_call(
        spread_kernel,
        grid=(steps,),
        in_specs=[orbitals_spec, mask_spec, smem_spec, whole(2 * length, 2 * length)],
        out_specs=chunks_spec,
        out_shape=jax.ShapeDtypeStruct(chunk_shape, bf16),
        scratch_shapes=[pltpu.VMEM((length * span, 128), f32)],
        compiler_params=params,
        cost_estimate=cost(4),
        name="spread",
    )(orbitals, cutoff_mask, occupations, inv_x)
    potential_part = lax.dynamic_slice_in_dim(potential, band * planes, planes, 0)

    spread, positions = lax.optimization_barrier((spread, positions))
    arrived = exchange(spread)

    cos_y, sin_y = axis_phase(positions[:, 1], frequencies(first_y, rows_y, length))
    cos_z, sin_z = axis_phase(positions[:, 2], frequencies(first_z, rows_z, length))
    cos_x, sin_x = axis_phase(positions[:, 0], frequencies(0, length, length))
    cos_yz = cos_y[:, :, None] * cos_z[:, None, :] - sin_y[:, :, None] * sin_z[:, None, :]
    sin_yz = sin_y[:, :, None] * cos_z[:, None, :] + cos_y[:, :, None] * sin_z[:, None, :]
    phase = jnp.concatenate([cos_yz, sin_yz], axis=0).astype(bf16).reshape(2 * atoms, rows_y * rows_z)
    wave = jnp.concatenate([cos_x, sin_x], axis=0)
    positions, coupling = lax.optimization_barrier((positions, coupling))
    strength = pl.pallas_call(
        strength_kernel,
        in_specs=[smem_spec] * 3,
        out_shape=jax.ShapeDtypeStruct((atoms, 128), f32),
        compiler_params=pltpu.CompilerParams(vmem_limit_bytes=16384 * 1024),
        cost_estimate=cost(0.1),
        name="strength",
    )(proj_atom, proj_chan, coupling)
    profile_spec = pl.BlockSpec((kinds + 1, span, rows_z, length), lambda i: (0, i, 0, 0))
    overlap, profile = pl.pallas_call(
        overlap_kernel,
        grid=(steps,),
        in_specs=[orbitals_spec, mask_spec, channels_spec, phase_spec, whole(2 * atoms, length)],
        out_specs=[whole(2 * atoms, 128), profile_spec],
        out_shape=[
            jax.ShapeDtypeStruct((2 * atoms, 128), bf16),
            jax.ShapeDtypeStruct((kinds + 1, rows_y, rows_z, length), bf16),
        ],
        scratch_shapes=[pltpu.VMEM((2 * atoms, kinds * 4 * length), f32)],
        compiler_params=pltpu.CompilerParams(vmem_limit_bytes=32768 * 1024),
        cost_estimate=cost(0.1),
        name="overlap",
    )(orbitals, cutoff_mask, channels, phase, wave)
    arrived, overlap, strength = lax.optimization_barrier((arrived, overlap, strength))

    rows = planes * rows_y
    half = planes // 2 * length
    mine, theirs, folded = pl.pallas_call(
        field_kernel,
        grid=(1,),
        in_specs=[
            whole(bands * places, rows, 128),
            whole(planes, length, length),
            whole(2 * atoms, 128),
            pl.BlockSpec(memory_space=pl.ANY),
            whole(2 * length, 2 * length),
            whole(2 * length, 2 * length),
        ],
        out_specs=[
            whole(half, length),
            whole(half, length),
            pl.BlockSpec(memory_space=pl.ANY),
        ],
        out_shape=[
            jax.ShapeDtypeStruct((half, length), bf16),
            jax.ShapeDtypeStruct((half, length), bf16),
            jax.ShapeDtypeStruct((bands * places, rows + 2 * atoms, 128), bf16),
        ],
        scratch_shapes=[
            pltpu.VMEM((2, 4 * length, 4 * length), bf16),
            pltpu.VMEM((bands * places, rows + 2 * atoms, 128), bf16),
            pltpu.SemaphoreType.DMA((2,)),
            pltpu.SemaphoreType.DMA((bands,)),
        ],
        compiler_params=pltpu.CompilerParams(vmem_limit_bytes=53248 * 1024),
        cost_estimate=cost(6),
        name="field",
    )(arrived.reshape(bands * places, rows, 128), potential_part, overlap, both_z, inv_y, fwd_y)
    returned = exchange(folded)

    near = lax.ppermute(theirs, "band", partners("band", bands))
    mine = (mine.astype(f32) + near.astype(f32)).astype(bf16)
    got = lax.ppermute(mine, "band", partners("band", 2 * bands))
    mine = (mine.astype(f32) + got.astype(f32)).astype(bf16)
    far, near, both = [lax.ppermute(mine, "band", partners("band", d * bands)) for d in (6, 1, 7)]
    mine = (mine.astype(f32) + far.astype(f32)).astype(bf16)
    near = (near.astype(f32) + both.astype(f32)).astype(bf16)
    upper = lax.axis_index("band") // bands % 2
    mine = jnp.where(upper == 0, jnp.stack([mine, near]), jnp.stack([near, mine]))
    other = lax.ppermute(mine, "band", partners("band", 1))
    applied = pl.pallas_call(
        apply_kernel,
        grid=(steps,),
        in_specs=[
            pl.BlockSpec((bands * places, planes * span, 128), lambda i: (0, i, 0)),
            pl.BlockSpec((bands * places, 2 * atoms, 128), lambda i: (0, rows // (2 * atoms), 0)),
            orbitals_spec,
            profile_spec,
            phase_spec,
            whole(2 * atoms, length),
            whole(atoms, 128),
            smem_spec,
            whole(2 * length, 2 * length),
        ],
        out_specs=orbitals_spec,
        out_shape=jax.ShapeDtypeStruct(orbitals.shape, bf16),
        scratch_shapes=[
            pltpu.VMEM((2 * atoms, kinds * 4 * length), bf16),
            pltpu.VMEM((length * span, 128), f32),
        ],
        compiler_params=pltpu.CompilerParams(vmem_limit_bytes=52224 * 1024),
        cost_estimate=cost(4),
        name="apply",
    )(returned, returned, orbitals, profile, phase, wave, strength, occupations, fwd_x)
    other, applied = lax.optimization_barrier((other, applied))
    density = jnp.where(band == 0, jnp.stack([mine, other]), jnp.stack([other, mine]))
    return (applied, density.astype(f32).reshape(potential.shape))


def solution(mesh):
    placed = (
        P("band", "gy", "gz", None),
        P(("gy", "gz"), None, None),
        P("gy", "gz", None),
        P(None, "gy", "gz", None),
        P(),
        P(),
        P(),
        P(),
        P("band"),
    )
    return jax.shard_map(
        shards,
        mesh=mesh,
        in_specs=placed,
        out_specs=(P("band", "gy", "gz", None), P(("gy", "gz"), None, None)),
        check_vma=False,
    )
```
